32 devices in a mesh: pipe: 2 (over core), dp: 16 (over z, y, x).
Axes of the slice: x: 2, y: 2, z: 4, core: 2. Of those that a mesh axis runs over, the one named last changes fastest.
Arguments:
- inputs: bfloat16 [8192, 768], P('dp'), may hold values from -6 to 6
- cotangent: bfloat16 [8192, 768], P('dp'), may hold values from -6 to 6
- lengths: int32 [32, 4], P('dp'), may hold values from 1 to 192, 256 in all within a row
- proj_stack: float32 [4, 64, 32], replicated, may hold values from -6 to 6
- gain_one: float32 [2, 768], P('pipe'), may hold values from 0.1 to 1.9
- bias_one: float32 [2, 768], P('pipe'), may hold values from -1.5 to 1.5
- w_qkv: bfloat16 [2, 768, 2304], P('pipe'), may hold values from -0.21875 to 0.21875
- w_out: bfloat16 [2, 768, 768], P('pipe'), may hold values from -0.625 to 0.625
- gain_two: float32 [2, 768], P('pipe'), may hold values from 0.1 to 1.9
- bias_two: float32 [2, 768], P('pipe'), may hold values from -1.5 to 1.5
- w_up: bfloat16 [2, 768, 3072], P('pipe'), may hold values from -0.21875 to 0.21875
- w_down: bfloat16 [2, 3072, 768], P('pipe'), may hold values from -0.109375 to 0.109375
Outputs:
- layer_out: bfloat16 [2, 8192, 768], P('pipe', 'dp')
- grad_in: float32 [2, 8192, 768], P('pipe', 'dp')
- grad_gain_one: float32 [2, 768], P('pipe', 'dp')
- grad_bias_one: float32 [2, 768], P('pipe', 'dp')
- grad_w_qkv: float32 [2, 768, 2304], P('pipe', 'dp')
- grad_w_out: float32 [2, 768, 768], P('pipe', 'dp')
- grad_gain_two: float32 [2, 768], P('pipe', 'dp')
- grad_bias_two: float32 [2, 768], P('pipe', 'dp')
- grad_w_up: float32 [2, 768, 3072], P('pipe', 'dp')
- grad_w_down: float32 [2, 3072, 768], P('pipe', 'dp')
The draws below stay inside these ranges and needn't reach their ends.
Inputs may be any that keep to these rules, and one draw needn't show every extreme that they name: `lengths`: each row holds the token counts of 3 molecules of a block of 256 rows and last the count of padding rows at the block's end; they sum to 256, and the largest in each row is 192.
All inputs are finite; a program needn't handle non-finite values.
Results may differ from the reference program's by a relative error of at most 0.017.
The reference program's roundings to bfloat16 on the way count: a program that leaves them out, or rounds other values in their place, can miss the bound.
Values may be sent and summed in bfloat16 or wider, within the bound.
No kernel may reach another device: no remote copies, remote signals or barrier semaphores. Data moves between devices by JAX's collectives and lax.ppermute only.
A program may use at most 192 MiB of HBM per device.

```python
import math
import jax
import jax.numpy as jnp
import numpy as np
from jax import lax

D = 768
HEADS = 12
HEAD = 64
FEAT = 32
FF = 3072
ROWS = 256
MOLS = 3
NSTACK = 4
STEP = 7
MOST = 192
BLOCKS = 32
TOKENS = 8192


def spiked(entries, stream_key, source, target, parts, factor):
    def block_of(axis_at):
        return (jnp.arange(entries.shape[axis_at]) // (entries.shape[axis_at] // parts)).reshape((-1,) + (1,) * (entries.ndim - 1 - axis_at))

    one_side = jax.random.permutation(stream_key, parts)[block_of(target)]
    other_side = (block_of(target) + parts // 2) % parts
    return jnp.where((block_of(source) == one_side) | (block_of(source) == other_side), factor * entries, entries)


def block_scale(own_key, shape, split, smallest, top_value):
    def one(axis_at, blocks):
        steps = jax.random.uniform(jax.random.fold_in(jax.random.fold_in(own_key, 6), axis_at), (blocks,), jnp.float32, smallest / len(split), top_value / len(split))
        return jnp.repeat(jnp.exp(steps), shape[axis_at] // blocks).reshape((-1,) + (1,) * (len(shape) - axis_at - 1))

    level = one(*split[0])
    for cut in split[1:]:
        level = level * one(*cut)
    return level


def profile(number_of, total, limit, lean):
    loads = [(1 << 20) // math.isqrt(grade ** lean) + 1 for grade in range(2, number_of + 1)]
    surplus, given = total - limit - (number_of - 1), [1] * (number_of - 1)
    while surplus > 0:
        free = [i for i in range(number_of - 1) if given[i] < limit]
        mass, left = sum([loads[i] for i in free]), surplus
        for i in free:
            more = min(limit - given[i], max(1, left * loads[i] // mass), surplus)
            given[i] = given[i] + more
            surplus = surplus - more
    return np.array([limit] + given)


def ragged(stream_key, number_of, total, most, skew):
    if number_of == 2:
        one = jax.random.randint(stream_key, (), max(1, total - most), min(most, total - 1) + 1)
        return jnp.stack([one, total - one])
    tallies = jnp.asarray(profile(number_of, total, most, skew), jnp.int32)
    twos = (number_of - 1) // 2
    donor, sink = tallies[1:1 + 2 * twos:2], tallies[2:2 + 2 * twos:2]
    slack = jnp.minimum(donor - 1, most - sink)
    passed = jax.random.randint(jax.random.fold_in(stream_key, 1), (twos,), 0, 1 << 20) % (slack + 1)
    tallies = tallies.at[1:1 + 2 * twos:2].set(donor - passed).at[2:2 + 2 * twos:2].set(sink + passed)
    return tallies[jax.random.permutation(jax.random.fold_in(stream_key, 2), number_of)]


def bell_draw(stream_key, extent, scale, bound, split=(), held_as=jnp.bfloat16):
    values = jax.random.normal(stream_key, extent, jnp.float32) * scale
    if len(split) > 0:
        values = block_scale(stream_key, extent, split, -0.22, 0.18) * values
    return jnp.clip(values, min=-bound, max=bound).astype(held_as)


def gaussian_with(stream_key, extent, deviation, reach, split, heavy, kind=jnp.bfloat16):
    values = deviation * jax.random.normal(stream_key, extent, jnp.float32)
    if split:
        values = values * block_scale(stream_key, extent, split, -0.22, 0.18)
    return jnp.clip(spiked(values, jax.random.fold_in(stream_key, 3), *heavy), -reach, reach).astype(kind)


def setup_inputs(seed: int = 0) -> dict:
    arg_keys = jax.random.split(jax.random.key(seed), 13)
    inputs = gaussian_with(arg_keys[0], (TOKENS, D), 1.0, 6.0, ((0, 16),), (0, 1, 16, 2.0))
    cotangent = bell_draw(arg_keys[1], (TOKENS, D), 1.0, 6.0, ((0, 16),))
    lengths = jax.vmap(lambda own: ragged(own, MOLS + 1, ROWS, MOST, 2))(jax.random.split(arg_keys[2], BLOCKS)).reshape((BLOCKS, MOLS + 1)).astype(jnp.int32)
    proj_stack = bell_draw(arg_keys[3], (NSTACK, HEAD, FEAT), 1.0, 6.0, (), jnp.float32)
    gain_one = jnp.clip(1.0 + 0.18 * jax.random.normal(arg_keys[4], (2, D), jnp.float32), 0.1, 1.9)
    bias_one = bell_draw(arg_keys[5], (2, D), 0.3, 1.5, ((0, 2),), jnp.float32)
    w_qkv = bell_draw(arg_keys[6], (2, D, 3 * D), D ** -0.5, 0.21875, ((0, 2),))
    w_out = bell_draw(arg_keys[7], (2, D, D), (D // 8) ** -0.5, 0.625, ((0, 2),))
    gain_two = jnp.clip(1.0 + 0.18 * jax.random.normal(arg_keys[8], (2, D), jnp.float32), 0.1, 1.9)
    bias_two = bell_draw(arg_keys[9], (2, D), 0.3, 1.5, ((0, 2),), jnp.float32)
    w_up = bell_draw(arg_keys[10], (2, D, FF), D ** -0.5, 0.21875, ((0, 2),))
    w_down = bell_draw(arg_keys[11], (2, FF, D), FF ** -0.5, 0.109375, ((0, 2),))
    return dict(inputs=inputs, cotangent=cotangent, lengths=lengths, proj_stack=proj_stack, gain_one=gain_one, bias_one=bias_one, w_qkv=w_qkv, w_out=w_out, gain_two=gain_two, bias_two=bias_two, w_up=w_up, w_down=w_down)


EPSILON = 1e-05
PRECISE = lax.Precision.HIGHEST

@jax.custom_vjp
def low(v):
    return lax.optimization_barrier(v.astype(jnp.bfloat16)).astype(jnp.float32)

@jax.custom_vjp
def low_back(v):
    return v

def low_keep(v):
    return (low(v), None)

def low_pass(kept, grad):
    return (grad,)

def back_keep(v):
    return (v, None)

def back_low(kept, grad):
    return (low(grad),)
low.defvjp(low_keep, low_pass)
low_back.defvjp(back_keep, back_low)

def mult(left_side, right_side):
    return jnp.dot(left_side, right_side, precision=PRECISE, preferred_element_type=jnp.float32)

def normalize(hidden):
    average = lax.optimization_barrier(jnp.mean(hidden, axis=-1, keepdims=True))
    centred = hidden - average
    inverse = lax.rsqrt(lax.optimization_barrier(jnp.mean(centred * centred, axis=-1, keepdims=True)) + EPSILON)
    return centred * inverse

def layout(counts, row_count):
    counts = counts.astype(jnp.int32)
    closing = jnp.cumsum(counts).astype(jnp.int32)
    opening = (closing - counts).astype(jnp.int32)
    row_index = lax.broadcasted_iota(jnp.int32, (row_count, counts.shape[0]), 0)
    inside = jnp.logical_and(row_index >= opening[None, :], row_index < closing[None, :])
    member = inside[:, :-1].astype(jnp.float32)
    offset = lax.optimization_barrier(jnp.sum(member * opening[None, :-1].astype(jnp.float32), axis=1))
    position = lax.broadcasted_iota(jnp.float32, (row_count,), 0) - offset
    return (member, position)

def rotary_tables(position, head_size):
    half_size = head_size // 2
    frequency = 10000.0 ** (-2.0 * lax.broadcasted_iota(jnp.float32, (half_size,), 0) / head_size)
    angles = position[:, None] * frequency[None, :]
    cosine = jnp.concatenate([jnp.cos(angles), jnp.cos(angles)], axis=1)
    sine_table = jnp.concatenate([jnp.sin(angles), jnp.sin(angles)], axis=1)
    return (cosine, sine_table)

def rotate_half(vectors):
    half_size = vectors.shape[-1] // 2
    return jnp.concatenate([-vectors[..., half_size:], vectors[..., :half_size]], axis=-1)

def turn_heads(vectors, cosine, sine_table):
    return vectors * cosine[:, None, :] + rotate_half(vectors) * sine_table[:, None, :]

def features(rotated, projection):
    scaled = rotated * rotated.shape[-1] ** (-0.25)
    lifted = jnp.einsum('rhe,ef->rhf', scaled, projection, precision=PRECISE)
    return jnp.exp(lifted - 0.5 * lax.optimization_barrier(jnp.sum(scaled * scaled, axis=-1, keepdims=True))) / math.sqrt(projection.shape[-1])

def spread_rows(member, values):
    return jnp.transpose(member)[:, :, None, None] * values[None]

def linear_attention(phi_query, phi_key, values, member):
    key_parts = spread_rows(member, phi_key)
    query_parts = spread_rows(member, phi_query)
    kv_state = jnp.einsum('srhf,rhe->shfe', key_parts, values, precision=PRECISE)
    totals = lax.optimization_barrier(jnp.sum(key_parts, axis=1))
    numerator = jnp.einsum('srhf,shfe->rhe', query_parts, kv_state, precision=PRECISE)
    denominator = jnp.einsum('srhf,shf->rh', query_parts, totals, precision=PRECISE)
    denominator = jnp.where(lax.optimization_barrier(jnp.sum(member, axis=1))[:, None] > 0.5, denominator, 1.0)
    return numerator / denominator[:, :, None]

def layer(hidden, weights, member, cosine, sine_table, projection):
    gain_first, bias_first, qkv_weight, out_weight, gain_second, bias_second, up_weight, down_weight = weights
    entry = low(normalize(hidden) * gain_first + bias_first)
    projected = low_back(mult(entry, qkv_weight))
    query = turn_heads(projected[:, :D].reshape(ROWS, HEADS, HEAD), cosine, sine_table)
    keyed = turn_heads(projected[:, D:2 * D].reshape(ROWS, HEADS, HEAD), cosine, sine_table)
    values = projected[:, 2 * D:].reshape(ROWS, HEADS, HEAD)
    mixed = linear_attention(features(query, projection), features(keyed, projection), values, member)
    mixed = low(mixed.reshape(ROWS, D))
    middle = hidden + low_back(mult(mixed, out_weight))
    second = low(normalize(middle) * gain_second + bias_second)
    upward = low_back(mult(second, up_weight))
    activated = low(jax.nn.gelu(upward, approximate=False))
    return middle + low_back(mult(activated, down_weight))

def two_layers(block_in, block_delta, counts, weights, projection):
    member, position = layout(counts, ROWS)
    cosine, sine_table = rotary_tables(position, HEAD)
    first_weights = jax.tree.map(lambda weight: weight[0], weights)
    second_weights = jax.tree.map(lambda weight: weight[1], weights)
    handed = low(layer(block_in, first_weights, member, cosine, sine_table, projection))
    second_in = low_back(handed + block_delta)
    return (layer(second_in, second_weights, member, cosine, sine_table, projection), handed)

def reference(inputs, cotangent, lengths, proj_stack, gain_one, bias_one, w_qkv, w_out, gain_two, bias_two, w_up, w_down):
    projection = proj_stack[STEP % NSTACK]
    blocks = lengths.shape[0]
    start_in = inputs.astype(jnp.float32).reshape(blocks, ROWS, D)
    delta_zero = jnp.zeros((blocks, ROWS, D), jnp.float32)
    weights = (gain_one, bias_one, w_qkv.astype(jnp.float32), w_out.astype(jnp.float32), gain_two, bias_two, w_up.astype(jnp.float32), w_down.astype(jnp.float32))

    def forward(block_inputs, block_deltas, weight_set):

        def advance(carried, pieces):
            outcome, handed = jax.checkpoint(two_layers)(pieces[0], pieces[1], pieces[2], weight_set, projection)
            return (carried, (outcome, handed))
        _, (outcomes, handed_all) = lax.scan(advance, jnp.zeros((), jnp.float32), (block_inputs, block_deltas, lengths))
        return (outcomes, handed_all)
    outcomes, pullback, handed_all = jax.vjp(forward, start_in, delta_zero, weights, has_aux=True)
    grad_start, grad_delta, grad_weights = pullback(cotangent.astype(jnp.float32).reshape(blocks, ROWS, D))
    total_rows = blocks * ROWS
    layer_out = jnp.stack([handed_all.reshape(total_rows, D), outcomes.reshape(total_rows, D)]).astype(jnp.bfloat16)
    grad_in = jnp.stack([grad_start.reshape(total_rows, D), grad_delta.reshape(total_rows, D)])
    return (layer_out, grad_in, grad_weights[0], grad_weights[1], grad_weights[2], grad_weights[3], grad_weights[4], grad_weights[5], grad_weights[6], grad_weights[7])
```

```python
import functools
import math

import jax
import jax.numpy as jnp
from jax import lax
from jax.experimental import pallas as pl
from jax.experimental.pallas import tpu as pltpu
from jax.sharding import PartitionSpec as P

D = 768
HEADS = 12
HEAD = 64
FEAT = 32
FF = 3072
ROWS = 256
MOLS = 3
NSTACK = 4
STEP = 7
EPSILON = 1e-05

PACK = 4
GROUPS = HEADS // PACK
WIDE = PACK * HEAD
THIN = PACK * FEAT
SPREAD = MOLS * THIN
CHUNK = 512
CHUNKS = FF // CHUNK
SCALE = HEAD ** -0.25
VMEM_LIMIT = 56 * 1024 * 1024

F32 = jnp.float32
BF16 = jnp.bfloat16

KEPT = (
    ("hidden", ROWS, D, BF16),
    ("entry", ROWS, D, BF16),
    ("turned_q", ROWS, D, F32),
    ("turned_k", ROWS, D, F32),
    ("value", ROWS, D, BF16),
    ("phi_q", ROWS, GROUPS * THIN, F32),
    ("phi_k", ROWS, GROUPS * THIN, F32),
    ("state", GROUPS * SPREAD, 2 * WIDE, BF16),
    ("inv_den", ROWS, D, F32),
    ("mixed", ROWS, D, BF16),
    ("middle", ROWS, D, F32),
    ("second", ROWS, D, BF16),
    ("activated", ROWS, FF, BF16),
    ("slope", ROWS, FF, BF16),
    ("cosine", ROWS, 2 * HEAD, F32),
    ("sine", ROWS, 2 * HEAD, F32),
    ("layer_out", ROWS, D, BF16),
)
LEFT = (
    ("grad_ffn", ROWS, D, BF16),
    ("grad_up", ROWS, FF, BF16),
    ("grad_attn", ROWS, D, BF16),
    ("grad_proj", ROWS, 3 * D, BF16),
    ("grad_in", ROWS, D, F32),
    ("vectors", 8, D, F32),
)
TAKEN = tuple(k for k in KEPT if k[0] not in ("entry", "second", "activated", "layer_out"))


def dot(a, b):
    return jnp.dot(a, b, preferred_element_type=F32)


def dot_nt(a, b):
    return lax.dot_general(a, b, (((1,), (1,)), ((), ())), preferred_element_type=F32)


def dot_tn(a, b):
    return lax.dot_general(a, b, (((0,), (0,)), ((), ())), preferred_element_type=F32)


def normalize(hidden):
    average = jnp.mean(hidden, axis=-1, keepdims=True)
    centred = hidden - average
    inverse = lax.rsqrt(jnp.mean(centred * centred, axis=-1, keepdims=True) + EPSILON)
    return centred * inverse, inverse


def normalize_back(grad_normed, normed, inverse):
    return inverse * (
        grad_normed
        - jnp.mean(grad_normed, axis=-1, keepdims=True)
        - normed * jnp.mean(grad_normed * normed, axis=-1, keepdims=True)
    )


def iota(shape, axis):
    return lax.broadcasted_iota(jnp.int32, shape, axis)


def molecules(lengths, micro):
    row = iota((ROWS, THIN), 0)
    which = jnp.full((ROWS, THIN), MOLS, jnp.int32)
    first = jnp.zeros((ROWS, THIN), jnp.int32)
    opening = jnp.int32(0)
    for s in range(MOLS):
        closing = opening + lengths[micro, s]
        inside = (row >= opening) & (row < closing)
        which = jnp.where(inside, s, which)
        first = jnp.where(inside, opening, first)
        opening = closing
    return which, (row - first).astype(F32)


def tables(position):
    lane = iota((ROWS, 2 * HEAD), 1)
    index = (lane % (HEAD // 2)).astype(F32)
    angles = position * jnp.exp(index * (-2.0 * math.log(10000.0) / HEAD))
    sine = jnp.sin(angles)
    return jnp.cos(angles), jnp.where(lane % HEAD < HEAD // 2, -sine, sine)


def swap_halves(x):
    half = HEAD // 2
    width = x.shape[1]
    low = iota(x.shape, 1) % HEAD < half
    return jnp.where(low, pltpu.roll(x, width - half, 1), pltpu.roll(x, half, 1))


def twice(x):
    return jnp.concatenate([x, x], axis=1)


def block_diagonal(projection):
    tiled = jnp.concatenate([projection] * PACK, axis=1)
    tiled = jnp.concatenate([tiled] * PACK, axis=0)
    same = iota((WIDE, THIN), 0) // HEAD == iota((WIDE, THIN), 1) // FEAT
    return jnp.where(same, tiled, 0.0), same.astype(F32)


def two_parts(x):
    high = x.astype(BF16)
    return high, (x - high.astype(F32)).astype(BF16)


def features(turned, proj_both, proj_high, norm_part):
    scaled = turned * SCALE
    high, low = two_parts(scaled)
    square_high, square_low = two_parts(scaled * scaled)
    both = dot(high, proj_both)
    lifted = both[:, :THIN] + both[:, THIN:] + dot(low, proj_high)
    lifted = lifted + dot(square_high, norm_part) + dot(square_low, norm_part)
    return jnp.exp(lifted) * (1.0 / math.sqrt(FEAT))


def spread(which, phi):
    return jnp.concatenate(
        [jnp.where(which == s, phi, 0.0).astype(BF16) for s in range(MOLS)], axis=1
    )


def gather(which, parts):
    total = jnp.zeros((ROWS, THIN), F32)
    for s in range(MOLS):
        total = jnp.where(which == s, parts[:, s * THIN : (s + 1) * THIN], total)
    return total


def own_head(state):
    row_head = (iota(state.shape, 0) // FEAT) % PACK
    col_head = (iota(state.shape, 1) // HEAD) % PACK
    return jnp.where(row_head == col_head, state, 0.0).astype(BF16)


def gelu_and_slope(u):
    bell = jnp.exp(-0.5 * u * u)
    t = 1.0 / (1.0 + jnp.abs(u) * (0.3275911 * math.sqrt(0.5)))
    tail = 0.5 * 1.061405429
    for c in (-1.453152027, 1.421413741, -0.284496736, 0.254829592):
        tail = tail * t + 0.5 * c
    tail = tail * t * bell
    phi = jnp.where(u >= 0.0, 1.0 - tail, tail)
    return u * phi, phi + u * bell * (1.0 / math.sqrt(2.0 * math.pi))


class Copies:
    def __init__(self, semaphores):
        self.semaphores = semaphores
        self.count = 0

    def next(self):
        self.count += 1
        return self.semaphores.at[self.count - 1]

    def start(self, source, target):
        copy = pltpu.make_async_copy(source, target, self.next())
        copy.start()
        return copy

    def either(self, condition, source, other, target):
        semaphore = self.next()
        copy = pltpu.make_async_copy(source, target, semaphore)

        @pl.when(condition)
        def _():
            copy.start()

        @pl.when(jnp.logical_not(condition))
        def _():
            pltpu.make_async_copy(other, target, semaphore).start()

        return copy


def forward_kernel(step, micros, given, lengths, *refs):
    refs = list(refs)
    inputs, arrived, gain1, bias1, gain2, bias2, stack, w_qkv, w_out, w_up, w_down = refs[:11]
    refs = refs[11 + given :]
    kept = dict(zip([k[0] for k in KEPT], refs[: len(KEPT)]))
    outgoing = refs[len(KEPT)]
    refs = refs[len(KEPT) + 1 :]
    held = dict(zip([k[0] for k in KEPT], refs[: len(KEPT)]))
    (v_gain1, v_bias1, v_gain2, v_bias2, v_proj, v_qkv, v_out, v_up, v_down, semaphores) = refs[
        len(KEPT) :
    ]
    core = lax.axis_index("pipe")
    micro = step - core

    @pl.when((micro >= 0) & (micro < micros))
    def _():
        copies = Copies(semaphores)
        rows = pl.ds(pl.multiple_of(micro * ROWS, ROWS), ROWS)
        first = copies.either(core == 0, inputs.at[rows], arrived, held["hidden"])

        small = [
            copies.start(a, b)
            for a, b in (
                (gain1, v_gain1),
                (bias1, v_bias1),
                (gain2, v_gain2),
                (bias2, v_bias2),
                (stack.at[STEP % NSTACK], v_proj),
            )
        ]
        load_qkv = copies.start(w_qkv.at[0], v_qkv)
        load_out = copies.start(w_out.at[0], v_out)
        load_ffn = []
        for c in range(CHUNKS):
            columns = pl.ds(c * CHUNK, CHUNK)
            load_ffn.append(
                (
                    copies.start(w_up.at[0, :, columns], v_up.at[c]),
                    copies.start(w_down.at[0, columns], v_down.at[c]),
                )
            )
        saves = []

        def save(name):
            size = held[name].shape[0]
            at = pl.ds(pl.multiple_of(micro * size, size), size)
            saves.append(copies.start(held[name], kept[name].at[at]))

        which, position = molecules(lengths, micro)
        cosine, sine = tables(position)
        held["cosine"][...] = cosine
        held["sine"][...] = sine
        save("cosine")
        save("sine")
        cosine, sine = twice(cosine), twice(sine)
        for copy in small:
            copy.wait()
        proj_block, own = block_diagonal(v_proj[...])
        proj_high, proj_low = two_parts(proj_block)
        proj_both = jnp.concatenate([proj_high, proj_low], axis=1)
        norm_part = (-0.5 * own).astype(BF16)

        first.wait()
        save("hidden")
        hidden = held["hidden"][...].astype(F32)
        normed, _ = normalize(hidden)
        entry = (normed * v_gain1[...] + v_bias1[...]).astype(BF16)
        held["entry"][...] = entry
        save("entry")
        load_qkv.wait()
        ones = jnp.ones((ROWS, WIDE), BF16)
        for g in range(GROUPS):
            cols = slice(g * WIDE, (g + 1) * WIDE)
            thin = slice(g * THIN, (g + 1) * THIN)
            deep = slice(g * SPREAD, (g + 1) * SPREAD)
            query = dot(entry, v_qkv[:, g * WIDE : (g + 1) * WIDE])
            key = dot(entry, v_qkv[:, D + g * WIDE : D + (g + 1) * WIDE])
            value = dot(entry, v_qkv[:, 2 * D + g * WIDE : 2 * D + (g + 1) * WIDE]).astype(BF16)
            query = query * cosine + swap_halves(query) * sine
            key = key * cosine + swap_halves(key) * sine
            phi_q = features(query, proj_both, proj_high, norm_part)
            phi_k = features(key, proj_both, proj_high, norm_part)
            held["turned_q"][:, cols] = query
            held["turned_k"][:, cols] = key
            held["value"][:, cols] = value
            held["phi_q"][:, thin] = phi_q
            held["phi_k"][:, thin] = phi_k
            state = own_head(dot_tn(spread(which, phi_k), jnp.concatenate([value, ones], axis=1)))
            held["state"][deep, :] = state
            both = dot(spread(which, phi_q), state)
            inside = twice(which) < MOLS
            inverse = jnp.where(inside, 1.0 / jnp.where(inside, both[:, WIDE:], 1.0), 0.0)
            held["inv_den"][:, cols] = inverse
            held["mixed"][:, cols] = (both[:, :WIDE] * inverse).astype(BF16)
        for name in ("turned_q", "turned_k", "value", "phi_q", "phi_k", "state", "inv_den", "mixed"):
            save(name)
        load_out.wait()
        middle = hidden + dot(held["mixed"][...], v_out[...])
        held["middle"][...] = middle
        save("middle")
        normed, _ = normalize(middle)
        second = (normed * v_gain2[...] + v_bias2[...]).astype(BF16)
        held["second"][...] = second
        save("second")

        total = middle
        for copy in load_ffn[0]:
            copy.wait()
        upward = dot(second, v_up[0])
        for c in range(CHUNKS):
            if c + 1 < CHUNKS:
                for copy in load_ffn[c + 1]:
                    copy.wait()
                upcoming = dot(second, v_up[c + 1])
            activated, slope = gelu_and_slope(upward)
            activated = activated.astype(BF16)
            held["activated"][:, c * CHUNK : (c + 1) * CHUNK] = activated
            held["slope"][:, c * CHUNK : (c + 1) * CHUNK] = slope.astype(BF16)
            total = total + dot(activated, v_down[c])
            if c + 1 < CHUNKS:
                upward = upcoming
        save("activated")
        save("slope")
        held["layer_out"][...] = total.astype(BF16)
        save("layer_out")
        saves.append(copies.start(held["layer_out"], outgoing))
        for copy in saves:
            copy.wait()


def backward_kernel(step, micros, given, *refs):
    refs = list(refs)
    cotangent, arrived, gain1, gain2, stack, lengths, w_qkv, w_out, w_up, w_down = refs[:10]
    taken = dict(zip([k[0] for k in TAKEN], refs[10 : 10 + len(TAKEN)]))
    refs = refs[10 + len(TAKEN) + given :]
    left = dict(zip([k[0] for k in LEFT], refs[: len(LEFT)]))
    outgoing = refs[len(LEFT)]
    refs = refs[len(LEFT) + 1 :]
    have = dict(zip([k[0] for k in TAKEN], refs[: len(TAKEN)]))
    refs = refs[len(TAKEN) :]
    held = dict(zip([k[0] for k in LEFT], refs[: len(LEFT)]))
    (v_send, v_gain1, v_gain2, v_proj, v_qkv, v_out, v_up, v_down, semaphores) = refs[len(LEFT) :]
    core = lax.axis_index("pipe")
    micro = step - (1 - core)

    @pl.when((micro >= 0) & (micro < micros))
    def _():
        copies = Copies(semaphores)
        rows = pl.ds(pl.multiple_of(micro * ROWS, ROWS), ROWS)
        first = copies.either(core != 0, cotangent.at[rows], arrived, held["grad_ffn"])

        loads = {}

        def load(name):
            size = have[name].shape[0]
            at = pl.ds(pl.multiple_of(micro * size, size), size)
            loads[name] = copies.start(taken[name].at[at], have[name])

        load("slope")
        load_ffn = []
        for c in range(CHUNKS):
            columns = pl.ds(c * CHUNK, CHUNK)
            load_ffn.append(
                (
                    copies.start(w_down.at[0, columns], v_down.at[c]),
                    copies.start(w_up.at[0, :, columns], v_up.at[c]),
                )
            )
        small = [
            copies.start(a, b)
            for a, b in ((gain1, v_gain1), (gain2, v_gain2), (stack.at[STEP % NSTACK], v_proj))
        ]
        load("middle")
        load_out = copies.start(w_out.at[0], v_out)
        for name, *_ in TAKEN:
            if name not in loads:
                load(name)
        load_qkv = copies.start(w_qkv.at[0], v_qkv)
        saves = []

        def save(name):
            size = held[name].shape[0]
            at = pl.ds(pl.multiple_of(micro * size, size), size)
            saves.append(copies.start(held[name], left[name].at[at]))

        which, _ = molecules(lengths, micro)
        first.wait()
        save("grad_ffn")
        grad_ffn = held["grad_ffn"][...]
        loads["slope"].wait()
        for copy in load_ffn[0]:
            copy.wait()
        grad_act = dot_nt(grad_ffn, v_down[0])
        grad_second = None
        for c in range(CHUNKS):
            if c + 1 < CHUNKS:
                for copy in load_ffn[c + 1]:
                    copy.wait()
                upcoming = dot_nt(grad_ffn, v_down[c + 1])
            cols = slice(c * CHUNK, (c + 1) * CHUNK)
            grad_up = (grad_act * have["slope"][:, cols].astype(F32)).astype(BF16)
            held["grad_up"][:, cols] = grad_up
            piece = dot_nt(grad_up, v_up[c])
            grad_second = piece if grad_second is None else grad_second + piece
            if c + 1 < CHUNKS:
                grad_act = upcoming
        save("grad_up")
        loads["middle"].wait()
        for copy in small:
            copy.wait()
        normed, inverse = normalize(have["middle"][...])
        gain_two = jnp.sum(grad_second * normed, axis=0, keepdims=True)
        bias_two = jnp.sum(grad_second, axis=0, keepdims=True)
        grad_middle = grad_ffn.astype(F32) + normalize_back(
            grad_second * v_gain2[...], normed, inverse
        )
        grad_attn = grad_middle.astype(BF16)
        held["grad_attn"][...] = grad_attn
        save("grad_attn")

        proj_block, own = block_diagonal(v_proj[...])
        back_part = jnp.concatenate([proj_block, own], axis=0).astype(BF16)
        load_out.wait()
        for name, copy in loads.items():
            if name not in ("slope", "middle"):
                copy.wait()
        load_qkv.wait()
        cosine, sine = twice(have["cosine"][...]), twice(have["sine"][...])
        same = iota((WIDE, WIDE), 0) // HEAD == iota((WIDE, WIDE), 1) // HEAD
        per_head = jnp.where(same, -1.0, 0.0).astype(BF16)
        part = jnp.full((ROWS, WIDE), 1.0 / HEAD, BF16)
        grad_entry = None
        for g in range(GROUPS):
            cols = slice(g * WIDE, (g + 1) * WIDE)
            thin = slice(g * THIN, (g + 1) * THIN)
            deep = slice(g * SPREAD, (g + 1) * SPREAD)
            grad_mixed = dot_nt(grad_attn, v_out[cols, :])
            value = have["value"][:, cols]
            state = have["state"][deep, :]
            phi_q = have["phi_q"][:, thin]
            phi_k = have["phi_k"][:, thin]
            grad_num = grad_mixed * have["inv_den"][:, cols]
            grad_den = dot((grad_num * have["mixed"][:, cols].astype(F32)).astype(BF16), per_head)
            grad_num = grad_num.astype(BF16)
            query_back = jnp.concatenate([grad_num, (grad_den * (1.0 / HEAD)).astype(BF16)], axis=1)
            grad_phi_q = gather(which, dot_nt(query_back, state))
            query_forth = jnp.concatenate([grad_num, grad_den.astype(BF16)], axis=1)
            grad_state = own_head(dot_tn(spread(which, phi_q), query_forth))
            grad_phi_k = gather(which, dot_nt(jnp.concatenate([value, part], axis=1), grad_state))
            grad_value = dot(spread(which, phi_k), grad_state[:, :WIDE])

            def features_back(grad_phi, phi, turned):
                back = dot_nt((grad_phi * phi).astype(BF16), back_part)
                grad = (back[:, :WIDE] - turned * SCALE * back[:, WIDE:]) * SCALE
                return (grad * cosine + swap_halves(grad * sine)).astype(BF16)

            grad_query = features_back(grad_phi_q, phi_q, have["turned_q"][:, cols])
            grad_key = features_back(grad_phi_k, phi_k, have["turned_k"][:, cols])
            for i, piece in enumerate((grad_query, grad_key, grad_value.astype(BF16))):
                at = slice(i * D + g * WIDE, i * D + (g + 1) * WIDE)
                held["grad_proj"][:, at] = piece
                piece = dot_nt(piece, v_qkv[:, at])
                grad_entry = piece if grad_entry is None else grad_entry + piece
        save("grad_proj")
        normed, inverse = normalize(have["hidden"][...].astype(F32))
        gain_one = jnp.sum(grad_entry * normed, axis=0, keepdims=True)
        bias_one = jnp.sum(grad_entry, axis=0, keepdims=True)
        held["vectors"][...] = jnp.concatenate(
            [gain_one, bias_one, gain_two, bias_two, jnp.zeros((4, D), F32)], axis=0
        )
        save("vectors")
        grad_hidden = grad_middle + normalize_back(grad_entry * v_gain1[...], normed, inverse)
        rounded = grad_hidden.astype(BF16)
        v_send[...] = rounded
        saves.append(copies.start(v_send, outgoing))
        held["grad_in"][...] = jnp.where(core == 0, grad_hidden, rounded.astype(F32))
        save("grad_in")
        for copy in saves:
            copy.wait()


ANYWHERE = pl.BlockSpec(memory_space=pl.ANY)
SMALL = pl.BlockSpec(memory_space=pltpu.SMEM)


def forward(step, micros, lengths, operands, before):
    shapes = [jax.ShapeDtypeStruct((micros * r, c), t) for _, r, c, t in KEPT]
    shapes.append(jax.ShapeDtypeStruct((ROWS, D), BF16))
    given = len(before)
    return pl.pallas_call(
        functools.partial(forward_kernel, step, micros, given),
        out_shape=shapes,
        in_specs=[SMALL] + [ANYWHERE] * (11 + given),
        out_specs=[ANYWHERE] * len(shapes),
        input_output_aliases={12 + i: i for i in range(given)},
        scratch_shapes=[pltpu.VMEM((r, c), t) for _, r, c, t in KEPT]
        + [pltpu.VMEM((1, D), F32)] * 4
        + [
            pltpu.VMEM((HEAD, FEAT), F32),
            pltpu.VMEM((D, 3 * D), BF16),
            pltpu.VMEM((D, D), BF16),
            pltpu.VMEM((CHUNKS, D, CHUNK), BF16),
            pltpu.VMEM((CHUNKS, CHUNK, D), BF16),
            pltpu.SemaphoreType.DMA((64,)),
        ],
        compiler_params=pltpu.CompilerParams(vmem_limit_bytes=VMEM_LIMIT),
        cost_estimate=pl.CostEstimate(flops=8 * 10**9, bytes_accessed=25 * 10**6, transcendentals=0),
        name="layer_forward",
    )(lengths, *operands, *before)


def backward(step, micros, operands, kept, before):
    shapes = [jax.ShapeDtypeStruct((micros * r, c), t) for _, r, c, t in LEFT]
    shapes.append(jax.ShapeDtypeStruct((ROWS, D), BF16))
    given = len(before)
    taken = [kept[k[0]] for k in TAKEN]
    first = 10 + len(TAKEN)
    return pl.pallas_call(
        functools.partial(backward_kernel, step, micros, given),
        out_shape=shapes,
        in_specs=[ANYWHERE] * 5 + [SMALL] + [ANYWHERE] * (4 + len(TAKEN) + given),
        out_specs=[ANYWHERE] * len(shapes),
        input_output_aliases={first + i: i for i in range(given)},
        scratch_shapes=[pltpu.VMEM((r, c), t) for _, r, c, t in TAKEN]
        + [pltpu.VMEM((r, c), t) for _, r, c, t in LEFT]
        + [pltpu.VMEM((ROWS, D), BF16)]
        + [pltpu.VMEM((1, D), F32)] * 2
        + [
            pltpu.VMEM((HEAD, FEAT), F32),
            pltpu.VMEM((D, 3 * D), BF16),
            pltpu.VMEM((D, D), BF16),
            pltpu.VMEM((CHUNKS, D, CHUNK), BF16),
            pltpu.VMEM((CHUNKS, CHUNK, D), BF16),
            pltpu.SemaphoreType.DMA((64,)),
        ],
        compiler_params=pltpu.CompilerParams(vmem_limit_bytes=VMEM_LIMIT),
        cost_estimate=pl.CostEstimate(flops=8 * 10**9, bytes_accessed=25 * 10**6, transcendentals=0),
        name="layer_backward",
    )(*operands, *taken, *before)


CORNERS = (1, 2, 4, 8)
VECTORS = -1
DOWN_PLAN = (((0, 0, 384),), ((0, 384, 384),))
UP_PLAN = (
    ((0, 0, 512), (0, 512, 512), (0, 1024, 512)),
    ((0, 1536, 512), (0, 2048, 512), (0, 2560, 512)),
)
ATTN_PLAN = (
    ((0, 0, 512), (0, 512, 512), (0, 1024, 512)),
    ((0, 1536, 512), (0, 2048, 256), (1, 0, 512), (1, 512, 256), (VECTORS, 0, 128)),
)


def product_kernel(shard, pairs, plan, *refs):
    refs = list(refs)
    lefts, rights, vectors, refs = refs[:pairs], refs[pairs : 2 * pairs], refs[2 * pairs], refs[2 * pairs + 1 :]
    outs, refs = refs[: 4 * len(plan)], refs[4 * len(plan) :]
    v_left, v_right, v_turned = refs[:pairs], refs[pairs : 2 * pairs], refs[2 * pairs : 3 * pairs]
    refs = refs[3 * pairs :]
    v_vectors, v_out, semaphores = refs[0], refs[1 : 1 + len(plan)], refs[1 + len(plan)]
    copies = Copies(semaphores)
    me = lax.axis_index("dp")
    loads = [
        (copies.start(a, b), copies.start(c, d))
        for a, b, c, d in zip(lefts, v_left, rights, v_right)
    ]
    load_vectors = copies.start(vectors, v_vectors)
    for i in range(pairs):
        loads[i][0].wait()
        v_turned[i][...] = v_left[i][...].T
    for i in range(pairs):
        loads[i][1].wait()
    load_vectors.wait()
    rows = v_turned[0].shape[0]
    saves = []
    for group, tiles in enumerate(plan):
        at = 0
        for pair, first, width in tiles:
            if pair == VECTORS:
                total = jnp.sum(v_vectors[...].reshape(-1, 8, D), axis=0)
                total = jnp.concatenate([total, jnp.zeros((width - 8, D), F32)], axis=0)
                v_out[group][:, at : at + width] = total.T.astype(BF16)
            else:
                for r in range(0, rows, D):
                    got = dot(v_turned[pair][r : r + D], v_right[pair][:, first : first + width])
                    v_out[group][r : r + D, at : at + width] = got.astype(BF16)
            at += width
        for quarter in range(4):
            for slot in range(4):
                block = me ^ (quarter + (4, 8)[0] * (slot // 2) + (4, 8)[1] * (slot % 2))
                source = pl.ds(pl.multiple_of(block * shard, 16), shard)
                target = outs[group * 4 + quarter].at[pl.ds(slot * shard, shard)]
                saves.append(copies.start(v_out[group].at[source], target))
    for copy in saves:
        copy.wait()


def product(lefts, rights, vectors, plan, count):
    rows = lefts[0].shape[1]
    shard = rows // count
    widths = [sum(t[2] for t in tiles) for tiles in plan]
    pairs = len(lefts)
    return pl.pallas_call(
        functools.partial(product_kernel, shard, pairs, plan),
        out_shape=[jax.ShapeDtypeStruct((4 * shard, w), BF16) for w in widths for _ in range(4)],
        in_specs=[ANYWHERE] * (2 * pairs + 1),
        out_specs=[ANYWHERE] * (4 * len(plan)),
        scratch_shapes=[pltpu.VMEM(x.shape, x.dtype) for x in (*lefts, *rights)]
        + [pltpu.VMEM(x.shape[::-1], x.dtype) for x in lefts]
        + [pltpu.VMEM(vectors.shape, F32)]
        + [pltpu.VMEM((rows, w), BF16) for w in widths]
        + [pltpu.SemaphoreType.DMA((64,))],
        compiler_params=pltpu.CompilerParams(vmem_limit_bytes=VMEM_LIMIT),
        cost_estimate=pl.CostEstimate(flops=5 * 10**9, bytes_accessed=10**7, transcendentals=0),
        name="weight_products",
    )(*lefts, *rights, vectors)


def corner_sum(quarters, ahead, across):
    count = lax.axis_size("dp")

    def hop(x, bit):
        return lax.ppermute(x, "dp", [(i, i ^ bit) for i in range(count)])

    kept, first, second, both = (quarters[i] for i in (0, ahead, across, ahead + across))
    forward_on = hop(both, ahead)
    stay = hop(first, ahead)
    crossed = hop((second.astype(F32) + forward_on.astype(F32)).astype(BF16), across)
    half = kept.shape[0] // 2
    shard = half // 2

    def total(rows):
        return kept[rows].astype(F32) + stay[rows].astype(F32) + crossed[rows].astype(F32)

    low = hop(total(slice(half, None)).astype(BF16), CORNERS[2])
    high = hop((total(slice(shard, half)) + low[shard:].astype(F32)).astype(BF16), CORNERS[3])
    return total(slice(0, shard)) + low[:shard].astype(F32) + high.astype(F32)


def weights_by_corners(lefts, rights, vectors):
    count = lax.axis_size("dp")
    activated, second, entry, mixed = lefts
    grad_ffn, grad_up, grad_proj, grad_attn = rights
    sums = []
    for left, right, plan in (
        ((activated,), (grad_ffn,), DOWN_PLAN),
        ((second,), (grad_up,), UP_PLAN),
        ((entry, mixed), (grad_proj, grad_attn), ATTN_PLAN),
    ):
        quarters = product(left, right, vectors, plan, count)
        sums.append(
            (
                corner_sum(quarters[:4], CORNERS[0], CORNERS[1]),
                corner_sum(quarters[4:], CORNERS[1], CORNERS[0]),
            )
        )
    down, up, (attn_low, attn_high) = sums
    rest = 3 * D - attn_low.shape[1]
    return (
        jnp.concatenate(down, axis=1),
        jnp.concatenate(up, axis=1),
        jnp.concatenate([attn_low, attn_high[:, :rest]], axis=1),
        attn_high[:, rest : rest + D],
        attn_high[:, rest + D : rest + D + 4].T,
    )


def weights_plain(lefts, rights, vectors):
    def summed(lhs, rhs):
        return lax.psum_scatter(dot_tn(lhs, rhs), "dp", scatter_dimension=0, tiled=True)

    total = jnp.sum(vectors.reshape(-1, 8, D), axis=0)
    total = lax.psum_scatter(total, "dp", scatter_dimension=1, tiled=True)
    return (*(summed(lhs, rhs) for lhs, rhs in zip(lefts, rights)), total)


def body(
    inputs,
    cotangent,
    lengths,
    proj_stack,
    gain_one,
    bias_one,
    w_qkv,
    w_out,
    gain_two,
    bias_two,
    w_up,
    w_down,
):
    micros = inputs.shape[0] // ROWS
    names = [k[0] for k in KEPT]

    before = []
    arrived = inputs[:ROWS]
    for step in range(micros + 1):
        operands = (
            inputs,
            arrived,
            gain_one,
            bias_one,
            gain_two,
            bias_two,
            proj_stack,
            w_qkv,
            w_out,
            w_up,
            w_down,
        )
        *before, outgoing = forward(step, micros, lengths, operands, before)
        if step < micros:
            arrived = lax.ppermute(outgoing, "pipe", [(0, 1)])
    kept = dict(zip(names, before))
    before = []
    arrived = cotangent[:ROWS]
    for step in range(micros + 1):
        operands = (
            cotangent,
            arrived,
            gain_one,
            gain_two,
            proj_stack,
            lengths,
            w_qkv,
            w_out,
            w_up,
            w_down,
        )
        *before, outgoing = backward(step, micros, operands, kept, before)
        if step < micros:
            arrived = lax.ppermute(outgoing, "pipe", [(1, 0)])
    left = dict(zip([k[0] for k in LEFT], before))

    lefts = (kept["activated"], kept["second"], kept["entry"], kept["mixed"])
    rights = (left["grad_ffn"], left["grad_up"], left["grad_proj"], left["grad_attn"])
    count = lax.axis_size("dp")
    if count == 2 ** len(CORNERS) and D // count % 16 == 0:
        totals = weights_by_corners(lefts, rights, left["vectors"])
    else:
        totals = weights_plain(lefts, rights, left["vectors"])
    grad_w_down, grad_w_up, grad_w_qkv, grad_w_out, vectors = totals
    return (
        kept["layer_out"][None],
        left["grad_in"][None],
        vectors[0][None],
        vectors[1][None],
        grad_w_qkv[None],
        grad_w_out[None],
        vectors[2][None],
        vectors[3][None],
        grad_w_up[None],
        grad_w_down[None],
    )


def solution(mesh):
    placed = (
        P("dp", None),
        P("dp", None),
        P("dp", None),
        P(),
        P("pipe", None),
        P("pipe", None),
        P("pipe", None, None),
        P("pipe", None, None),
        P("pipe", None),
        P("pipe", None),
        P("pipe", None, None),
        P("pipe", None, None),
    )
    return jax.shard_map(
        body,
        mesh=mesh,
        in_specs=placed,
        out_specs=(
            P("pipe", "dp", None),
            P("pipe", "dp", None),
            P("pipe", "dp"),
            P("pipe", "dp"),
            P("pipe", "dp", None),
            P("pipe", "dp", None),
            P("pipe", "dp"),
            P("pipe", "dp"),
            P("pipe", "dp", None),
            P("pipe", "dp", None),
        ),
        check_vma=False,
    )
```

```python
import math
import types

import jax
import jax.numpy as jnp
from jax import lax
from jax.experimental import pallas as pl
from jax.experimental.pallas import tpu as pltpu
from jax.sharding import PartitionSpec as P

D = 768
HEADS = 12
HEAD = 64
FEAT = 32
FF = 3072
ROWS = 256
MOLS = 3
NSTACK = 4
STEP = 7
EPSILON = 1e-05

PACK = 4
GROUPS = HEADS // PACK
WIDE = PACK * HEAD
THIN = PACK * FEAT
PAIR = 2 * HEAD
CHUNK = 512
CHUNKS = FF // CHUNK
SCALE = HEAD ** -0.25
MIB = 1024 * 1024
LIMIT = 40 * MIB

F32 = jnp.float32
BF16 = jnp.bfloat16

ATTN_KEPT = {
    "turned_q": (D, F32),
    "turned_k": (D, F32),
    "value": (D, F32),
    "phi_q": (GROUPS * THIN, F32),
    "phi_k": (GROUPS * THIN, F32),
    "middle": (D, F32),
    "cosine": (PAIR, F32),
    "sine": (PAIR, F32),
}
WEIGHTS = {
    "w_qkv": ((D, 3 * D), BF16),
    "w_out": ((D, D), BF16),
    "w_up": ((CHUNKS, D, CHUNK), BF16),
    "w_down": ((CHUNKS, CHUNK, D), BF16),
    "gains": ((4, D), F32),
    "projection": ((FEAT, HEAD), F32),
}
PLACES = {
    "entry": ("fwd_pack", 0, D),
    "mixed": ("fwd_pack", D, D),
    "second": ("fwd_pack", 2 * D, D),
    "activated": ("fwd_pack", 3 * D, FF),
    "grad_attn": ("mid_pack", 0, D),
    "grad_up": ("mid_pack", D, FF),
    "grad_proj": ("end_pack", 0, 3 * D),
    "outgoing": ("end_pack", 3 * D, D),
}
PACKS = {"fwd_pack": 3 * D + FF, "mid_pack": D + FF, "end_pack": 4 * D}


class Copies:
    def __init__(self, semaphores):
        self.semaphores = semaphores
        self.count = 0

    def start(self, source, target):
        copy = pltpu.make_async_copy(source, target, self.semaphores.at[self.count])
        self.count += 1
        copy.start()
        return copy

    def either(self, condition, source, other, target):
        semaphore = self.semaphores.at[self.count]
        self.count += 1
        copy = pltpu.make_async_copy(source, target, semaphore)

        @pl.when(condition)
        def _():
            copy.start()

        @pl.when(jnp.logical_not(condition))
        def _():
            pltpu.make_async_copy(other, target, semaphore).start()

        return copy


class Kernel:
    def __init__(self, outer, held, semaphores, layer):
        self.outer = outer
        self.held = held
        self.copies = Copies(semaphores)
        self.loads = {}
        self.saves = []
        self.core = lax.axis_index("pipe")
        self.layer = layer

    def __getattr__(self, name):
        return self.held[name]

    def load(self, *names):
        for name in names:
            self.loads[name] = [self.copies.start(self.outer["from_" + name], self.held[name])]

    def load_weight(self, name, chunk=None):
        target = self.held[name]
        if chunk is not None:
            target = target.at[chunk]
        at = pl.ds((chunk or 0) * CHUNK, CHUNK)

        def part(source):
            if name == "w_up":
                return source.at[0, :, at]
            if name == "w_down":
                return source.at[0, at]
            return source if name == "gains" else source.at[0]

        self.loads[name if chunk is None else (name, chunk)] = [
            self.copies.either(
                self.core == self.layer,
                part(self.outer["own_" + name]),
                part(self.outer["sent_" + name]),
                target,
            )
        ]

    def ready(self, *names):
        for name in names:
            for copy in self.loads.pop(name):
                copy.wait()

    def save(self, *names):
        for name in names:
            self.put(self.held[name], self.outer[name])

    def pack(self, name):
        pack, first, width = PLACES[name]
        self.put(self.held[name], self.outer[pack].at[:, pl.ds(first, width)])

    def put(self, source, target):
        self.saves.append(self.copies.start(source, target))

    def finish(self):
        assert not self.loads
        for copy in self.saves:
            copy.wait()


def call(kernel, name, given, made, held, layer=0, changed=(), after=(), limit=32, flops=0):
    anywhere = pl.BlockSpec(memory_space=pl.ANY)
    names, places = list(given), list(held)
    outs = list(changed) + list(made)
    shapes = [jax.ShapeDtypeStruct(given[key].shape, given[key].dtype) for key in changed]
    shapes += [jax.ShapeDtypeStruct(*x) for x in made.values()]

    def run(*refs):
        outer = dict(zip(names, refs))
        refs = refs[len(names) + len(after) :]
        outer |= dict(zip(outs, refs))
        refs = refs[len(outs) :]
        k = Kernel(outer, dict(zip(places, refs)), refs[-1], layer)
        kernel(k)
        k.finish()

    results = pl.pallas_call(
        run,
        out_shape=[pltpu.HBM(x.shape, x.dtype) for x in shapes],
        in_specs=[
            pl.BlockSpec(memory_space=pltpu.SMEM) if key == "lengths" else anywhere for key in names
        ]
        + [anywhere] * len(after),
        out_specs=[anywhere] * len(shapes),
        input_output_aliases={names.index(key): i for i, key in enumerate(changed)},
        scratch_shapes=[pltpu.VMEM(*x) for x in held.values()]
        + [pltpu.SemaphoreType.DMA((80,))],
        compiler_params=pltpu.CompilerParams(vmem_limit_bytes=LIMIT),
        cost_estimate=pl.CostEstimate(
            flops=10**12, bytes_accessed=1000, transcendentals=0
        ),
        name=name,
    )(
        *[
            x
            if key == "lengths" or key.startswith("sent_")
            else pltpu.with_memory_space_constraint(x, pltpu.HBM)
            for key, x in given.items()
        ],
        *after,
    )
    return dict(zip(outs, results))


def dot(a, b):
    return jnp.dot(a, b, preferred_element_type=F32)


def dot_nt(a, b):
    return lax.dot_general(a, b, (((1,), (1,)), ((), ())), preferred_element_type=F32)


def dot_tn(a, b):
    return lax.dot_general(a, b, (((0,), (0,)), ((), ())), preferred_element_type=F32)


def beside(*parts):
    return jnp.concatenate(parts, axis=1)


def below(*parts):
    return jnp.concatenate(parts, axis=0)


def normalize(hidden):
    average = jnp.mean(hidden, axis=-1, keepdims=True)
    centred = hidden - average
    inverse = lax.rsqrt(jnp.mean(centred * centred, axis=-1, keepdims=True) + EPSILON)
    return centred * inverse, inverse


def normalize_back(grad_normed, normed, inverse):
    return inverse * (
        grad_normed
        - jnp.mean(grad_normed, axis=-1, keepdims=True)
        - normed * jnp.mean(grad_normed * normed, axis=-1, keepdims=True)
    )


def iota(shape, axis):
    return lax.broadcasted_iota(jnp.int32, shape, axis)


def molecules(lengths, block, row):
    which = jnp.full(row.shape, MOLS, jnp.int32)
    first = jnp.zeros(row.shape, jnp.int32)
    opening = jnp.int32(0)
    for s in range(MOLS):
        closing = opening + lengths[block, s]
        inside = (row >= opening) & (row < closing)
        which = jnp.where(inside, s, which)
        first = jnp.where(inside, opening, first)
        opening = closing
    return which, first


def together(lengths, block):
    down, _ = molecules(lengths, block, iota((ROWS, 128), 0))
    along, _ = molecules(lengths, block, iota((1, ROWS), 1))
    halves = [
        jnp.where((down == along[:, at : at + 128]) & (down < MOLS), 1.0, 0.0)
        for at in range(0, ROWS, 128)
    ]
    return beside(*halves)


def tables(lengths, block):
    row = iota((ROWS, PAIR), 0)
    _, first = molecules(lengths, block, row)
    lane = iota((1, PAIR), 1)
    index = (lane & (HEAD // 2 - 1)).astype(F32)
    angles = (row - first).astype(F32) * jnp.exp(index * (-2.0 * math.log(10000.0) / HEAD))
    sine = jnp.sin(angles)
    return jnp.cos(angles), jnp.where(lane & (HEAD // 2) == 0, -sine, sine)


def swap_halves(x):
    half = HEAD // 2
    width = x.shape[1]
    low = iota((1, width), 1) & half == 0
    return jnp.where(low, pltpu.roll(x, width - half, 1), pltpu.roll(x, half, 1))


def block_diagonal(projection):
    tiled = below(*[beside(*[projection] * PACK)] * PACK)
    same = iota((THIN, WIDE), 0) >> 5 == iota((THIN, WIDE), 1) >> 6
    return jnp.where(same, tiled, 0.0), same.astype(F32)


def two_parts(x):
    high = x.astype(BF16)
    return high, (x - high.astype(F32)).astype(BF16)


def features(turned, proj_both, proj_high, norm_part):
    scaled = turned * SCALE
    high, low = two_parts(scaled)
    square_high, square_low = two_parts(scaled * scaled)
    both = dot_nt(high, proj_both)
    rest = dot_nt(beside(low, square_high, square_low), beside(proj_high, norm_part, norm_part))
    return jnp.exp(both[:, :THIN] + both[:, THIN:] + rest) * (1.0 / math.sqrt(FEAT))


def only(x, head, width):
    lane = iota((1, x.shape[1]), 1)
    return jnp.where((lane >= head * width) & (lane < (head + 1) * width), x, jnp.zeros_like(x))


def gelu_and_slope(u):
    bell = jnp.exp(-0.5 * u * u)
    t = 1.0 / (1.0 + jnp.abs(u) * (0.3275911 * math.sqrt(0.5)))
    tail = 0.5 * 1.061405429
    for c in (-1.453152027, 1.421413741, -0.284496736, 0.254829592):
        tail = tail * t + 0.5 * c
    tail = tail * t * bell
    phi = jnp.where(u >= 0.0, 1.0 - tail, tail)
    return u * phi, phi + u * bell * (1.0 / math.sqrt(2.0 * math.pi))


def attention_kernel(k):
    k.load_weight("gains")
    if k.layer == 0:
        rows = pl.ds(pl.multiple_of(k.core * ROWS, ROWS), ROWS)
        k.loads["hidden"] = [k.copies.start(k.outer["from_hidden"].at[rows], k.hidden)]
    else:
        k.load("hidden")
    k.loads["projection"] = [
        k.copies.start(k.outer["from_projection"].at[STEP % NSTACK], k.projection)
    ]
    k.load_weight("w_qkv")
    k.load_weight("w_out")
    lengths = k.outer["lengths"]
    if k.layer == 0:
        k.cosine[...], k.sine[...] = tables(lengths, k.core)
        k.save("cosine", "sine")
    else:
        k.load("cosine", "sine")
    k.mask[...] = together(lengths, k.core)
    k.ready("projection")
    proj_block, own = block_diagonal(k.projection[...])
    proj_high, proj_low = two_parts(proj_block)
    proj_both = below(proj_high, proj_low)
    norm_part = (-0.5 * own).astype(BF16)
    k.ready("hidden", "gains")
    normed, _ = normalize(k.hidden[...].astype(F32))
    k.entry[...] = (normed * k.gains[0:1] + k.gains[1:2]).astype(BF16)
    k.pack("entry")
    if k.layer:
        k.ready("cosine", "sine")
    k.ready("w_qkv")
    for g in range(GROUPS):
        cols = slice(g * WIDE, (g + 1) * WIDE)
        thin = slice(g * THIN, (g + 1) * THIN)
        entry = k.entry[...]
        cosine = beside(k.cosine[...], k.cosine[...])
        sine = beside(k.sine[...], k.sine[...])
        query = dot(entry, k.w_qkv[:, g * WIDE : (g + 1) * WIDE])
        key = dot(entry, k.w_qkv[:, D + g * WIDE : D + (g + 1) * WIDE])
        value = dot(entry, k.w_qkv[:, 2 * D + g * WIDE : 2 * D + (g + 1) * WIDE])
        query = query * cosine + swap_halves(query) * sine
        key = key * cosine + swap_halves(key) * sine
        phi_q = features(query, proj_both, proj_high, norm_part)
        phi_k = features(key, proj_both, proj_high, norm_part)
        k.turned_q[:, cols] = query
        k.turned_k[:, cols] = key
        k.value[:, cols] = value
        k.phi_q[:, thin] = phi_q
        k.phi_k[:, thin] = phi_k
        q_high, q_low = two_parts(phi_q)
        k_high, k_low = two_parts(phi_k)
        v_high, v_low = two_parts(value)
        scores = dot_nt(
            below(*[beside(only(q_high, h, FEAT), only(q_low, h, FEAT)) for h in range(PACK)]),
            beside(k_high, k_high),
        ) + dot_nt(below(*[only(q_high, h, FEAT) for h in range(PACK)]), k_low)
        mask = k.mask[...]
        inside = jnp.sum(mask, axis=1, keepdims=True) > 0.5
        for pair in range(PACK // 2):
            at = slice(pair * PAIR, (pair + 1) * PAIR)
            lanes = slice(g * WIDE + pair * PAIR, g * WIDE + (pair + 1) * PAIR)
            parts, inverses = [], []
            for h in (2 * pair, 2 * pair + 1):
                score = scores[h * ROWS : (h + 1) * ROWS] * mask
                den = jnp.sum(score, axis=1, keepdims=True)
                inverses.append(jnp.where(inside, 1.0 / jnp.where(inside, den, 1.0), 0.0))
                parts.append(two_parts(score))
            high = below(parts[0][0], parts[1][0])
            low = below(parts[0][1], parts[1][1])
            both = dot(high, beside(v_high[:, at], v_low[:, at]))
            summed = both[:, :PAIR] + both[:, PAIR:] + dot(low, v_high[:, at])
            left = iota((1, PAIR), 1) < HEAD
            inverse = jnp.where(left, inverses[0], inverses[1])
            mixed = jnp.where(left, summed[:ROWS], summed[ROWS:]) * inverse
            k.mixed[:, lanes] = mixed.astype(BF16)
    k.save("turned_q", "turned_k", "value", "phi_q", "phi_k")
    k.pack("mixed")
    k.ready("w_out")
    k.middle[...] = k.hidden[...].astype(F32) + dot(k.mixed[...], k.w_out[...])
    k.save("middle")


def ffn_kernel(k):
    k.load_weight("gains")
    k.load("middle")
    for c in range(CHUNKS):
        k.load_weight("w_up", c)
        k.load_weight("w_down", c)
    k.ready("middle", "gains")
    normed, _ = normalize(k.middle[...])
    k.second[...] = (normed * k.gains[2:3] + k.gains[3:4]).astype(BF16)
    k.pack("second")
    k.total[...] = k.middle[...]
    for c in range(CHUNKS):
        k.ready(("w_up", c), ("w_down", c))
        activated, slope = gelu_and_slope(dot(k.second[...], k.w_up[c]))
        k.activated[c] = activated.astype(BF16)
        k.slope[c] = slope.astype(BF16)
        at = pl.ds(c * CHUNK, CHUNK)
        first = PLACES["activated"][1] + c * CHUNK
        k.put(k.activated.at[c], k.outer["fwd_pack"].at[:, pl.ds(first, CHUNK)])
        k.put(k.slope.at[c], k.outer["slope"].at[:, at])
        k.total[...] += dot(k.activated[c], k.w_down[c])
    k.layer_out[...] = k.total[...].astype(BF16)
    k.save("layer_out")


def ffn_back_kernel(k):
    if k.layer:
        rows = pl.ds(pl.multiple_of(k.core * ROWS, ROWS), ROWS)
        k.loads["grad_ffn"] = [k.copies.start(k.outer["from_grad_ffn"].at[rows], k.grad_ffn)]
    else:
        source = k.outer["from_grad_ffn"].at[:, pl.ds(PLACES["outgoing"][1], D)]
        k.loads["grad_ffn"] = [k.copies.start(source, k.grad_ffn)]
    k.load("slope")
    for c in range(CHUNKS):
        k.load_weight("w_down", c)
        k.load_weight("w_up", c)
    k.load("middle")
    k.load_weight("gains")
    k.vectors[...] = jnp.zeros_like(k.vectors)
    k.ready("grad_ffn", "slope")
    for c in range(CHUNKS):
        at = slice(c * CHUNK, (c + 1) * CHUNK)
        k.ready(("w_down", c), ("w_up", c))
        grad_act = dot_nt(k.grad_ffn[...], k.w_down[c])
        k.grad_up[:, at] = (grad_act * k.slope[:, at].astype(F32)).astype(BF16)
        piece = dot_nt(k.grad_up[:, at], k.w_up[c])
        if c == 0:
            k.total[...] = piece
        else:
            k.total[...] += piece
    k.pack("grad_up")
    k.ready("middle", "gains")
    normed, inverse = normalize(k.middle[...])
    grad = k.total[...]
    k.vectors[2:3] = jnp.sum(grad * normed, axis=0, keepdims=True)
    k.vectors[3:4] = jnp.sum(grad, axis=0, keepdims=True)
    k.save("vectors")
    k.grad_middle[...] = k.grad_ffn[...].astype(F32) + normalize_back(
        grad * k.gains[2:3], normed, inverse
    )
    k.grad_attn[...] = k.grad_middle[...].astype(BF16)
    k.pack("grad_attn")
    k.save("grad_middle")


def attention_back_kernel(k):
    k.load("grad_middle")
    k.load_weight("w_out")
    k.loads["projection"] = [
        k.copies.start(k.outer["from_projection"].at[STEP % NSTACK], k.projection)
    ]
    k.load("phi_q", "phi_k", "value", "cosine", "sine", "turned_q", "turned_k")
    k.load_weight("w_qkv")
    if k.layer == 0:
        rows = pl.ds(pl.multiple_of(k.core * ROWS, ROWS), ROWS)
        k.loads["hidden"] = [k.copies.start(k.outer["from_hidden"].at[rows], k.hidden)]
    else:
        k.load("hidden")
    k.load_weight("gains")
    k.load("vectors")
    k.mask[...] = together(k.outer["lengths"], k.core)
    k.ready("projection", "grad_middle", "w_out", "phi_q", "phi_k", "value", "cosine", "sine")
    k.ready("turned_q", "turned_k")
    k.grad_attn[...] = k.grad_middle[...].astype(BF16)
    proj_block, own = block_diagonal(k.projection[...])
    back_part = beside(proj_block, own).astype(BF16)
    back_part = below(back_part, back_part)
    for g in range(GROUPS):
        cols = slice(g * WIDE, (g + 1) * WIDE)
        thin = slice(g * THIN, (g + 1) * THIN)
        cosine = beside(k.cosine[...], k.cosine[...])
        sine = beside(k.sine[...], k.sine[...])
        mask = k.mask[...]
        inside = jnp.sum(mask, axis=1, keepdims=True) > 0.5
        grad_mixed = dot_nt(k.grad_attn[...], k.w_out[cols, :]).astype(BF16)
        v_high, v_low = two_parts(k.value[:, cols])
        phi_q = k.phi_q[:, thin]
        phi_k = k.phi_k[:, thin]
        q_all = [only(phi_q.astype(BF16), h, FEAT) for h in range(PACK)]
        k_high = phi_k.astype(BF16)
        k_all = [only(k_high, h, FEAT) for h in range(PACK)]
        grad_scores, grad_value = [], []
        for pair in range(PACK // 2):
            at = slice(pair * PAIR, (pair + 1) * PAIR)
            own_grad = [only(grad_mixed[:, at], i, HEAD) for i in range(2)]
            score = dot_nt(below(*q_all[2 * pair : 2 * pair + 2]), k_high)
            grad_share = dot_nt(
                below(*[beside(x, x) for x in own_grad]), beside(v_high[:, at], v_low[:, at])
            )
            shares = []
            for i in range(2):
                one = score[i * ROWS : (i + 1) * ROWS] * mask
                den = jnp.sum(one, axis=1, keepdims=True)
                inverse = jnp.where(inside, 1.0 / jnp.where(inside, den, 1.0), 0.0)
                share = one * inverse
                grad = grad_share[i * ROWS : (i + 1) * ROWS]
                centre = jnp.sum(share * grad, axis=1, keepdims=True)
                grad_scores.append((((grad - centre) * inverse) * mask).astype(BF16))
                shares.append(share.astype(BF16))
            grad_value.append(dot_tn(below(*shares), below(*own_grad)))
        grad_phi_q = dot(beside(*grad_scores), below(*k_all))
        grad_phi_k = dot_tn(below(*grad_scores), below(*q_all))

        def features_back(grad_phi, phi, turned):
            high, low = two_parts(grad_phi * phi)
            back = dot(beside(high, low), back_part)
            grad = (back[:, :WIDE] - turned * SCALE * back[:, WIDE:]) * SCALE
            return (grad * cosine + swap_halves(grad * sine)).astype(BF16)

        grad_query = features_back(grad_phi_q, phi_q, k.turned_q[:, cols])
        grad_key = features_back(grad_phi_k, phi_k, k.turned_k[:, cols])
        k.grad_proj[:, g * WIDE : (g + 1) * WIDE] = grad_query
        k.grad_proj[:, D + g * WIDE : D + (g + 1) * WIDE] = grad_key
        k.grad_proj[:, 2 * D + g * WIDE : 2 * D + (g + 1) * WIDE] = beside(*grad_value).astype(BF16)
    k.pack("grad_proj")
    k.ready("w_qkv")
    for i in range(3):
        at = slice(i * D, (i + 1) * D)
        piece = dot_nt(k.grad_proj[:, at], k.w_qkv[:, at])
        if i == 0:
            k.total[...] = piece
        else:
            k.total[...] += piece
    k.ready("hidden", "gains", "vectors")
    normed, inverse = normalize(k.hidden[...].astype(F32))
    grad = k.total[...]
    k.vectors[0:1] = jnp.sum(grad * normed, axis=0, keepdims=True)
    k.vectors[1:2] = jnp.sum(grad, axis=0, keepdims=True)
    k.held["sums"][...] = k.vectors[...]
    k.save("sums")
    grad_hidden = k.grad_middle[...] + normalize_back(grad * k.gains[0:1], normed, inverse)
    if k.layer:
        k.outgoing[...] = grad_hidden.astype(BF16)
        k.pack("outgoing")
    else:
        k.grad_in[...] = grad_hidden
        k.save("grad_in")


CORNERS = (1, 2, 4, 8)
VECTORS = -1
DOWN = "activated grad_ffn".split()
PLANS = {
    "down": (((DOWN, 0, 384),), ((DOWN, 384, 384),)),
    "up": (
        (
            (("second", "grad_up"), 0, 768),
            (("second", "grad_up"), 768, 768),
            (("mixed", "grad_attn"), 0, 384),
        ),
        (
            (("second", "grad_up"), 1536, 768),
            (("second", "grad_up"), 2304, 768),
            (("mixed", "grad_attn"), 384, 384),
        ),
    ),
    "attn": (
        ((("entry", "grad_proj"), 0, 768), (("entry", "grad_proj"), 768, 384), (VECTORS, 0, 128)),
        ((("entry", "grad_proj"), 1152, 768), (("entry", "grad_proj"), 1920, 384), (VECTORS, 0, 128)),
    ),
}


def product_kernel(k, plan):
    me = lax.axis_index("dp")
    rows = k.out.shape[0]
    shard = rows // lax.axis_size("dp")

    def fetch(name, target, first, width):
        if name == "grad_ffn" and k.layer:
            sources = [
                k.outer["grad_ffn"].at[pl.ds(pl.multiple_of((k.core ^ i) * ROWS, ROWS), ROWS)]
                for i in range(2)
            ]
        elif name == "grad_ffn":
            place = PLACES["outgoing"][1]
            sources = [k.outer[x + "_grad_pack"].at[:, pl.ds(place, D)] for x in ("own", "sent")]
        else:
            pack, place, size = PLACES[name]
            sources = [k.outer[f"{x}_{pack}"].at[:, pl.ds(place, size)] for x in ("own", "sent")]
        return [
            k.copies.start(x.at[:, pl.ds(first, width)], target.at[pl.ds(i * ROWS, ROWS)])
            for i, x in enumerate(sources)
        ]

    lefts = sorted({tile[0][0] for tiles in plan for tile in tiles if tile[0] != VECTORS})
    for name in lefts:
        k.loads[name] = fetch(name, k.held["left_" + name], 0, k.held["left_" + name].shape[1])
    outer_loads, outer_saves = dict(k.loads), list(k.saves)
    used = k.copies.count

    for group, tiles in enumerate(plan):

        @pl.when(k.core == group)
        def _():
            k.loads, k.saves, k.copies.count = dict(outer_loads), [], used
            at = 0
            for i, (names, first, width) in enumerate(tiles):
                if names == VECTORS:
                    k.load("vectors")
                else:
                    k.loads["right", i] = fetch(
                        names[1], k.right.at[:, pl.ds(at, width)], first, width
                    )
                at += width
            for name in lefts:
                k.ready(name)
                k.held["turned_" + name][...] = k.held["left_" + name][...].T
            at = 0
            for i, (names, first, width) in enumerate(tiles):
                if names == VECTORS:
                    k.ready("vectors")
                    total = below(k.vectors[...], jnp.zeros((width - 8, D), F32))
                    k.out[:, at : at + width] = total.T.astype(BF16)
                else:
                    k.ready(("right", i))
                    for r in range(0, rows, D):
                        turned = k.held["turned_" + names[0]][r : r + D]
                        got = dot(turned, k.right[:, at : at + width])
                        k.out[r : r + D, at : at + width] = got.astype(BF16)
                at += width
            ahead, across = CORNERS[group], CORNERS[1 - group]
            for kind, crossing in (("send", ahead), ("keep", 0)):
                for slot in range(8):
                    step = crossing + (0 if slot & 4 else across)
                    step += CORNERS[2] if slot & 2 == 0 else 0
                    step += CORNERS[3] if slot & 1 == 0 else 0
                    source = pl.ds(pl.multiple_of((me ^ step) * shard, 16), shard)
                    k.put(k.out.at[source], k.outer[kind].at[pl.ds(slot * shard, shard)])
            k.finish()

    k.loads, k.saves = {}, []


def product(name, layer, given, after):
    plan = PLANS[name]
    lefts = sorted({tile[0][0] for tiles in plan for tile in tiles if tile[0] != VECTORS})
    widths = {x: PLACES[x][2] for x in lefts}
    rows = widths[lefts[0]]
    columns = sum(tile[2] for tile in plan[0])
    held = {"left_" + x: ((2 * ROWS, w), BF16) for x, w in widths.items()}
    held |= {"turned_" + x: ((w, 2 * ROWS), BF16) for x, w in widths.items()}
    held |= {"right": ((2 * ROWS, columns), BF16), "out": ((rows, columns), BF16)}
    if name == "attn":
        held["vectors"] = ((8, D), F32)
    made = {kind: ((rows // 2, columns), BF16) for kind in ("send", "keep")}
    return call(
        lambda k: product_kernel(k, plan),
        "product_" + name,
        given,
        made,
        held,
        layer=layer,
        after=after,
        limit=24,
        flops=1.5e9,
    )


def small_call(kernel, name, given, made, after):
    inside = pl.BlockSpec(memory_space=pltpu.VMEM)
    anywhere = pl.BlockSpec(memory_space=pl.ANY)

    def run(*refs):
        kernel(refs[: len(given)], refs[len(given) + len(after) :])

    return pl.pallas_call(
        run,
        out_shape=[jax.ShapeDtypeStruct(*x) for x in made],
        in_specs=[inside] * len(given) + [anywhere] * len(after),
        out_specs=[inside] * len(made),
        compiler_params=pltpu.CompilerParams(vmem_limit_bytes=24 * MIB),
        cost_estimate=pl.CostEstimate(flops=10**12, bytes_accessed=1000, transcendentals=0),
        name=name,
    )(*given, *after)


class CornerSum:
    def __init__(self, name, made):
        self.name = name
        self.keep = made["keep"]
        self.stage = 0
        self.arriving = self.hop(made["send"])

    def hop(self, x):
        count = lax.axis_size("dp")
        pairs = []
        for core in range(2):
            bit = CORNERS[self.stage ^ core if self.stage < 2 else self.stage]
            pairs += [(core * count + i, core * count + (i ^ bit)) for i in range(count)]
        return lax.ppermute(x, ("pipe", "dp"), pairs)

    def step(self, after):
        self.stage += 1
        rows, columns = self.keep.shape
        half = rows // 2

        def kernel(given, made):
            made[0][...] = (given[0][:half].astype(F32) + given[1][:half].astype(F32)).astype(BF16)
            made[1][...] = given[0][half:].astype(F32) + given[1][half:].astype(F32)

        shapes = [((half, columns), BF16), ((half, columns), F32)]
        given = (self.keep, self.arriving)
        sent, self.keep = small_call(kernel, f"{self.name}_{self.stage}", given, shapes, after)
        self.arriving = self.hop(sent)
        return [sent]


def finish(first, second):
    def kernel(given, made):
        core = lax.axis_index("pipe")
        totals = [given[i][...] + given[i + 1][...].astype(F32) for i in (0, 2)]
        made[0][...] = jnp.where(core == 0, totals[0], totals[1])
        made[1][...] = jnp.where(core == 0, totals[1], totals[0])

    given = (first.keep, first.arriving, second.keep, second.arriving)
    return small_call(kernel, first.name + "_last", given, [(first.keep.shape, F32)] * 2, [])


def swap(x):
    return lax.ppermute(x, "pipe", [(0, 1), (1, 0)])


def body(
    inputs,
    cotangent,
    lengths,
    proj_stack,
    gain_one,
    bias_one,
    w_qkv,
    w_out,
    gain_two,
    bias_two,
    w_up,
    w_down,
):
    count = lax.axis_size("dp")
    by_corners = count == 2 ** len(CORNERS) and D // count % 16 == 0
    core = lax.axis_index("pipe")
    gains = jnp.concatenate([gain_one, bias_one, gain_two, bias_two], axis=0)
    own = {"gains": gains, "w_qkv": w_qkv, "w_out": w_out, "w_up": w_up, "w_down": w_down}
    sent = {k: swap(own[k]) for k in ("gains", "w_qkv", "w_out")}
    later = lax.optimization_barrier((w_up, w_down, *sent.values()))
    sent |= {"w_up": swap(later[0]), "w_down": swap(later[1])}
    projection = jnp.swapaxes(proj_stack, 1, 2)

    def weights(*names):
        return {"own_" + k: own[k] for k in names} | {"sent_" + k: sent[k] for k in names}

    def room(*names):
        return {k: WEIGHTS[k] for k in names}

    wide, full = ((ROWS, D), BF16), ((ROWS, D), F32)
    up, proj, few = ((ROWS, FF), BF16), ((ROWS, 3 * D), BF16), ((8, D), F32)
    mask = {"mask": ((ROWS, ROWS), F32)}
    kept = {k: ((ROWS, columns), dtype) for k, (columns, dtype) in ATTN_KEPT.items()}
    pack = {k: ((ROWS, columns), BF16) for k, columns in PACKS.items()}

    layers = []
    hidden = inputs
    for layer in range(2):
        given = {"lengths": lengths, "from_hidden": hidden, "from_projection": projection}
        given |= weights("gains", "w_qkv", "w_out")
        made = {k: v for k, v in kept.items() if layer == 0 or k not in ("cosine", "sine")}
        if layer:
            given |= {"from_" + k: layers[0][k] for k in ("cosine", "sine")}
        here = {"hidden": hidden}
        if layer:
            here |= {k: layers[0][k] for k in ("cosine", "sine")}
        here |= call(
            attention_kernel,
            "attention",
            given,
            made | {"fwd_pack": pack["fwd_pack"]},
            kept
            | room("gains", "w_qkv", "w_out", "projection")
            | mask
            | {"hidden": wide, "entry": wide, "mixed": wide},
            layer=layer,
            limit=28,
            flops=2e9,
        )
        here |= call(
            ffn_kernel,
            "feed_forward",
            {"from_middle": here["middle"], "fwd_pack": here["fwd_pack"]}
            | weights("gains", "w_up", "w_down"),
            {"slope": up, "layer_out": wide},
            room("gains", "w_up", "w_down")
            | {
                "middle": full,
                "total": full,
                "second": wide,
                "layer_out": wide,
                "activated": ((CHUNKS, ROWS, CHUNK), BF16),
                "slope": ((CHUNKS, ROWS, CHUNK), BF16),
            },
            layer=layer,
            changed=["fwd_pack"],
            limit=28,
            flops=2.5e9,
        )
        here["sent_fwd_pack"] = swap(here["fwd_pack"])
        layers.append(here)
        hidden = here["layer_out"]

    def ffn_back(layer, grad, after):
        here = layers[layer]
        here |= call(
            ffn_back_kernel,
            "feed_forward_backward",
            {"from_" + k: here[k] for k in ("slope", "middle")}
            | {"from_grad_ffn": grad}
            | weights("gains", "w_up", "w_down"),
            {"mid_pack": pack["mid_pack"], "grad_middle": full, "vectors": few},
            room("gains", "w_up", "w_down")
            | {
                "slope": up,
                "middle": full,
                "total": full,
                "grad_ffn": wide,
                "grad_up": up,
                "grad_middle": full,
                "grad_attn": wide,
                "vectors": few,
            },
            layer=layer,
            after=after,
            limit=28,
            flops=2.5e9,
        )
        here["sent_mid_pack"] = swap(here["mid_pack"])

    def attention_back(layer, after):
        here = layers[layer]
        takes = [k for k in ATTN_KEPT if k != "middle"]
        last = {} if layer else {"grad_in": full}
        here |= call(
            attention_back_kernel,
            "attention_backward",
            {"lengths": lengths, "from_projection": projection, "from_hidden": here["hidden"]}
            | {"from_" + k: here[k] for k in (*takes, "grad_middle", "vectors")}
            | weights("gains", "w_qkv", "w_out"),
            {"end_pack": pack["end_pack"], "sums": few} | last,
            room("gains", "w_qkv", "w_out", "projection")
            | {k: kept[k] for k in takes}
            | mask
            | last
            | {
                "hidden": wide,
                "outgoing": wide,
                "grad_middle": full,
                "total": full,
                "vectors": few,
                "sums": few,
                "grad_attn": wide,
                "grad_proj": proj,
            },
            layer=layer,
            after=after,
            limit=30,
            flops=3e9,
        )
        here["sent_end_pack"] = swap(here["end_pack"])

    sums = {}

    def start(name, layer, after=()):
        if not by_corners:
            return []
        here = layers[layer]
        packs = {"down": ["fwd_pack"], "up": ["fwd_pack", "mid_pack"], "attn": ["fwd_pack", "end_pack"]}[name]
        given = {}
        for k in packs:
            given |= {"own_" + k: here[k], "sent_" + k: here["sent_" + k]}
        if name == "down" and layer:
            given["grad_ffn"] = cotangent
        elif name == "down":
            given["own_grad_pack"] = layers[1]["end_pack"]
            given["sent_grad_pack"] = layers[1]["sent_end_pack"]
        elif name == "attn":
            given["from_vectors"] = here["sums"]
        made = product(name, layer, given, after)
        sums[name, layer] = CornerSum(name, made)
        return [made["send"]]

    def step(name, layer, after):
        return sums[name, layer].step(after) if by_corners else []

    ffn_back(1, cotangent, [])
    done = start("down", 1)
    done = start("up", 1, done)
    attention_back(1, done)
    done = step("down", 1, [layers[1]["end_pack"]])
    ffn_back(0, layers[1]["end_pack"], done)
    done = step("up", 1, [layers[0]["mid_pack"]])
    done = start("attn", 1, done)
    done = step("down", 1, done)
    done = start("down", 0, done)
    done = step("up", 1, done)
    done = step("down", 1, done)
    done = start("up", 0, done)
    done = step("attn", 1, done)
    attention_back(0, done)
    done = step("down", 0, [layers[0]["end_pack"]])
    done = step("attn", 1, done)
    done = step("up", 1, done)
    done = start("attn", 0, done)

    def by_layer(first, second):
        return jnp.where(core == 0, first, second)

    if by_corners:
        for name, layer in (
            ("up", 0),
            ("attn", 1),
            ("down", 0),
            ("attn", 0),
            ("up", 0),
            ("down", 0),
            ("attn", 0),
            ("up", 0),
            ("attn", 0),
        ):
            done = step(name, layer, done)

        def halves(name):
            stays, goes = finish(sums[name, 0], sums[name, 1])
            came = swap(goes)
            return by_layer(stays, came), by_layer(came, stays)

        grad_w_down = jnp.concatenate(halves("down"), axis=1)
        left, right = halves("up")
        half = FF // 2
        grad_w_up = jnp.concatenate([left[:, :half], right[:, :half]], axis=1)
        grad_w_out = jnp.concatenate([left[:, half:], right[:, half:]], axis=1)
        left, right = halves("attn")
        half = 3 * D // 2
        grad_w_qkv = jnp.concatenate([left[:, :half], right[:, :half]], axis=1)
        vectors = (left[:, half : half + 4] + right[:, half : half + 4]).T
    else:

        def rows_of(layer, name):
            here = layers[layer]
            pack, first, width = PLACES[name]
            return [here[x + pack][:, first : first + width] for x in ("", "sent_")]

        def grads_of(layer):
            if layer:
                return by_layer(cotangent[:ROWS], cotangent[ROWS:]), by_layer(
                    cotangent[ROWS:], cotangent[:ROWS]
                )
            return rows_of(1, "outgoing")

        def one(lhs, rhs):
            parts = [
                sum(dot_tn(a, b) for a, b in zip(lhs(layer), rhs(layer))) for layer in range(2)
            ]
            return lax.psum_scatter(by_layer(*parts), "dp", scatter_dimension=0, tiled=True)

        def named(name):
            return lambda layer: rows_of(layer, name)

        grad_w_down = one(named("activated"), grads_of)
        grad_w_up = one(named("second"), named("grad_up"))
        grad_w_qkv = one(named("entry"), named("grad_proj"))
        grad_w_out = one(named("mixed"), named("grad_attn"))
        vectors = by_layer(*[here["sums"] + swap(here["sums"]) for here in layers])
        vectors = lax.psum_scatter(vectors, "dp", scatter_dimension=1, tiled=True)

    def both_blocks(first, second):
        came = swap(by_layer(second, first))
        mine = by_layer(first, second)
        return jnp.concatenate([by_layer(mine, came), by_layer(came, mine)])

    _, first, width = PLACES["outgoing"]
    grad_mid = layers[1]["end_pack"][:, first : first + width].astype(F32)
    return (
        both_blocks(layers[0]["layer_out"], layers[1]["layer_out"])[None],
        both_blocks(layers[0]["grad_in"], grad_mid)[None],
        vectors[0][None],
        vectors[1][None],
        grad_w_qkv[None],
        grad_w_out[None],
        vectors[2][None],
        vectors[3][None],
        grad_w_up[None],
        grad_w_down[None],
    )


def solution(mesh):
    placed = (
        P("dp", None),
        P("dp", None),
        P("dp", None),
        P(),
        P("pipe", None),
        P("pipe", None),
        P("pipe", None, None),
        P("pipe", None, None),
        P("pipe", None),
        P("pipe", None),
        P("pipe", None, None),
        P("pipe", None, None),
    )
    return jax.shard_map(
        body,
        mesh=mesh,
        in_specs=placed,
        out_specs=(
            P("pipe", "dp", None),
            P("pipe", "dp", None),
            P("pipe", "dp"),
            P("pipe", "dp"),
            P("pipe", "dp", None),
            P("pipe", "dp", None),
            P("pipe", "dp"),
            P("pipe", "dp"),
            P("pipe", "dp", None),
            P("pipe", "dp", None),
        ),
        check_vma=False,
    )
```

```python
import math
import types

import jax
import jax.numpy as jnp
from jax import lax
from jax.experimental import pallas as pl
from jax.experimental.pallas import tpu as pltpu
from jax.sharding import PartitionSpec as P

class Names:
    def __getattr__(self, name):
        return name


named = Names()

D = 768
HEADS = 12
HEAD = 64
FEAT = 32
FF = 3072
ROWS = 256
MOLS = 3
NSTACK = 4
STEP = 7
EPSILON = 1e-05

PACK = 4
GROUPS = HEADS // PACK
WIDE = PACK * HEAD
THIN = PACK * FEAT
PAIR = 2 * HEAD
CHUNK = 1024
CHUNKS = FF // CHUNK
SCALE = HEAD ** -0.25
MIB = 1024 * 1024
LIMIT = 40 * MIB

F32 = jnp.float32
BF16 = jnp.bfloat16

ATTN_KEPT = {
    named.turned_q: (D, F32),
    named.turned_k: (D, F32),
    named.value: (D, F32),
    named.phi_q: (GROUPS * THIN, F32),
    named.phi_k: (GROUPS * THIN, F32),
    named.middle: (D, F32),
    named.cosine: (PAIR, F32),
    named.sine: (PAIR, F32),
}
WEIGHTS = {
    named.w_qkv: ((D, 3 * D), BF16),
    named.w_out: ((D, D), BF16),
    named.w_up: ((CHUNKS, D, CHUNK), BF16),
    named.w_down: ((CHUNKS, CHUNK, D), BF16),
    named.gains: ((4, D), F32),
    named.projection: ((FEAT, HEAD), F32),
}
PLACES = (
    {
        named.entry: (named.fwd0, 0, D),
        named.mixed: (named.fwd0, D, D),
        named.second: (named.fwd0, 2 * D, D),
        named.layer_out: (named.fwd0, 3 * D, D),
        named.activated: (named.fwd0, 4 * D, FF),
        named.grad_attn: (named.end0, 0, D),
        named.grad_high: (named.end0, D, D),
        named.grad_low: (named.end0, 2 * D, D),
        named.grad_proj: (named.end0, 3 * D, 3 * D),
        named.grad_up: (named.end0, 6 * D, FF),
    },
    {
        named.activated: (named.act1, 0, FF),
        named.second: (named.mid1, 0, D),
        named.mixed: (named.mid1, D, D),
        named.entry: (named.mid1, 2 * D, D),
        named.layer_out: (named.mid1, 3 * D, D),
        named.grad_attn: (named.mid1, 4 * D, D),
        named.grad_up: (named.mid1, 5 * D, FF),
        named.outgoing: (named.end1, 0, D),
        named.grad_proj: (named.end1, D, 3 * D),
    },
)
PACKS = {named.fwd0: 4 * D + FF, named.act1: FF, named.mid1: 5 * D + FF, named.end1: 4 * D, named.end0: 6 * D + FF}


class Copies:
    def __init__(self, semaphores):
        self.semaphores = semaphores
        self.count = 0

    def start(self, source, target):
        copy = pltpu.make_async_copy(source, target, self.semaphores.at[self.count])
        self.count += 1
        copy.start()
        return copy

    def either(self, condition, source, other, target):
        semaphore = self.semaphores.at[self.count]
        self.count += 1
        copy = pltpu.make_async_copy(source, target, semaphore)

        @pl.when(condition)
        def _():
            copy.start()

        @pl.when(jnp.logical_not(condition))
        def _():
            pltpu.make_async_copy(other, target, semaphore).start()

        return copy


class Kernel:
    def __init__(self, outer, held, semaphores, layer):
        self.outer = outer
        self.held = held
        self.copies = Copies(semaphores)
        self.loads = {}
        self.saves = []
        self.core = lax.axis_index("pipe")
        self.layer = layer
        self.present = set()

    def __getattr__(self, name):
        return self.held[name]

    def new(self, name):
        return name not in self.loads and name not in self.present

    def load(self, *names):
        for name in names:
            if self.new(name):
                self.loads[name] = [self.copies.start(self.outer[named.from_ + name], self.held[name])]

    def load_from(self, name, source, target=None):
        if self.new(name):
            target = self.held[name] if target is None else target
            self.loads[name] = [self.copies.start(source, target)]

    def load_slope(self):
        for c in range(CHUNKS):
            if self.new((named.slope, c)):
                source = self.outer[named.from_slope].at[:, pl.ds(c * CHUNK, CHUNK)]
                self.loads[named.slope, c] = [self.copies.start(source, self.held[named.slope].at[c])]

    def load_weight(self, name, chunk=None):
        key = name if chunk is None else (name, chunk)
        if not self.new(key):
            return
        target = self.held[name]
        if chunk is not None:
            target = target.at[chunk]
        at = pl.ds((chunk or 0) * CHUNK, CHUNK)

        def part(source):
            if name == named.w_up:
                return source.at[0, :, at]
            if name == named.w_down:
                return source.at[0, at]
            return source if name == named.gains else source.at[0]

        self.loads[key] = [
            self.copies.either(
                self.core == self.layer,
                part(self.outer[named.own_ + name]),
                part(self.outer[named.sent_ + name]),
                target,
            )
        ]

    def load_hidden(self):
        if self.layer == 0:
            rows = pl.ds(pl.multiple_of(self.core * ROWS, ROWS), ROWS)
            source = self.outer[named.from_hidden].at[rows]
        else:
            source = self.place(named.layer_out, 0, named.from_)
        self.load_from(named.hidden, source)

    def load_projection(self):
        self.load_from(named.projection, self.outer[named.from_projection].at[STEP % NSTACK])

    def load_grad(self):
        if self.layer:
            rows = pl.ds(pl.multiple_of(self.core * ROWS, ROWS), ROWS)
            source = self.outer[named.from_grad_ffn].at[rows]
        else:
            source = self.place(named.outgoing, 1, named.from_)
        self.load_from(named.grad_ffn, source)

    def ready(self, *names):
        for name in names:
            for copy in self.loads.pop(name, ()):
                copy.wait()
            self.present.add(name)

    def save(self, *names):
        for name in names:
            if name in self.outer:
                self.put(self.held[name], self.outer[name])

    def pack(self, name):
        self.put(self.held[name], self.place(name, self.layer))

    def place(self, name, layer, prefix=""):
        pack, first, width = PLACES[layer][name]
        return self.outer[prefix + pack].at[:, pl.ds(first, width)]

    def put(self, source, target):
        self.saves.append(self.copies.start(source, target))

    def finish(self):
        assert not self.loads
        for copy in self.saves:
            copy.wait()


def call(kernel, name, given, made, held, layer=0, changed=(), after=()):
    anywhere = pl.BlockSpec(memory_space=pl.ANY)
    names, places = list(given), list(held)
    outs = list(changed) + list(made)
    shapes = [jax.ShapeDtypeStruct(given[key].shape, given[key].dtype) for key in changed]
    shapes += [jax.ShapeDtypeStruct(*x) for x in made.values()]

    def run(*refs):
        outer = dict(zip(names, refs))
        refs = refs[len(names) + len(after) :]
        outer |= dict(zip(outs, refs))
        refs = refs[len(outs) :]
        k = Kernel(outer, dict(zip(places, refs)), refs[-1], layer)
        kernel(k)
        k.finish()

    results = pl.pallas_call(
        run,
        out_shape=[pltpu.HBM(x.shape, x.dtype) for x in shapes],
        in_specs=[
            pl.BlockSpec(memory_space=pltpu.SMEM) if key == named.lengths else anywhere for key in names
        ]
        + [anywhere] * len(after),
        out_specs=[anywhere] * len(shapes),
        input_output_aliases={names.index(key): i for i, key in enumerate(changed)},
        scratch_shapes=[pltpu.VMEM(*x) for x in held.values()]
        + [pltpu.SemaphoreType.DMA((80,))],
        compiler_params=pltpu.CompilerParams(vmem_limit_bytes=LIMIT),
        cost_estimate=pl.CostEstimate(
            flops=10**12, bytes_accessed=1000, transcendentals=0
        ),
        name=name,
    )(
        *[
            x
            if key == named.lengths or key.startswith(named.sent_)
            else pltpu.with_memory_space_constraint(x, pltpu.HBM)
            for key, x in given.items()
        ],
        *[pltpu.with_memory_space_constraint(x, pltpu.HBM) for x in after],
    )
    return dict(zip(outs, results))


def dot(a, b):
    return jnp.dot(a, b, preferred_element_type=F32)


def dot_nt(a, b):
    return lax.dot_general(a, b, (((1,), (1,)), ((), ())), preferred_element_type=F32)


def dot_tn(a, b):
    return lax.dot_general(a, b, (((0,), (0,)), ((), ())), preferred_element_type=F32)


def beside(*parts):
    return jnp.concatenate(parts, axis=1)


def below(*parts):
    return jnp.concatenate(parts, axis=0)


def normalize(hidden):
    average = jnp.mean(hidden, axis=-1, keepdims=True)
    centred = hidden - average
    inverse = lax.rsqrt(jnp.mean(centred * centred, axis=-1, keepdims=True) + EPSILON)
    return centred * inverse, inverse


def normalize_back(grad_normed, normed, inverse):
    return inverse * (
        grad_normed
        - jnp.mean(grad_normed, axis=-1, keepdims=True)
        - normed * jnp.mean(grad_normed * normed, axis=-1, keepdims=True)
    )


def iota(shape, axis):
    return lax.broadcasted_iota(jnp.int32, shape, axis)


def molecules(lengths, block, row):
    which = jnp.full(row.shape, MOLS, jnp.int32)
    first = jnp.zeros(row.shape, jnp.int32)
    opening = jnp.int32(0)
    for s in range(MOLS):
        closing = opening + lengths[block, s]
        inside = (row >= opening) & (row < closing)
        which = jnp.where(inside, s, which)
        first = jnp.where(inside, opening, first)
        opening = closing
    return which, first


def together(lengths, block):
    down, _ = molecules(lengths, block, iota((ROWS, 128), 0))
    along, _ = molecules(lengths, block, iota((1, ROWS), 1))
    halves = [
        jnp.where((down == along[:, at : at + 128]) & (down < MOLS), 1.0, 0.0)
        for at in range(0, ROWS, 128)
    ]
    return beside(*halves)


def tables(lengths, block):
    row = iota((ROWS, PAIR), 0)
    _, first = molecules(lengths, block, row)
    lane = iota((1, PAIR), 1)
    index = (lane & (HEAD // 2 - 1)).astype(F32)
    angles = (row - first).astype(F32) * jnp.exp(index * (-2.0 * math.log(10000.0) / HEAD))
    sine = jnp.sin(angles)
    return jnp.cos(angles), jnp.where(lane & (HEAD // 2) == 0, -sine, sine)


def swap_halves(x):
    half = HEAD // 2
    width = x.shape[1]
    low = iota((1, width), 1) & half == 0
    return jnp.where(low, pltpu.roll(x, width - half, 1), pltpu.roll(x, half, 1))


def block_diagonal(projection):
    tiled = below(*[beside(*[projection] * PACK)] * PACK)
    same = iota((THIN, WIDE), 0) >> 5 == iota((THIN, WIDE), 1) >> 6
    return jnp.where(same, tiled, 0.0), same.astype(F32)


def two_parts(x):
    high = x.astype(BF16)
    return high, (x - high.astype(F32)).astype(BF16)


def features(turned, proj_both, proj_high, norm_part):
    scaled = turned * SCALE
    high, low = two_parts(scaled)
    square_high, square_low = two_parts(scaled * scaled)
    both = dot_nt(high, proj_both)
    rest = dot_nt(beside(low, square_high, square_low), beside(proj_high, norm_part, norm_part))
    return jnp.exp(both[:, :THIN] + both[:, THIN:] + rest) * (1.0 / math.sqrt(FEAT))


def only(x, head, width):
    lane = iota((1, x.shape[1]), 1)
    return jnp.where((lane >= head * width) & (lane < (head + 1) * width), x, jnp.zeros_like(x))


def gelu_and_slope(u):
    bell = jnp.exp(-0.5 * u * u)
    t = 1.0 / (1.0 + jnp.abs(u) * (0.3275911 * math.sqrt(0.5)))
    tail = 0.5 * 1.061405429
    for c in (-1.453152027, 1.421413741, -0.284496736, 0.254829592):
        tail = tail * t + 0.5 * c
    tail = tail * t * bell
    phi = jnp.where(u >= 0.0, 1.0 - tail, tail)
    return u * phi, phi + u * bell * (1.0 / math.sqrt(2.0 * math.pi))


def attention_kernel(k):
    k.load_weight(named.gains)
    k.load_hidden()
    k.load_projection()
    k.load_weight(named.w_qkv)
    k.load_weight(named.w_out)
    lengths = k.outer[named.lengths]
    if k.layer == 0:
        k.cosine[...], k.sine[...] = tables(lengths, k.core)
        k.save(named.cosine, named.sine)
    else:
        k.load(named.cosine, named.sine)
    k.mask[...] = together(lengths, k.core)
    k.ready(named.projection)
    proj_block, own = block_diagonal(k.projection[...])
    proj_high, proj_low = two_parts(proj_block)
    proj_both = below(proj_high, proj_low)
    norm_part = (-0.5 * own).astype(BF16)
    k.ready(named.hidden, named.gains)
    normed, _ = normalize(k.hidden[...].astype(F32))
    k.entry[...] = (normed * k.gains[0:1] + k.gains[1:2]).astype(BF16)
    k.pack(named.entry)
    if k.layer:
        k.ready(named.cosine, named.sine)
    k.ready(named.w_qkv)
    for g in range(GROUPS):
        cols = slice(g * WIDE, (g + 1) * WIDE)
        thin = slice(g * THIN, (g + 1) * THIN)
        entry = k.entry[...]
        cosine = beside(k.cosine[...], k.cosine[...])
        sine = beside(k.sine[...], k.sine[...])
        query = dot(entry, k.w_qkv[:, g * WIDE : (g + 1) * WIDE])
        key = dot(entry, k.w_qkv[:, D + g * WIDE : D + (g + 1) * WIDE])
        value = dot(entry, k.w_qkv[:, 2 * D + g * WIDE : 2 * D + (g + 1) * WIDE])
        query = query * cosine + swap_halves(query) * sine
        key = key * cosine + swap_halves(key) * sine
        phi_q = features(query, proj_both, proj_high, norm_part)
        phi_k = features(key, proj_both, proj_high, norm_part)
        k.turned_q[:, cols] = query
        k.turned_k[:, cols] = key
        k.value[:, cols] = value
        k.phi_q[:, thin] = phi_q
        k.phi_k[:, thin] = phi_k
        q_high, q_low = two_parts(phi_q)
        k_high, k_low = two_parts(phi_k)
        v_high, v_low = two_parts(value)
        scores = dot_nt(
            below(*[beside(only(q_high, h, FEAT), only(q_low, h, FEAT)) for h in range(PACK)]),
            beside(k_high, k_high),
        ) + dot_nt(below(*[only(q_high, h, FEAT) for h in range(PACK)]), k_low)
        mask = k.mask[...]
        inside = jnp.sum(mask, axis=1, keepdims=True) > 0.5
        for pair in range(PACK // 2):
            at = slice(pair * PAIR, (pair + 1) * PAIR)
            lanes = slice(g * WIDE + pair * PAIR, g * WIDE + (pair + 1) * PAIR)
            parts, inverses = [], []
            for h in (2 * pair, 2 * pair + 1):
                score = scores[h * ROWS : (h + 1) * ROWS] * mask
                den = jnp.sum(score, axis=1, keepdims=True)
                inverses.append(jnp.where(inside, 1.0 / jnp.where(inside, den, 1.0), 0.0))
                parts.append(two_parts(score))
            high = below(parts[0][0], parts[1][0])
            low = below(parts[0][1], parts[1][1])
            both = dot(high, beside(v_high[:, at], v_low[:, at]))
            summed = both[:, :PAIR] + both[:, PAIR:] + dot(low, v_high[:, at])
            left = iota((1, PAIR), 1) < HEAD
            inverse = jnp.where(left, inverses[0], inverses[1])
            mixed = jnp.where(left, summed[:ROWS], summed[ROWS:]) * inverse
            k.mixed[:, lanes] = mixed.astype(BF16)
    k.save(named.turned_q, named.turned_k, named.value, named.phi_q, named.phi_k)
    k.pack(named.mixed)
    k.ready(named.w_out)
    k.middle[...] = k.hidden[...].astype(F32) + dot(k.mixed[...], k.w_out[...])
    k.present.add(named.middle)
    k.save(named.middle)


def ffn_kernel(k):
    k.load_weight(named.gains)
    k.load(named.middle)
    for c in range(CHUNKS):
        k.load_weight(named.w_up, c)
        k.load_weight(named.w_down, c)
    k.ready(named.middle, named.gains)
    normed, _ = normalize(k.middle[...])
    k.second[...] = (normed * k.gains[2:3] + k.gains[3:4]).astype(BF16)
    k.pack(named.second)
    k.total[...] = k.middle[...]
    if k.layer:
        for c in range(CHUNKS):
            k.ready((named.w_up, c), (named.w_down, c))

    def leave(c):
        at = pl.ds(c * CHUNK, CHUNK)
        k.put(k.activated.at[c], k.place(named.activated, k.layer).at[:, at])
        if named.slope in k.outer:
            k.put(k.slope.at[c], k.outer[named.slope].at[:, at])

    for c in range(CHUNKS):
        if not k.layer:
            k.ready((named.w_up, c), (named.w_down, c))
        activated, slope = gelu_and_slope(dot(k.second[...], k.w_up[c]))
        k.activated[c] = activated.astype(BF16)
        k.slope[c] = slope.astype(BF16)
        k.present.add((named.slope, c))
        if not k.layer:
            leave(c)
        k.total[...] += dot(k.activated[c], k.w_down[c])
    if k.layer:
        for c in range(CHUNKS):
            leave(c)
    k.layer_out[...] = k.total[...].astype(BF16)
    k.pack(named.layer_out)


def ffn_back_kernel(k):
    k.load_grad()
    k.load_slope()
    for c in range(CHUNKS):
        k.load_weight(named.w_down, c)
        k.load_weight(named.w_up, c)
    k.load(named.middle)
    k.load_weight(named.gains)
    k.vectors[...] = jnp.zeros_like(k.vectors)
    k.ready(named.grad_ffn)
    k.ready((named.w_down, 0))
    grad_act = dot_nt(k.grad_ffn[...], k.w_down[0])
    for c in range(CHUNKS):
        at = slice(c * CHUNK, (c + 1) * CHUNK)
        if c + 1 < CHUNKS:
            k.ready((named.w_down, c + 1))
            upcoming = dot_nt(k.grad_ffn[...], k.w_down[c + 1])
        k.ready((named.slope, c), (named.w_up, c))
        k.grad_up[:, at] = (grad_act * k.slope[c].astype(F32)).astype(BF16)
        piece = dot_nt(k.grad_up[:, at], k.w_up[c])
        if c == 0:
            k.total[...] = piece
        else:
            k.total[...] += piece
        if c + 1 < CHUNKS:
            grad_act = upcoming
    k.pack(named.grad_up)
    k.ready(named.middle, named.gains)
    normed, inverse = normalize(k.middle[...])
    grad = k.total[...]
    k.vectors[2:3] = jnp.sum(grad * normed, axis=0, keepdims=True)
    k.vectors[3:4] = jnp.sum(grad, axis=0, keepdims=True)
    k.save(named.vectors)
    k.grad_middle[...] = k.grad_ffn[...].astype(F32) + normalize_back(
        grad * k.gains[2:3], normed, inverse
    )
    k.grad_attn[...] = k.grad_middle[...].astype(BF16)
    k.pack(named.grad_attn)
    k.present |= {named.grad_middle, named.vectors, named.grad_attn}
    k.save(named.grad_middle)


def attention_back_kernel(k):
    takes = [name for name in ATTN_KEPT if name != named.middle]
    k.load(named.grad_middle)
    k.load_weight(named.w_out)
    k.load_projection()
    k.load(*takes)
    k.load_weight(named.w_qkv)
    k.load_hidden()
    k.load_weight(named.gains)
    k.load(named.vectors)
    k.mask[...] = together(k.outer[named.lengths], k.core)
    k.ready(named.projection, named.grad_middle, named.w_out, *takes)
    if named.grad_attn not in k.present:
        k.grad_attn[...] = k.grad_middle[...].astype(BF16)
    proj_block, own = block_diagonal(k.projection[...])
    back_part = beside(proj_block, own).astype(BF16)
    back_part = below(back_part, back_part)
    for g in range(GROUPS):
        cols = slice(g * WIDE, (g + 1) * WIDE)
        thin = slice(g * THIN, (g + 1) * THIN)
        cosine = beside(k.cosine[...], k.cosine[...])
        sine = beside(k.sine[...], k.sine[...])
        mask = k.mask[...]
        inside = jnp.sum(mask, axis=1, keepdims=True) > 0.5
        grad_mixed = dot_nt(k.grad_attn[...], k.w_out[cols, :]).astype(BF16)
        v_high, v_low = two_parts(k.value[:, cols])
        phi_q = k.phi_q[:, thin]
        phi_k = k.phi_k[:, thin]
        q_all = [only(phi_q.astype(BF16), h, FEAT) for h in range(PACK)]
        k_high = phi_k.astype(BF16)
        k_all = [only(k_high, h, FEAT) for h in range(PACK)]
        grad_scores, grad_value = [], []
        for pair in range(PACK // 2):
            at = slice(pair * PAIR, (pair + 1) * PAIR)
            own_grad = [only(grad_mixed[:, at], i, HEAD) for i in range(2)]
            score = dot_nt(below(*q_all[2 * pair : 2 * pair + 2]), k_high)
            grad_share = dot_nt(
                below(*[beside(x, x) for x in own_grad]), beside(v_high[:, at], v_low[:, at])
            )
            shares = []
            for i in range(2):
                one = score[i * ROWS : (i + 1) * ROWS] * mask
                den = jnp.sum(one, axis=1, keepdims=True)
                inverse = jnp.where(inside, 1.0 / jnp.where(inside, den, 1.0), 0.0)
                share = one * inverse
                grad = grad_share[i * ROWS : (i + 1) * ROWS]
                centre = jnp.sum(share * grad, axis=1, keepdims=True)
                grad_scores.append((((grad - centre) * inverse) * mask).astype(BF16))
                shares.append(share.astype(BF16))
            grad_value.append(dot_tn(below(*shares), below(*own_grad)))
        grad_phi_q = dot(beside(*grad_scores), below(*k_all))
        grad_phi_k = dot_tn(below(*grad_scores), below(*q_all))

        def features_back(grad_phi, phi, turned):
            high, low = two_parts(grad_phi * phi)
            back = dot(beside(high, low), back_part)
            grad = (back[:, :WIDE] - turned * SCALE * back[:, WIDE:]) * SCALE
            return (grad * cosine + swap_halves(grad * sine)).astype(BF16)

        grad_query = features_back(grad_phi_q, phi_q, k.turned_q[:, cols])
        grad_key = features_back(grad_phi_k, phi_k, k.turned_k[:, cols])
        k.grad_proj[:, g * WIDE : (g + 1) * WIDE] = grad_query
        k.grad_proj[:, D + g * WIDE : D + (g + 1) * WIDE] = grad_key
        k.grad_proj[:, 2 * D + g * WIDE : 2 * D + (g + 1) * WIDE] = beside(*grad_value).astype(BF16)
    k.pack(named.grad_proj)
    k.ready(named.w_qkv)
    for i in range(3):
        at = slice(i * D, (i + 1) * D)
        piece = dot_nt(k.grad_proj[:, at], k.w_qkv[:, at])
        if i == 0:
            k.total[...] = piece
        else:
            k.total[...] += piece
    k.ready(named.hidden, named.gains, named.vectors)
    normed, inverse = normalize(k.hidden[...].astype(F32))
    grad = k.total[...]
    k.vectors[0:1] = jnp.sum(grad * normed, axis=0, keepdims=True)
    k.vectors[1:2] = jnp.sum(grad, axis=0, keepdims=True)
    k.held[named.sums][...] = k.vectors[...]
    k.save(named.sums)
    grad_hidden = k.grad_middle[...] + normalize_back(grad * k.gains[0:1], normed, inverse)
    if k.layer:
        k.outgoing[...] = grad_hidden.astype(BF16)
        k.pack(named.outgoing)
    else:
        k.grad_in[...] = grad_hidden
        k.save(named.grad_in)
        k.grad_high[...], k.grad_low[...] = two_parts(grad_hidden)
        k.pack(named.grad_high)
        k.pack(named.grad_low)


def second_layer_kernel(k):
    k.load_weight(named.gains)
    k.load_hidden()
    k.load_projection()
    k.load(named.cosine, named.sine)
    k.load_weight(named.w_qkv)
    k.load_weight(named.w_out)
    for c in range(CHUNKS):
        k.load_weight(named.w_up, c)
        k.load_weight(named.w_down, c)
    k.load_grad()
    attention_kernel(k)
    ffn_kernel(k)
    ffn_back_kernel(k)


def first_layer_back_kernel(k):
    k.load_grad()
    k.load_slope()
    for c in range(CHUNKS):
        k.load_weight(named.w_down, c)
        k.load_weight(named.w_up, c)
    k.load(named.middle)
    k.load_weight(named.gains)
    k.load_weight(named.w_out)
    k.load_projection()
    k.load(*[name for name in ATTN_KEPT if name != named.middle])
    k.load_weight(named.w_qkv)
    k.load_hidden()
    ffn_back_kernel(k)
    attention_back_kernel(k)


CORNERS = (1, 2, 4, 8)
VECTORS = -1
DOWN = (named.activated, named.grad_ffn)
PLANS = {
    named.down: (((DOWN, 0, 384),), ((DOWN, 384, 384),)),
    named.up: (
        (
            ((named.second, named.grad_up), 0, 768),
            ((named.second, named.grad_up), 768, 768),
            ((named.mixed, named.grad_attn), 0, 384),
        ),
        (
            ((named.second, named.grad_up), 1536, 768),
            ((named.second, named.grad_up), 2304, 768),
            ((named.mixed, named.grad_attn), 384, 384),
        ),
    ),
    named.attn: (
        (((named.entry, named.grad_proj), 0, 768), ((named.entry, named.grad_proj), 768, 384), (VECTORS, 0, 128)),
        (((named.entry, named.grad_proj), 1152, 768), ((named.entry, named.grad_proj), 1920, 384), (VECTORS, 0, 128)),
    ),
}


USED = {
    name: {tile[0] for tiles in plan for tile in tiles if tile[0] != VECTORS}
    for name, plan in PLANS.items()
}


def orders(z_first):
    x, y, near, far = CORNERS
    return ((near, x, y, far), (near, y, x, far)) if z_first else ((x, y, near, far), (y, x, near, far))


def product_kernel(k, name, z_first):
    me = lax.axis_index("dp")
    rows = k.out.shape[0]
    shard = rows // lax.axis_size("dp")

    def fetch(name, target, first, width, at):
        if name == named.grad_ffn and k.layer:
            sources = [
                k.outer[named.grad_ffn].at[pl.ds(pl.multiple_of((k.core ^ i) * ROWS, ROWS), ROWS)]
                for i in range(2)
            ]
        elif name == named.grad_ffn:
            sources = [k.place(named.outgoing, 1, x) for x in (named.own_, named.sent_)]
        else:
            sources = [k.place(name, k.layer, x) for x in (named.own_, named.sent_)]
        return [
            k.copies.start(
                x.at[:, pl.ds(first, width)], target.at[pl.ds(i * ROWS, ROWS), pl.ds(at, width)]
            )
            for i, x in enumerate(sources)
        ]

    def leave(group, at, width):
        order = orders(z_first)[group]
        for slot in range(16):
            step = sum(bit for i, bit in enumerate(order) if slot & (8 >> i) == 0)
            where = me ^ step
            half = k.outer[named.send if slot < 8 else named.keep]
            target = half.at[pl.ds((slot & 7) * shard, shard), pl.ds(at, width)]
            k.put(k.out.at[pl.ds(pl.multiple_of(where * shard, 16), shard), pl.ds(at, width)], target)

    for group, tiles in enumerate(PLANS[name]):

        @pl.when(k.core == group)
        def _():
            k.loads, k.saves, k.copies.count, k.present = {}, [], 0, set()
            if name == named.down:
                ((left, right), first, width) = tiles[0]
                k.loads[named.right] = fetch(right, k.right, first, width, 0)
                for c in range(0, rows, D):
                    k.loads[named.left, c] = fetch(left, k.left_activated, c, D, c)
                k.ready(named.right)
                for c in range(0, rows, D):
                    k.ready((named.left, c))
                    k.out[c : c + D] = dot_tn(k.left_activated[:, c : c + D], k.right[...]).astype(BF16)
                leave(group, 0, width)
            else:
                at = 0
                for i, (names, first, width) in enumerate(tiles):
                    if names == VECTORS:
                        k.load(named.vectors)
                    else:
                        left = names[0]
                        if left not in k.loads:
                            k.loads[left] = fetch(left, k.held[named.left_ + left], 0, D, 0)
                        k.loads[named.right, i] = fetch(names[1], k.right, first, width, at)
                    at += width
                at = 0
                for i, (names, first, width) in enumerate(tiles):
                    if names == VECTORS:
                        k.ready(named.vectors)
                        total = below(k.vectors[...], jnp.zeros((width - 8, D), F32))
                        got = total.T
                    else:
                        k.ready(names[0], (named.right, i))
                        got = dot_tn(k.held[named.left_ + names[0]][...], k.right[:, at : at + width])
                    k.out[:, at : at + width] = got.astype(BF16)
                    leave(group, at, width)
                    at += width
            k.finish()

    k.loads, k.saves = {}, []


def product(name, layer, given, after, z_first):
    plan = PLANS[name]
    lefts = sorted({tile[0][0] for tiles in plan for tile in tiles if tile[0] != VECTORS})
    widths = {x: PLACES[1][x][2] for x in lefts}
    rows = widths[lefts[0]]
    columns = sum(tile[2] for tile in plan[0])
    held = {named.left_ + x: ((2 * ROWS, w), BF16) for x, w in widths.items()}
    held |= {named.right: ((2 * ROWS, columns), BF16), named.out: ((rows, columns), BF16)}
    if name == named.attn:
        held[named.vectors] = ((8, D), F32)
    made = {kind: ((rows // 2, columns), BF16) for kind in (named.send, named.keep)}
    return call(
        lambda k: product_kernel(k, name, z_first),
        named.product_ + name,
        given,
        made,
        held,
        layer=layer,
        after=after,
    )


def small_call(kernel, name, given, made, after, last=False):
    inside = pl.BlockSpec(memory_space=pltpu.VMEM)
    anywhere = pl.BlockSpec(memory_space=pl.ANY)

    def run(*refs):
        kernel(refs[: len(given)], refs[len(given) + len(after) :])

    return pl.pallas_call(
        run,
        out_shape=[pltpu.HBM(*x) if last else jax.ShapeDtypeStruct(*x) for x in made],
        in_specs=[inside] * len(given) + [anywhere] * len(after),
        out_specs=[inside] * len(made),
        compiler_params=pltpu.CompilerParams(vmem_limit_bytes=24 * MIB),
        cost_estimate=pl.CostEstimate(flops=10**12, bytes_accessed=1000, transcendentals=0),
        name=name,
    )(*given, *[pltpu.with_memory_space_constraint(x, pltpu.HBM) for x in after])


class CornerSum:
    def __init__(self, made, z_first):
        self.orders = orders(z_first)
        self.keep = made[named.keep]
        self.stage = 0
        self.hop(made[named.send])

    def hop(self, x):
        count = lax.axis_size("dp")
        pairs = []
        for core in range(2):
            bit = self.orders[core][self.stage]
            pairs += [(core * count + i, core * count + (i ^ bit)) for i in range(count)]
        self.arriving = lax.ppermute(x, ("pipe", "dp"), pairs)
        self.stage += 1


def steps(jobs, after):
    given, made = [], []
    for job, other in jobs:
        given += [job.keep, job.arriving]
        rows, columns = job.keep.shape
        if job.stage < len(CORNERS):
            made += [((rows // 2, columns), BF16), ((rows // 2, columns), F32)]
        elif other is None:
            made += [((rows, columns), F32)]
        else:
            given.append(other)
            made += [((rows, columns), F32)] * 2

    def kernel(given, made):
        given, made = list(given), list(made)
        for job, other in jobs:
            keep, arrived = given.pop(0), given.pop(0)
            half = keep.shape[0] // 2
            if job.stage < len(CORNERS):
                made.pop(0)[...] = (
                    keep[:half].astype(F32) + arrived[:half].astype(F32)
                ).astype(BF16)
                made.pop(0)[...] = keep[half:].astype(F32) + arrived[half:].astype(F32)
                continue
            total = keep[...] + arrived[...].astype(F32)
            if other is None:
                made.pop(0)[...] = total
                continue
            second = given.pop(0)[...]
            core = lax.axis_index("pipe")
            made.pop(0)[...] = jnp.where(core == 0, total, second)
            made.pop(0)[...] = jnp.where(core == 0, second, total)

    made = list(small_call(kernel, named.steps, given, made, after))
    done = [made[0]]
    for job, other in jobs:
        if job.stage < len(CORNERS):
            sent, job.keep = made.pop(0), made.pop(0)
            job.hop(sent)
        elif other is None:
            job.total = made.pop(0)
        else:
            job.total = (made.pop(0), swap(made.pop(0)))
    return done


def assemble(parts, name, shapes, after):
    def kernel(given, made):
        core = lax.axis_index("pipe")
        for out, (i, first, (rows, columns)) in zip(made, shapes):
            stayed, came = given[2 * i : 2 * i + 2]
            if first is None:
                total = stayed[:, -PAIR:] + came[:, -PAIR:]
                total = below(total, jnp.zeros((PAIR - total.shape[0], PAIR), F32)).T
                for j in range(4):
                    made[len(shapes) - 1 + j][...] = total[j : j + 1, :columns]
                break
            half = columns // 2
            at = slice(first, first + half)

            @pl.when(core == 0)
            def _():
                out[:, :half] = stayed[:, at]
                out[:, half:] = came[:, at]

            @pl.when(core != 0)
            def _():
                out[:, :half] = came[:, at]
                out[:, half:] = stayed[:, at]

    made = []
    for _, first, shape in shapes:
        made += [(shape, F32)] * (4 if first is None else 1)
    return small_call(kernel, name, [x for pair in parts for x in pair], made, after, True)


def place_rows(packs, sent, grad_in, after):
    def kernel(k):
        for layer in range(2):

            @pl.when(k.core == layer)
            def _():
                k.saves, k.loads, k.copies.count, k.present = [], {}, 0, set()
                for i, whose in enumerate((named.own_, named.sent_)):
                    k.load_from((named.out, i), k.place(named.layer_out, layer, whose), k.low.at[i])
                    if layer:
                        k.load_from((named.grad, i), k.place(named.outgoing, 1, whose), k.low.at[2 + i])
                if not layer:
                    k.load_from((named.grad, 0), k.outer[named.from_grad_in], k.high.at[0])
                    for i, name in enumerate((named.grad_high, named.grad_low)):
                        k.load_from((named.grad, 1 + i), k.place(name, 0, named.sent_), k.low.at[2 + i])
                for i in range(2):
                    rows = pl.ds((layer ^ i) * ROWS, ROWS)
                    k.ready((named.out, i))
                    k.put(k.low.at[i], k.outer[named.layer_out].at[rows])
                    k.ready((named.grad, i))
                    if layer:
                        k.high[i] = k.low[2 + i].astype(F32)
                    elif i:
                        k.ready((named.grad, 2))
                        k.high[i] = k.low[2].astype(F32) + k.low[3].astype(F32)
                    k.put(k.high.at[i], k.outer[named.grad_in].at[rows])
                k.finish()

        k.saves = []

    given = {named.from_grad_in: grad_in}
    for name in (named.fwd0, named.mid1, named.end0, named.end1):
        given |= {named.own_ + name: packs[name], named.sent_ + name: sent[name]}
    made = {named.layer_out: ((2 * ROWS, D), BF16), named.grad_in: ((2 * ROWS, D), F32)}
    held = {named.low: ((4, ROWS, D), BF16), named.high: ((2, ROWS, D), F32)}
    return call(kernel, named.place_rows, given, made, held, after=after)


def swap(x):
    return lax.ppermute(x, "pipe", [(0, 1), (1, 0)])


def body(
    inputs,
    cotangent,
    lengths,
    proj_stack,
    gain_one,
    bias_one,
    w_qkv,
    w_out,
    gain_two,
    bias_two,
    w_up,
    w_down,
):
    count = lax.axis_size("dp")
    by_corners = count == 2 ** len(CORNERS) and D // count % 16 == 0
    core = lax.axis_index("pipe")
    gains = jnp.concatenate([gain_one, bias_one, gain_two, bias_two], axis=0)
    own = {named.gains: gains, named.w_qkv: w_qkv, named.w_out: w_out, named.w_up: w_up, named.w_down: w_down}
    sent = {k: swap(own[k]) for k in (named.gains, named.w_qkv, named.w_out)}
    later = lax.optimization_barrier((w_up, w_down, *sent.values()))
    sent |= {named.w_up: swap(later[0]), named.w_down: swap(later[1])}
    projection = jnp.swapaxes(proj_stack, 1, 2)

    def weights(*names):
        return {named.own_ + k: own[k] for k in names} | {named.sent_ + k: sent[k] for k in names}

    def room(*names):
        return {k: WEIGHTS[k] for k in names}

    wide, full = ((ROWS, D), BF16), ((ROWS, D), F32)
    up, proj, few = ((ROWS, FF), BF16), ((ROWS, 3 * D), BF16), ((8, D), F32)
    mask = {named.mask: ((ROWS, ROWS), F32)}
    kept = {k: ((ROWS, columns), dtype) for k, (columns, dtype) in ATTN_KEPT.items()}
    pack = {k: ((ROWS, columns), BF16) for k, columns in PACKS.items()}

    chunked = ((CHUNKS, ROWS, CHUNK), BF16)
    takes = [k for k in ATTN_KEPT if k != named.middle]
    attention_held = kept | room(named.gains, named.w_qkv, named.w_out, named.projection) | mask
    attention_held |= {named.hidden: wide, named.entry: wide, named.mixed: wide}
    ffn_held = room(named.gains, named.w_up, named.w_down) | {named.middle: full, named.total: full, named.slope: chunked}
    forward_held = ffn_held | {named.second: wide, named.layer_out: wide, named.activated: chunked}
    back_held = ffn_held | {named.grad_ffn: wide, named.grad_up: up, named.grad_middle: full}
    back_held |= {named.grad_attn: wide, named.vectors: few}
    last_held = room(named.gains, named.w_qkv, named.w_out, named.projection) | mask | {k: kept[k] for k in takes}
    last_held |= {named.hidden: wide, named.grad_middle: full, named.total: full, named.vectors: few, named.sums: few}
    last_held |= {named.grad_attn: wide, named.grad_proj: proj}
    places = {named.lengths: lengths, named.from_projection: projection}

    packs, sent_packs = {}, {}

    def run(kernel, name, given, made, held, packs_made=(), packs_changed=(), layer=0, after=()):
        given = given | {k: packs[k] for k in packs_changed}
        made = made | {k: pack[k] for k in packs_made}
        result = call(kernel, name, given, made, held, layer, list(packs_changed), after)
        packs.update({k: result.pop(k) for k in (*packs_made, *packs_changed)})
        return result

    first = run(
        attention_kernel,
        named.attention,
        places | {named.from_hidden: inputs} | weights(named.gains, named.w_qkv, named.w_out),
        kept,
        attention_held,
        [named.fwd0],
    )
    first |= run(
        ffn_kernel,
        named.feed_forward,
        {named.from_middle: first[named.middle]} | weights(named.gains, named.w_up, named.w_down),
        {named.slope: up},
        forward_held,
        [],
        [named.fwd0],
    )
    sent_packs[named.fwd0] = swap(packs[named.fwd0])
    second = {named.cosine: first[named.cosine], named.sine: first[named.sine]}
    second |= run(
        second_layer_kernel,
        named.second_layer,
        places
        | {named.from_fwd0: packs[named.fwd0], named.from_grad_ffn: cotangent}
        | {named.from_ + k: first[k] for k in (named.cosine, named.sine)}
        | weights(named.gains, named.w_qkv, named.w_out, named.w_up, named.w_down),
        {k: kept[k] for k in takes if k not in (named.cosine, named.sine)}
        | {named.grad_middle: full, named.vectors: few},
        attention_held | forward_held | back_held,
        [named.act1, named.mid1],
        layer=1,
    )
    sent_packs[named.act1] = swap(packs[named.act1])
    later, _ = lax.optimization_barrier((packs[named.mid1], sent_packs[named.act1]))
    sent_packs[named.mid1] = swap(later)

    def second_back(after):
        second.update(
            run(
                attention_back_kernel,
                named.second_layer_back,
                places
                | {named.from_fwd0: packs[named.fwd0]}
                | {named.from_ + k: second[k] for k in (*takes, named.grad_middle, named.vectors)}
                | weights(named.gains, named.w_qkv, named.w_out),
                {named.sums: few},
                last_held | {named.outgoing: wide},
                [named.end1],
                layer=1,
                after=after,
            )
        )
        sent_packs[named.end1] = swap(packs[named.end1])

    def first_back(after):
        first.update(
            run(
                first_layer_back_kernel,
                named.first_layer_back,
                places
                | {named.from_hidden: inputs, named.from_end1: packs[named.end1]}
                | {named.from_ + k: first[k] for k in (*takes, named.slope, named.middle)}
                | weights(named.gains, named.w_qkv, named.w_out, named.w_up, named.w_down),
                {named.sums: few, named.grad_in: full},
                back_held | last_held | {named.grad_in: full, named.grad_high: wide, named.grad_low: wide},
                [named.end0],
                after=after,
            )
        )
        sent_packs[named.end0] = swap(packs[named.end0])

    sums = {}

    def start(name, layer, after=()):
        if not by_corners:
            return []
        used = {PLACES[layer][x][0] for pair in USED[name] for x in pair if x in PLACES[layer]}
        if name == named.down and not layer:
            used.add(named.end1)
        given = {}
        for k in sorted(used):
            given |= {named.own_ + k: packs[k], named.sent_ + k: sent_packs[k]}
        if name == named.down and layer:
            given[named.grad_ffn] = cotangent
        if name == named.attn:
            given[named.from_vectors] = (first, second)[layer][named.sums]
        z_first = (name, layer) == (named.down, 0)
        made = product(name, layer, given, after, z_first)
        sums[name, layer] = CornerSum(made, z_first)
        return [made[named.send]]

    def step(after, *jobs):
        if not by_corners:
            return []
        pairs = []
        for name, layer in jobs:
            last = layer == 0 and sums[name, layer].stage == len(CORNERS)
            pairs.append((sums[name, layer], sums[name, 1].total if last else None))
        return steps(pairs, after)

    down1, up1, attn1 = (named.down, 1), (named.up, 1), (named.attn, 1)
    down0, up0, attn0 = (named.down, 0), (named.up, 0), (named.attn, 0)
    done = start(named.down, 1)
    done = start(named.up, 1, done)
    second_back([*done, sent_packs[named.fwd0]])
    done = step([packs[named.end1]], down1)
    done = start(named.attn, 1, done)
    done = start(named.down, 0, done)
    done = step(done, up1)
    first_back(done)
    done = step([packs[named.end0]], attn1, down1)
    done = start(named.up, 0, done)
    done = step(done, down0, up1)
    done = start(named.attn, 0, done)
    done = step(done, attn1, down1)
    rows = place_rows(packs, sent_packs, first[named.grad_in], done)
    done = step([rows[named.layer_out]], up0, up1)
    done = step(done, attn0, down0, attn1, down1)
    done = step(done, up0, up1)
    done = step(done, attn0, down0, attn1)
    done = step(done, up0)
    done = step(done, attn0, down0)
    done = step(done, up0, attn0)

    def by_layer(first, second):
        return jnp.where(core == 0, first, second)

    if by_corners:
        shard = D // count
        grad_w_down, grad_w_up, grad_w_out, grad_w_qkv, *vectors = assemble(
            [sums[name, 0].total for name in (named.down, named.up, named.attn)],
            named.gather,
            [
                (0, 0, (FF // count, D)),
                (1, 0, (shard, FF)),
                (1, FF // 2, (shard, D)),
                (2, 0, (shard, 3 * D)),
                (2, None, (1, shard)),
            ],
            done,
        )
    else:

        def rows_of(layer, name):
            name, at, width = PLACES[layer][name]
            return [x[name][:, at : at + width] for x in (packs, sent_packs)]

        def grads_of(layer):
            if layer:
                return by_layer(cotangent[:ROWS], cotangent[ROWS:]), by_layer(
                    cotangent[ROWS:], cotangent[:ROWS]
                )
            return rows_of(1, named.outgoing)

        def one(lhs, rhs):
            parts = [
                sum(dot_tn(a, b) for a, b in zip(lhs(layer), rhs(layer))) for layer in range(2)
            ]
            return lax.psum_scatter(by_layer(*parts), "dp", scatter_dimension=0, tiled=True)

        def both(name):
            return lambda layer: rows_of(layer, name)

        grad_w_down = one(both(named.activated), grads_of)
        grad_w_up = one(both(named.second), both(named.grad_up))
        grad_w_qkv = one(both(named.entry), both(named.grad_proj))
        grad_w_out = one(both(named.mixed), both(named.grad_attn))
        vectors = by_layer(*[x[named.sums] + swap(x[named.sums]) for x in (first, second)])
        vectors = lax.psum_scatter(vectors, "dp", scatter_dimension=1, tiled=True)
        vectors = [vectors[i][None] for i in range(4)]

    return (
        rows[named.layer_out][None],
        rows[named.grad_in][None],
        vectors[0],
        vectors[1],
        grad_w_qkv[None],
        grad_w_out[None],
        vectors[2],
        vectors[3],
        grad_w_up[None],
        grad_w_down[None],
    )


def solution(mesh):
    placed = (
        P("dp", None),
        P("dp", None),
        P("dp", None),
        P(),
        P("pipe", None),
        P("pipe", None),
        P("pipe", None, None),
        P("pipe", None, None),
        P("pipe", None),
        P("pipe", None),
        P("pipe", None, None),
        P("pipe", None, None),
    )
    return jax.shard_map(
        body,
        mesh=mesh,
        in_specs=placed,
        out_specs=(
            P("pipe", "dp", None),
            P("pipe", "dp", None),
            P("pipe", "dp"),
            P("pipe", "dp"),
            P("pipe", "dp", None),
            P("pipe", "dp", None),
            P("pipe", "dp"),
            P("pipe", "dp"),
            P("pipe", "dp", None),
            P("pipe", "dp", None),
        ),
        check_vma=False,
    )
```

```python
import math
import types

import jax
import jax.numpy as jnp
from jax import lax
from jax.experimental import pallas as pl
from jax.experimental.pallas import tpu as pltpu
from jax.sharding import PartitionSpec as P

class Names:
    def __getattr__(self, name):
        return name


named = Names()

D = 768
HEADS = 12
HEAD = 64
FEAT = 32
FF = 3072
ROWS = 256
MOLS = 3
NSTACK = 4
STEP = 7
EPSILON = 1e-05

PACK = 4
GROUPS = HEADS // PACK
WIDE = PACK * HEAD
THIN = PACK * FEAT
PAIR = 2 * HEAD
CHUNK = 1024
CHUNKS = FF // CHUNK
SCALE = HEAD ** -0.25
MIB = 1024 * 1024
LIMIT = 40 * MIB

F32 = jnp.float32
BF16 = jnp.bfloat16

ATTN_KEPT = {
    named.turned_q: (D, F32),
    named.turned_k: (D, F32),
    named.value: (D, F32),
    named.phi_q: (GROUPS * THIN, F32),
    named.phi_k: (GROUPS * THIN, F32),
    named.middle: (D, F32),
    named.cosine: (PAIR, F32),
    named.sine: (PAIR, F32),
}
WEIGHTS = {
    named.w_qkv: ((D, 3 * D), BF16),
    named.w_out: ((D, D), BF16),
    named.w_up: ((CHUNKS, D, CHUNK), BF16),
    named.w_down: ((CHUNKS, CHUNK, D), BF16),
    named.gains: ((4, D), F32),
    named.projection: ((FEAT, HEAD), F32),
}
PLACES = (
    {
        named.entry: (named.fwd0, 0, D),
        named.mixed: (named.fwd0, D, D),
        named.second: (named.fwd0, 2 * D, D),
        named.layer_out: (named.fwd0, 3 * D, D),
        named.activated: (named.fwd0, 4 * D, FF),
        named.grad_attn: (named.mid0, 0, D),
        named.grad_up: (named.mid0, D, FF),
        named.grad_high: (named.end0, 0, D),
        named.grad_low: (named.end0, D, D),
        named.grad_proj: (named.end0, 2 * D, 3 * D),
    },
    {
        named.activated: (named.act1, 0, FF),
        named.second: (named.mid1, 0, D),
        named.mixed: (named.mid1, D, D),
        named.entry: (named.mid1, 2 * D, D),
        named.layer_out: (named.mid1, 3 * D, D),
        named.grad_attn: (named.mid1, 4 * D, D),
        named.grad_up: (named.mid1, 5 * D, FF),
        named.outgoing: (named.end1, 0, D),
        named.grad_proj: (named.end1, D, 3 * D),
    },
)
PACKS = {named.fwd0: 4 * D + FF, named.act1: FF, named.mid1: 5 * D + FF, named.end1: 4 * D, named.mid0: D + FF, named.end0: 5 * D}


class Copies:
    def __init__(self, semaphores):
        self.semaphores = semaphores
        self.count = 0

    def start(self, source, target):
        copy = pltpu.make_async_copy(source, target, self.semaphores.at[self.count])
        self.count += 1
        copy.start()
        return copy

    def either(self, condition, source, other, target):
        semaphore = self.semaphores.at[self.count]
        self.count += 1
        copy = pltpu.make_async_copy(source, target, semaphore)

        @pl.when(condition)
        def _():
            copy.start()

        @pl.when(jnp.logical_not(condition))
        def _():
            pltpu.make_async_copy(other, target, semaphore).start()

        return copy


class Kernel:
    def __init__(self, outer, held, semaphores, layer):
        self.outer = outer
        self.held = held
        self.copies = Copies(semaphores)
        self.loads = {}
        self.saves = []
        self.core = lax.axis_index("pipe")
        self.layer = layer
        self.present = set()

    def __getattr__(self, name):
        return self.held[name]

    def new(self, name):
        return name not in self.loads and name not in self.present

    def load(self, *names):
        for name in names:
            if self.new(name):
                self.loads[name] = [self.copies.start(self.outer[named.from_ + name], self.held[name])]

    def load_from(self, name, source, target=None):
        if self.new(name):
            target = self.held[name] if target is None else target
            self.loads[name] = [self.copies.start(source, target)]

    def load_slope(self):
        for c in range(CHUNKS):
            if self.new((named.slope, c)):
                source = self.outer[named.from_slope].at[:, pl.ds(c * CHUNK, CHUNK)]
                self.loads[named.slope, c] = [self.copies.start(source, self.held[named.slope].at[c])]

    def load_weight(self, name, chunk=None):
        key = name if chunk is None else (name, chunk)
        if not self.new(key):
            return
        target = self.held[name]
        if chunk is not None:
            target = target.at[chunk]
        at = pl.ds((chunk or 0) * CHUNK, CHUNK)

        def part(source):
            if name == named.w_up:
                return source.at[0, :, at]
            if name == named.w_down:
                return source.at[0, at]
            return source if name == named.gains else source.at[0]

        self.loads[key] = [
            self.copies.either(
                self.core == self.layer,
                part(self.outer[named.own_ + name]),
                part(self.outer[named.sent_ + name]),
                target,
            )
        ]

    def load_hidden(self):
        if self.layer == 0:
            rows = pl.ds(pl.multiple_of(self.core * ROWS, ROWS), ROWS)
            source = self.outer[named.from_hidden].at[rows]
        else:
            source = self.place(named.layer_out, 0, named.from_)
        self.load_from(named.hidden, source)

    def load_projection(self):
        self.load_from(named.projection, self.outer[named.from_projection].at[STEP % NSTACK])

    def load_grad(self):
        if self.layer:
            rows = pl.ds(pl.multiple_of(self.core * ROWS, ROWS), ROWS)
            source = self.outer[named.from_grad_ffn].at[rows]
        else:
            source = self.place(named.outgoing, 1, named.from_)
        self.load_from(named.grad_ffn, source)

    def ready(self, *names):
        for name in names:
            for copy in self.loads.pop(name, ()):
                copy.wait()
            self.present.add(name)

    def save(self, *names):
        for name in names:
            if name in self.outer:
                self.put(self.held[name], self.outer[name])

    def pack(self, name):
        self.put(self.held[name], self.place(name, self.layer))

    def place(self, name, layer, prefix=""):
        pack, first, width = PLACES[layer][name]
        return self.outer[prefix + pack].at[:, pl.ds(first, width)]

    def put(self, source, target):
        self.saves.append(self.copies.start(source, target))

    def finish(self):
        assert not self.loads
        for copy in self.saves:
            copy.wait()


def call(kernel, name, given, made, held, layer=0, changed=(), after=()):
    anywhere = pl.BlockSpec(memory_space=pl.ANY)
    names, places = list(given), list(held)
    outs = list(changed) + list(made)
    shapes = [jax.ShapeDtypeStruct(given[key].shape, given[key].dtype) for key in changed]
    shapes += [jax.ShapeDtypeStruct(*x) for x in made.values()]

    def run(*refs):
        outer = dict(zip(names, refs))
        refs = refs[len(names) + len(after) :]
        outer |= dict(zip(outs, refs))
        refs = refs[len(outs) :]
        k = Kernel(outer, dict(zip(places, refs)), refs[-1], layer)
        kernel(k)
        k.finish()

    results = pl.pallas_call(
        run,
        out_shape=[pltpu.HBM(x.shape, x.dtype) for x in shapes],
        in_specs=[
            pl.BlockSpec(memory_space=pltpu.SMEM) if key == named.lengths else anywhere for key in names
        ]
        + [anywhere] * len(after),
        out_specs=[anywhere] * len(shapes),
        input_output_aliases={names.index(key): i for i, key in enumerate(changed)},
        scratch_shapes=[pltpu.VMEM(*x) for x in held.values()]
        + [pltpu.SemaphoreType.DMA((80,))],
        compiler_params=pltpu.CompilerParams(vmem_limit_bytes=LIMIT),
        cost_estimate=pl.CostEstimate(
            flops=10**12, bytes_accessed=1000, transcendentals=0
        ),
        name=name,
    )(
        *[
            x
            if key == named.lengths or key.startswith(named.sent_)
            else pltpu.with_memory_space_constraint(x, pltpu.HBM)
            for key, x in given.items()
        ],
        *[pltpu.with_memory_space_constraint(x, pltpu.HBM) for x in after],
    )
    return dict(zip(outs, results))


def dot(a, b):
    return jnp.dot(a, b, preferred_element_type=F32)


def dot_nt(a, b):
    return lax.dot_general(a, b, (((1,), (1,)), ((), ())), preferred_element_type=F32)


def dot_tn(a, b):
    return lax.dot_general(a, b, (((0,), (0,)), ((), ())), preferred_element_type=F32)


def beside(*parts):
    return jnp.concatenate(parts, axis=1)


def below(*parts):
    return jnp.concatenate(parts, axis=0)


def normalize(hidden):
    average = jnp.mean(hidden, axis=-1, keepdims=True)
    centred = hidden - average
    inverse = lax.rsqrt(jnp.mean(centred * centred, axis=-1, keepdims=True) + EPSILON)
    return centred * inverse, inverse


def normalize_back(grad_normed, normed, inverse):
    return inverse * (
        grad_normed
        - jnp.mean(grad_normed, axis=-1, keepdims=True)
        - normed * jnp.mean(grad_normed * normed, axis=-1, keepdims=True)
    )


def iota(shape, axis):
    return lax.broadcasted_iota(jnp.int32, shape, axis)


def molecules(lengths, block, row):
    which = jnp.full(row.shape, MOLS, jnp.int32)
    first = jnp.zeros(row.shape, jnp.int32)
    opening = jnp.int32(0)
    for s in range(MOLS):
        closing = opening + lengths[block, s]
        inside = (row >= opening) & (row < closing)
        which = jnp.where(inside, s, which)
        first = jnp.where(inside, opening, first)
        opening = closing
    return which, first


def together(lengths, block):
    down, _ = molecules(lengths, block, iota((ROWS, 128), 0))
    along, _ = molecules(lengths, block, iota((1, ROWS), 1))
    halves = [
        jnp.where((down == along[:, at : at + 128]) & (down < MOLS), 1.0, 0.0)
        for at in range(0, ROWS, 128)
    ]
    return beside(*halves)


def tables(lengths, block):
    row = iota((ROWS, PAIR), 0)
    _, first = molecules(lengths, block, row)
    lane = iota((1, PAIR), 1)
    index = (lane & (HEAD // 2 - 1)).astype(F32)
    angles = (row - first).astype(F32) * jnp.exp(index * (-2.0 * math.log(10000.0) / HEAD))
    sine = jnp.sin(angles)
    return jnp.cos(angles), jnp.where(lane & (HEAD // 2) == 0, -sine, sine)


def swap_halves(x):
    half = HEAD // 2
    width = x.shape[1]
    low = iota((1, width), 1) & half == 0
    return jnp.where(low, pltpu.roll(x, width - half, 1), pltpu.roll(x, half, 1))


def block_diagonal(projection):
    tiled = below(*[beside(*[projection] * PACK)] * PACK)
    same = iota((THIN, WIDE), 0) >> 5 == iota((THIN, WIDE), 1) >> 6
    return jnp.where(same, tiled, 0.0), same.astype(F32)


def two_parts(x):
    high = x.astype(BF16)
    return high, (x - high.astype(F32)).astype(BF16)


def features(turned, proj_both, proj_high, norm_part):
    scaled = turned * SCALE
    high, low = two_parts(scaled)
    square_high, square_low = two_parts(scaled * scaled)
    both = dot_nt(high, proj_both)
    rest = dot_nt(beside(low, square_high, square_low), beside(proj_high, norm_part, norm_part))
    return jnp.exp(both[:, :THIN] + both[:, THIN:] + rest) * (1.0 / math.sqrt(FEAT))


def only(x, head, width):
    lane = iota((1, x.shape[1]), 1)
    return jnp.where((lane >= head * width) & (lane < (head + 1) * width), x, jnp.zeros_like(x))


def gelu_and_slope(u):
    bell = jnp.exp(-0.5 * u * u)
    t = 1.0 / (1.0 + jnp.abs(u) * (0.3275911 * math.sqrt(0.5)))
    tail = 0.5 * 1.061405429
    for c in (-1.453152027, 1.421413741, -0.284496736, 0.254829592):
        tail = tail * t + 0.5 * c
    tail = tail * t * bell
    phi = jnp.where(u >= 0.0, 1.0 - tail, tail)
    return u * phi, phi + u * bell * (1.0 / math.sqrt(2.0 * math.pi))


def attention_kernel(k):
    k.load_weight(named.gains)
    k.load_hidden()
    k.load_projection()
    k.load_weight(named.w_qkv)
    k.load_weight(named.w_out)
    lengths = k.outer[named.lengths]
    if k.layer == 0:
        k.cosine[...], k.sine[...] = tables(lengths, k.core)
        k.save(named.cosine, named.sine)
    else:
        k.load(named.cosine, named.sine)
    k.mask[...] = together(lengths, k.core)
    k.ready(named.projection)
    proj_block, own = block_diagonal(k.projection[...])
    proj_high, proj_low = two_parts(proj_block)
    proj_both = below(proj_high, proj_low)
    norm_part = (-0.5 * own).astype(BF16)
    k.ready(named.hidden, named.gains)
    normed, _ = normalize(k.hidden[...].astype(F32))
    k.entry[...] = (normed * k.gains[0:1] + k.gains[1:2]).astype(BF16)
    k.pack(named.entry)
    if k.layer:
        k.ready(named.cosine, named.sine)
    k.ready(named.w_qkv)
    for g in range(GROUPS):
        cols = slice(g * WIDE, (g + 1) * WIDE)
        thin = slice(g * THIN, (g + 1) * THIN)
        entry = k.entry[...]
        cosine = beside(k.cosine[...], k.cosine[...])
        sine = beside(k.sine[...], k.sine[...])
        query = dot(entry, k.w_qkv[:, g * WIDE : (g + 1) * WIDE])
        key = dot(entry, k.w_qkv[:, D + g * WIDE : D + (g + 1) * WIDE])
        value = dot(entry, k.w_qkv[:, 2 * D + g * WIDE : 2 * D + (g + 1) * WIDE])
        query = query * cosine + swap_halves(query) * sine
        key = key * cosine + swap_halves(key) * sine
        phi_q = features(query, proj_both, proj_high, norm_part)
        phi_k = features(key, proj_both, proj_high, norm_part)
        k.turned_q[:, cols] = query
        k.turned_k[:, cols] = key
        k.value[:, cols] = value
        k.phi_q[:, thin] = phi_q
        k.phi_k[:, thin] = phi_k
        q_high, q_low = two_parts(phi_q)
        k_high, k_low = two_parts(phi_k)
        v_high, v_low = two_parts(value)
        scores = dot_nt(
            below(*[beside(only(q_high, h, FEAT), only(q_low, h, FEAT)) for h in range(PACK)]),
            beside(k_high, k_high),
        ) + dot_nt(below(*[only(q_high, h, FEAT) for h in range(PACK)]), k_low)
        mask = k.mask[...]
        inside = jnp.sum(mask, axis=1, keepdims=True) > 0.5
        for pair in range(PACK // 2):
            at = slice(pair * PAIR, (pair + 1) * PAIR)
            lanes = slice(g * WIDE + pair * PAIR, g * WIDE + (pair + 1) * PAIR)
            parts, inverses = [], []
            for h in (2 * pair, 2 * pair + 1):
                score = scores[h * ROWS : (h + 1) * ROWS] * mask
                den = jnp.sum(score, axis=1, keepdims=True)
                inverses.append(jnp.where(inside, 1.0 / jnp.where(inside, den, 1.0), 0.0))
                parts.append(two_parts(score))
            high = below(parts[0][0], parts[1][0])
            low = below(parts[0][1], parts[1][1])
            both = dot(high, beside(v_high[:, at], v_low[:, at]))
            summed = both[:, :PAIR] + both[:, PAIR:] + dot(low, v_high[:, at])
            left = iota((1, PAIR), 1) < HEAD
            inverse = jnp.where(left, inverses[0], inverses[1])
            mixed = jnp.where(left, summed[:ROWS], summed[ROWS:]) * inverse
            k.mixed[:, lanes] = mixed.astype(BF16)
    k.save(named.turned_q, named.turned_k, named.value, named.phi_q, named.phi_k)
    k.pack(named.mixed)
    k.ready(named.w_out)
    k.middle[...] = k.hidden[...].astype(F32) + dot(k.mixed[...], k.w_out[...])
    k.present.add(named.middle)
    k.save(named.middle)


def ffn_kernel(k):
    k.load_weight(named.gains)
    k.load(named.middle)
    for c in range(CHUNKS):
        k.load_weight(named.w_up, c)
        k.load_weight(named.w_down, c)
    k.ready(named.middle, named.gains)
    normed, _ = normalize(k.middle[...])
    k.second[...] = (normed * k.gains[2:3] + k.gains[3:4]).astype(BF16)
    k.pack(named.second)
    k.total[...] = k.middle[...]
    if k.layer:
        for c in range(CHUNKS):
            k.ready((named.w_up, c), (named.w_down, c))

    def leave(c):
        at = pl.ds(c * CHUNK, CHUNK)
        k.put(k.activated.at[c], k.place(named.activated, k.layer).at[:, at])
        if named.slope in k.outer:
            k.put(k.slope.at[c], k.outer[named.slope].at[:, at])

    for c in range(CHUNKS):
        if not k.layer:
            k.ready((named.w_up, c), (named.w_down, c))
        activated, slope = gelu_and_slope(dot(k.second[...], k.w_up[c]))
        k.activated[c] = activated.astype(BF16)
        k.slope[c] = slope.astype(BF16)
        k.present.add((named.slope, c))
        if not k.layer:
            leave(c)
        k.total[...] += dot(k.activated[c], k.w_down[c])
    if k.layer:
        for c in range(CHUNKS):
            leave(c)
    k.layer_out[...] = k.total[...].astype(BF16)
    k.pack(named.layer_out)


def ffn_back_kernel(k):
    k.load_grad()
    k.load_slope()
    for c in range(CHUNKS):
        k.load_weight(named.w_down, c)
        k.load_weight(named.w_up, c)
    k.load(named.middle)
    k.load_weight(named.gains)
    k.vectors[...] = jnp.zeros_like(k.vectors)
    k.ready(named.grad_ffn)
    k.ready((named.w_down, 0))
    grad_act = dot_nt(k.grad_ffn[...], k.w_down[0])
    for c in range(CHUNKS):
        at = slice(c * CHUNK, (c + 1) * CHUNK)
        if c + 1 < CHUNKS:
            k.ready((named.w_down, c + 1))
            upcoming = dot_nt(k.grad_ffn[...], k.w_down[c + 1])
        k.ready((named.slope, c), (named.w_up, c))
        k.grad_up[:, at] = (grad_act * k.slope[c].astype(F32)).astype(BF16)
        piece = dot_nt(k.grad_up[:, at], k.w_up[c])
        if c == 0:
            k.total[...] = piece
        else:
            k.total[...] += piece
        if c + 1 < CHUNKS:
            grad_act = upcoming
    k.pack(named.grad_up)
    k.ready(named.middle, named.gains)
    normed, inverse = normalize(k.middle[...])
    grad = k.total[...]
    k.vectors[2:3] = jnp.sum(grad * normed, axis=0, keepdims=True)
    k.vectors[3:4] = jnp.sum(grad, axis=0, keepdims=True)
    k.save(named.vectors)
    k.grad_middle[...] = k.grad_ffn[...].astype(F32) + normalize_back(
        grad * k.gains[2:3], normed, inverse
    )
    k.grad_attn[...] = k.grad_middle[...].astype(BF16)
    k.pack(named.grad_attn)
    k.present |= {named.grad_middle, named.vectors, named.grad_attn}
    k.save(named.grad_middle)


def attention_back_kernel(k):
    takes = [name for name in ATTN_KEPT if name != named.middle]
    k.load(named.grad_middle)
    k.load_weight(named.w_out)
    k.load_projection()
    k.load(*takes)
    k.load_weight(named.w_qkv)
    k.load_hidden()
    k.load_weight(named.gains)
    k.load(named.vectors)
    k.mask[...] = together(k.outer[named.lengths], k.core)
    k.ready(named.projection, named.grad_middle, named.w_out, *takes)
    if named.grad_attn not in k.present:
        k.grad_attn[...] = k.grad_middle[...].astype(BF16)
    proj_block, own = block_diagonal(k.projection[...])
    back_part = beside(proj_block, own).astype(BF16)
    back_part = below(back_part, back_part)
    for g in range(GROUPS):
        cols = slice(g * WIDE, (g + 1) * WIDE)
        thin = slice(g * THIN, (g + 1) * THIN)
        cosine = beside(k.cosine[...], k.cosine[...])
        sine = beside(k.sine[...], k.sine[...])
        mask = k.mask[...]
        inside = jnp.sum(mask, axis=1, keepdims=True) > 0.5
        grad_mixed = dot_nt(k.grad_attn[...], k.w_out[cols, :]).astype(BF16)
        v_high, v_low = two_parts(k.value[:, cols])
        phi_q = k.phi_q[:, thin]
        phi_k = k.phi_k[:, thin]
        q_all = [only(phi_q.astype(BF16), h, FEAT) for h in range(PACK)]
        k_high = phi_k.astype(BF16)
        k_all = [only(k_high, h, FEAT) for h in range(PACK)]
        grad_scores, grad_value = [], []
        for pair in range(PACK // 2):
            at = slice(pair * PAIR, (pair + 1) * PAIR)
            own_grad = [only(grad_mixed[:, at], i, HEAD) for i in range(2)]
            score = dot_nt(below(*q_all[2 * pair : 2 * pair + 2]), k_high)
            grad_share = dot_nt(
                below(*[beside(x, x) for x in own_grad]), beside(v_high[:, at], v_low[:, at])
            )
            shares = []
            for i in range(2):
                one = score[i * ROWS : (i + 1) * ROWS] * mask
                den = jnp.sum(one, axis=1, keepdims=True)
                inverse = jnp.where(inside, 1.0 / jnp.where(inside, den, 1.0), 0.0)
                share = one * inverse
                grad = grad_share[i * ROWS : (i + 1) * ROWS]
                centre = jnp.sum(share * grad, axis=1, keepdims=True)
                grad_scores.append((((grad - centre) * inverse) * mask).astype(BF16))
                shares.append(share.astype(BF16))
            grad_value.append(dot_tn(below(*shares), below(*own_grad)))
        grad_phi_q = dot(beside(*grad_scores), below(*k_all))
        grad_phi_k = dot_tn(below(*grad_scores), below(*q_all))

        def features_back(grad_phi, phi, turned):
            high, low = two_parts(grad_phi * phi)
            back = dot(beside(high, low), back_part)
            grad = (back[:, :WIDE] - turned * SCALE * back[:, WIDE:]) * SCALE
            return (grad * cosine + swap_halves(grad * sine)).astype(BF16)

        grad_query = features_back(grad_phi_q, phi_q, k.turned_q[:, cols])
        grad_key = features_back(grad_phi_k, phi_k, k.turned_k[:, cols])
        k.grad_proj[:, g * WIDE : (g + 1) * WIDE] = grad_query
        k.grad_proj[:, D + g * WIDE : D + (g + 1) * WIDE] = grad_key
        k.grad_proj[:, 2 * D + g * WIDE : 2 * D + (g + 1) * WIDE] = beside(*grad_value).astype(BF16)
    k.pack(named.grad_proj)
    k.ready(named.w_qkv)
    for i in range(3):
        at = slice(i * D, (i + 1) * D)
        piece = dot_nt(k.grad_proj[:, at], k.w_qkv[:, at])
        if i == 0:
            k.total[...] = piece
        else:
            k.total[...] += piece
    k.ready(named.hidden, named.gains, named.vectors)
    normed, inverse = normalize(k.hidden[...].astype(F32))
    grad = k.total[...]
    k.vectors[0:1] = jnp.sum(grad * normed, axis=0, keepdims=True)
    k.vectors[1:2] = jnp.sum(grad, axis=0, keepdims=True)
    k.held[named.sums][...] = k.vectors[...]
    k.save(named.sums)
    grad_hidden = k.grad_middle[...] + normalize_back(grad * k.gains[0:1], normed, inverse)
    if k.layer:
        k.outgoing[...] = grad_hidden.astype(BF16)
        k.pack(named.outgoing)
    else:
        k.grad_in[...] = grad_hidden
        k.save(named.grad_in)
        k.grad_high[...], k.grad_low[...] = two_parts(grad_hidden)
        k.pack(named.grad_high)
        k.pack(named.grad_low)


def second_layer_kernel(k):
    k.load_weight(named.gains)
    k.load_hidden()
    k.load_projection()
    k.load(named.cosine, named.sine)
    k.load_weight(named.w_qkv)
    k.load_weight(named.w_out)
    for c in range(CHUNKS):
        k.load_weight(named.w_up, c)
        k.load_weight(named.w_down, c)
    k.load_grad()
    attention_kernel(k)
    ffn_kernel(k)
    ffn_back_kernel(k)


CORNERS = (1, 2, 4, 8)
VECTORS = -1
DOWN = (named.activated, named.grad_ffn)
PLANS = {
    named.down: (((DOWN, 0, 384),), ((DOWN, 384, 384),)),
    named.up: (
        (
            ((named.second, named.grad_up), 0, 768),
            ((named.second, named.grad_up), 768, 768),
            ((named.mixed, named.grad_attn), 0, 384),
        ),
        (
            ((named.second, named.grad_up), 1536, 768),
            ((named.second, named.grad_up), 2304, 768),
            ((named.mixed, named.grad_attn), 384, 384),
        ),
    ),
    named.attn: (
        (((named.entry, named.grad_proj), 0, 768), ((named.entry, named.grad_proj), 768, 384), (VECTORS, 0, 128)),
        (((named.entry, named.grad_proj), 1152, 768), ((named.entry, named.grad_proj), 1920, 384), (VECTORS, 0, 128)),
    ),
}


USED = {
    name: {tile[0] for tiles in plan for tile in tiles if tile[0] != VECTORS}
    for name, plan in PLANS.items()
}


def orders(z_first):
    x, y, near, far = CORNERS
    return ((near, x, y, far), (near, y, x, far)) if z_first else ((x, y, near, far), (y, x, near, far))


def product_kernel(k, name, z_first):
    me = lax.axis_index("dp")
    rows = k.out.shape[0]
    shard = rows // lax.axis_size("dp")

    def fetch(name, target, first, width, at):
        if name == named.grad_ffn and k.layer:
            sources = [
                k.outer[named.grad_ffn].at[pl.ds(pl.multiple_of((k.core ^ i) * ROWS, ROWS), ROWS)]
                for i in range(2)
            ]
        elif name == named.grad_ffn:
            sources = [k.place(named.outgoing, 1, x) for x in (named.own_, named.sent_)]
        else:
            sources = [k.place(name, k.layer, x) for x in (named.own_, named.sent_)]
        return [
            k.copies.start(
                x.at[:, pl.ds(first, width)], target.at[pl.ds(i * ROWS, ROWS), pl.ds(at, width)]
            )
            for i, x in enumerate(sources)
        ]

    def leave(group, at, width):
        order = orders(z_first)[group]
        for slot in range(16):
            step = sum(bit for i, bit in enumerate(order) if slot & (8 >> i) == 0)
            where = me ^ step
            half = k.outer[named.send if slot < 8 else named.keep]
            target = half.at[pl.ds((slot & 7) * shard, shard), pl.ds(at, width)]
            k.put(k.out.at[pl.ds(pl.multiple_of(where * shard, 16), shard), pl.ds(at, width)], target)

    for group, tiles in enumerate(PLANS[name]):

        @pl.when(k.core == group)
        def _():
            k.loads, k.saves, k.copies.count, k.present = {}, [], 0, set()
            if name == named.down:
                ((left, right), first, width) = tiles[0]
                k.loads[named.right] = fetch(right, k.right, first, width, 0)
                for c in range(0, rows, D):
                    k.loads[named.left, c] = fetch(left, k.left_activated, c, D, c)
                k.ready(named.right)
                for c in range(0, rows, D):
                    k.ready((named.left, c))
                    k.out[c : c + D] = dot_tn(k.left_activated[:, c : c + D], k.right[...]).astype(BF16)
                leave(group, 0, width)
            else:
                at = 0
                for i, (names, first, width) in enumerate(tiles):
                    if names == VECTORS:
                        k.load(named.vectors)
                    else:
                        left = names[0]
                        if left not in k.loads:
                            k.loads[left] = fetch(left, k.held[named.left_ + left], 0, D, 0)
                        k.loads[named.right, i] = fetch(names[1], k.right, first, width, at)
                    at += width
                at = 0
                for i, (names, first, width) in enumerate(tiles):
                    if names == VECTORS:
                        k.ready(named.vectors)
                        total = below(k.vectors[...], jnp.zeros((width - 8, D), F32))
                        got = total.T
                    else:
                        k.ready(names[0], (named.right, i))
                        got = dot_tn(k.held[named.left_ + names[0]][...], k.right[:, at : at + width])
                    k.out[:, at : at + width] = got.astype(BF16)
                    leave(group, at, width)
                    at += width
            k.finish()

    k.loads, k.saves = {}, []


def product(name, layer, given, after, z_first):
    plan = PLANS[name]
    lefts = sorted({tile[0][0] for tiles in plan for tile in tiles if tile[0] != VECTORS})
    widths = {x: PLACES[1][x][2] for x in lefts}
    rows = widths[lefts[0]]
    columns = sum(tile[2] for tile in plan[0])
    held = {named.left_ + x: ((2 * ROWS, w), BF16) for x, w in widths.items()}
    held |= {named.right: ((2 * ROWS, columns), BF16), named.out: ((rows, columns), BF16)}
    if name == named.attn:
        held[named.vectors] = ((8, D), F32)
    made = {kind: ((rows // 2, columns), BF16) for kind in (named.send, named.keep)}
    return call(
        lambda k: product_kernel(k, name, z_first),
        named.product_ + name,
        given,
        made,
        held,
        layer=layer,
        after=after,
    )


def small_call(kernel, name, given, made, after, last=False):
    inside = pl.BlockSpec(memory_space=pltpu.VMEM)
    anywhere = pl.BlockSpec(memory_space=pl.ANY)

    def run(*refs):
        kernel(refs[: len(given)], refs[len(given) + len(after) :])

    return pl.pallas_call(
        run,
        out_shape=[pltpu.HBM(*x) if last else jax.ShapeDtypeStruct(*x) for x in made],
        in_specs=[inside] * len(given) + [anywhere] * len(after),
        out_specs=[inside] * len(made),
        compiler_params=pltpu.CompilerParams(vmem_limit_bytes=24 * MIB),
        cost_estimate=pl.CostEstimate(flops=10**12, bytes_accessed=1000, transcendentals=0),
        name=name,
    )(*given, *[pltpu.with_memory_space_constraint(x, pltpu.HBM) for x in after])


class CornerSum:
    def __init__(self, made, z_first):
        self.orders = orders(z_first)
        self.keep = made[named.keep]
        self.stage = 0
        self.hop(made[named.send])

    def hop(self, x):
        count = lax.axis_size("dp")
        pairs = []
        for core in range(2):
            bit = self.orders[core][self.stage]
            pairs += [(core * count + i, core * count + (i ^ bit)) for i in range(count)]
        self.arriving = lax.ppermute(x, ("pipe", "dp"), pairs)
        self.stage += 1


def steps(jobs, after):
    given, made = [], []
    for job, other in jobs:
        given += [job.keep, job.arriving]
        rows, columns = job.keep.shape
        if job.stage < len(CORNERS):
            made += [((rows // 2, columns), BF16), ((rows // 2, columns), F32)]
        elif other is None:
            made += [((rows, columns), F32)]
        else:
            given.append(other)
            made += [((rows, columns), F32)] * 2

    def kernel(given, made):
        given, made = list(given), list(made)
        for job, other in jobs:
            keep, arrived = given.pop(0), given.pop(0)
            half = keep.shape[0] // 2
            if job.stage < len(CORNERS):
                made.pop(0)[...] = (
                    keep[:half].astype(F32) + arrived[:half].astype(F32)
                ).astype(BF16)
                made.pop(0)[...] = keep[half:].astype(F32) + arrived[half:].astype(F32)
                continue
            total = keep[...] + arrived[...].astype(F32)
            if other is None:
                made.pop(0)[...] = total
                continue
            second = given.pop(0)[...]
            core = lax.axis_index("pipe")
            made.pop(0)[...] = jnp.where(core == 0, total, second)
            made.pop(0)[...] = jnp.where(core == 0, second, total)

    made = list(small_call(kernel, named.steps, given, made, after))
    done = [made[0]]
    for job, other in jobs:
        if job.stage < len(CORNERS):
            sent, job.keep = made.pop(0), made.pop(0)
            job.hop(sent)
        elif other is None:
            job.total = made.pop(0)
        else:
            job.total = (made.pop(0), swap(made.pop(0)))
    return done


def assemble(parts, name, shapes, after):
    def kernel(given, made):
        core = lax.axis_index("pipe")
        for out, (i, first, (rows, columns)) in zip(made, shapes):
            stayed, came = given[2 * i : 2 * i + 2]
            if first is None:
                total = stayed[:, -PAIR:] + came[:, -PAIR:]
                total = below(total, jnp.zeros((PAIR - total.shape[0], PAIR), F32)).T
                for j in range(4):
                    made[len(shapes) - 1 + j][...] = total[j : j + 1, :columns]
                break
            half = columns // 2
            at = slice(first, first + half)

            @pl.when(core == 0)
            def _():
                out[:, :half] = stayed[:, at]
                out[:, half:] = came[:, at]

            @pl.when(core != 0)
            def _():
                out[:, :half] = came[:, at]
                out[:, half:] = stayed[:, at]

    made = []
    for _, first, shape in shapes:
        made += [(shape, F32)] * (4 if first is None else 1)
    return small_call(kernel, name, [x for pair in parts for x in pair], made, after, True)


def place_rows(packs, sent, grad_in, after):
    def kernel(k):
        for layer in range(2):

            @pl.when(k.core == layer)
            def _():
                k.saves, k.loads, k.copies.count, k.present = [], {}, 0, set()
                for i, whose in enumerate((named.own_, named.sent_)):
                    k.load_from((named.out, i), k.place(named.layer_out, layer, whose), k.low.at[i])
                    if layer:
                        k.load_from((named.grad, i), k.place(named.outgoing, 1, whose), k.low.at[2 + i])
                if not layer:
                    k.load_from((named.grad, 0), k.outer[named.from_grad_in], k.high.at[0])
                    for i, name in enumerate((named.grad_high, named.grad_low)):
                        k.load_from((named.grad, 1 + i), k.place(name, 0, named.sent_), k.low.at[2 + i])
                for i in range(2):
                    rows = pl.ds((layer ^ i) * ROWS, ROWS)
                    k.ready((named.out, i))
                    k.put(k.low.at[i], k.outer[named.layer_out].at[rows])
                    k.ready((named.grad, i))
                    if layer:
                        k.high[i] = k.low[2 + i].astype(F32)
                    elif i:
                        k.ready((named.grad, 2))
                        k.high[i] = k.low[2].astype(F32) + k.low[3].astype(F32)
                    k.put(k.high.at[i], k.outer[named.grad_in].at[rows])
                k.finish()

        k.saves = []

    given = {named.from_grad_in: grad_in}
    for name in (named.fwd0, named.mid1, named.end0, named.end1):
        given |= {named.own_ + name: packs[name], named.sent_ + name: sent[name]}
    made = {named.layer_out: ((2 * ROWS, D), BF16), named.grad_in: ((2 * ROWS, D), F32)}
    held = {named.low: ((4, ROWS, D), BF16), named.high: ((2, ROWS, D), F32)}
    return call(kernel, named.place_rows, given, made, held, after=after)


def swap(x):
    return lax.ppermute(x, "pipe", [(0, 1), (1, 0)])


def body(
    inputs,
    cotangent,
    lengths,
    proj_stack,
    gain_one,
    bias_one,
    w_qkv,
    w_out,
    gain_two,
    bias_two,
    w_up,
    w_down,
):
    count = lax.axis_size("dp")
    by_corners = count == 2 ** len(CORNERS) and D // count % 16 == 0
    core = lax.axis_index("pipe")
    gains = jnp.concatenate([gain_one, bias_one, gain_two, bias_two], axis=0)
    own = {named.gains: gains, named.w_qkv: w_qkv, named.w_out: w_out, named.w_up: w_up, named.w_down: w_down}
    sent = {k: swap(own[k]) for k in (named.gains, named.w_qkv, named.w_out)}
    later = lax.optimization_barrier((w_up, w_down, *sent.values()))
    sent |= {named.w_up: swap(later[0]), named.w_down: swap(later[1])}
    projection = jnp.swapaxes(proj_stack, 1, 2)

    def weights(*names):
        return {named.own_ + k: own[k] for k in names} | {named.sent_ + k: sent[k] for k in names}

    def room(*names):
        return {k: WEIGHTS[k] for k in names}

    wide, full = ((ROWS, D), BF16), ((ROWS, D), F32)
    up, proj, few = ((ROWS, FF), BF16), ((ROWS, 3 * D), BF16), ((8, D), F32)
    mask = {named.mask: ((ROWS, ROWS), F32)}
    kept = {k: ((ROWS, columns), dtype) for k, (columns, dtype) in ATTN_KEPT.items()}
    pack = {k: ((ROWS, columns), BF16) for k, columns in PACKS.items()}

    chunked = ((CHUNKS, ROWS, CHUNK), BF16)
    takes = [k for k in ATTN_KEPT if k != named.middle]
    attention_held = kept | room(named.gains, named.w_qkv, named.w_out, named.projection) | mask
    attention_held |= {named.hidden: wide, named.entry: wide, named.mixed: wide}
    ffn_held = room(named.gains, named.w_up, named.w_down) | {named.middle: full, named.total: full, named.slope: chunked}
    forward_held = ffn_held | {named.second: wide, named.layer_out: wide, named.activated: chunked}
    back_held = ffn_held | {named.grad_ffn: wide, named.grad_up: up, named.grad_middle: full}
    back_held |= {named.grad_attn: wide, named.vectors: few}
    last_held = room(named.gains, named.w_qkv, named.w_out, named.projection) | mask | {k: kept[k] for k in takes}
    last_held |= {named.hidden: wide, named.grad_middle: full, named.total: full, named.vectors: few, named.sums: few}
    last_held |= {named.grad_attn: wide, named.grad_proj: proj}
    places = {named.lengths: lengths, named.from_projection: projection}

    packs, sent_packs = {}, {}

    def run(kernel, name, given, made, held, packs_made=(), packs_changed=(), layer=0, after=()):
        given = given | {k: packs[k] for k in packs_changed}
        made = made | {k: pack[k] for k in packs_made}
        result = call(kernel, name, given, made, held, layer, list(packs_changed), after)
        packs.update({k: result.pop(k) for k in (*packs_made, *packs_changed)})
        return result

    first = run(
        attention_kernel,
        named.attention,
        places | {named.from_hidden: inputs} | weights(named.gains, named.w_qkv, named.w_out),
        kept,
        attention_held,
        [named.fwd0],
    )
    first |= run(
        ffn_kernel,
        named.feed_forward,
        {named.from_middle: first[named.middle]} | weights(named.gains, named.w_up, named.w_down),
        {named.slope: up},
        forward_held,
        [],
        [named.fwd0],
    )
    sent_packs[named.fwd0] = swap(packs[named.fwd0])
    second = {named.cosine: first[named.cosine], named.sine: first[named.sine]}
    second |= run(
        second_layer_kernel,
        named.second_layer,
        places
        | {named.from_fwd0: packs[named.fwd0], named.from_grad_ffn: cotangent}
        | {named.from_ + k: first[k] for k in (named.cosine, named.sine)}
        | weights(named.gains, named.w_qkv, named.w_out, named.w_up, named.w_down),
        {k: kept[k] for k in takes if k not in (named.cosine, named.sine)}
        | {named.grad_middle: full, named.vectors: few},
        attention_held | forward_held | back_held,
        [named.act1, named.mid1],
        layer=1,
    )
    sent_packs[named.act1] = swap(packs[named.act1])
    later, _ = lax.optimization_barrier((packs[named.mid1], sent_packs[named.act1]))
    sent_packs[named.mid1] = swap(later)

    def second_back(after):
        second.update(
            run(
                attention_back_kernel,
                named.second_layer_back,
                places
                | {named.from_fwd0: packs[named.fwd0]}
                | {named.from_ + k: second[k] for k in (*takes, named.grad_middle, named.vectors)}
                | weights(named.gains, named.w_qkv, named.w_out),
                {named.sums: few},
                last_held | {named.outgoing: wide},
                [named.end1],
                layer=1,
                after=after,
            )
        )
        sent_packs[named.end1] = swap(packs[named.end1])

    def first_ffn_back(after):
        first.update(
            run(
                ffn_back_kernel,
                named.first_layer_ffn_back,
                {named.from_end1: packs[named.end1]}
                | {named.from_ + k: first[k] for k in (named.slope, named.middle)}
                | weights(named.gains, named.w_up, named.w_down),
                {named.grad_middle: full, named.vectors: few},
                back_held,
                [named.mid0],
                after=after,
            )
        )
        sent_packs[named.mid0] = swap(packs[named.mid0])

    def first_attention_back(after):
        first.update(
            run(
                attention_back_kernel,
                named.first_layer_attention_back,
                places
                | {named.from_hidden: inputs}
                | {named.from_ + k: first[k] for k in (*takes, named.grad_middle, named.vectors)}
                | weights(named.gains, named.w_qkv, named.w_out),
                {named.sums: few, named.grad_in: full},
                last_held | {named.grad_in: full, named.grad_high: wide, named.grad_low: wide},
                [named.end0],
                after=after,
            )
        )
        sent_packs[named.end0] = swap(packs[named.end0])

    sums = {}

    def start(name, layer, after=()):
        if not by_corners:
            return []
        used = {PLACES[layer][x][0] for pair in USED[name] for x in pair if x in PLACES[layer]}
        if name == named.down and not layer:
            used.add(named.end1)
        given = {}
        for k in sorted(used):
            given |= {named.own_ + k: packs[k], named.sent_ + k: sent_packs[k]}
        if name == named.down and layer:
            given[named.grad_ffn] = cotangent
        if name == named.attn:
            given[named.from_vectors] = (first, second)[layer][named.sums]
        z_first = (name, layer) in ((named.attn, 1), (named.down, 0), (named.down, 1),)
        made = product(name, layer, given, after, z_first)
        sums[name, layer] = CornerSum(made, z_first)
        return [made[named.send]]

    def step(after, *jobs):
        if not by_corners:
            return []
        pairs = []
        for name, layer in jobs:
            last = layer == 0 and sums[name, layer].stage == len(CORNERS)
            pairs.append((sums[name, layer], sums[name, 1].total if last else None))
        return steps(pairs, after)

    down1, up1, attn1 = (named.down, 1), (named.up, 1), (named.attn, 1)
    down0, up0, attn0 = (named.down, 0), (named.up, 0), (named.attn, 0)
    done = start(named.down, 1)
    second_back([*done, sent_packs[named.fwd0]])
    done = [packs[named.end1]]
    done = start(named.up, 1, done)
    done = start(named.attn, 1, done)
    first_ffn_back(done)
    done = [packs[named.mid0]]
    done = step(done, down1)
    done = step(done, up1)
    done = start(named.up, 0, done)
    done = start(named.down, 0, done)
    done = step(done, down1, attn1)
    first_attention_back(done)
    done = [packs[named.end0]]
    done = step(done, up0, down1, up1)
    done = step(done, attn1)
    done = start(named.attn, 0, done)
    done = step(done, up0)
    done = step(done, attn1)
    done = step(done, down0, up1, down1)
    rows = place_rows(packs, sent_packs, first[named.grad_in], done)
    done = [rows[named.layer_out]]
    done = step(done, attn0)
    done = step(done, up0)
    done = step(done, down0)
    done = step(done, attn0)
    done = step(done, attn1)
    done = step(done, down0, up1)
    done = step(done, attn0)
    done = step(done, up0)
    done = step(done, down0)
    done = step(done, attn0)

    def by_layer(first, second):
        return jnp.where(core == 0, first, second)

    if by_corners:
        shard = D // count
        grad_w_down, grad_w_up, grad_w_out, grad_w_qkv, *vectors = assemble(
            [sums[name, 0].total for name in (named.down, named.up, named.attn)],
            named.gather,
            [
                (0, 0, (FF // count, D)),
                (1, 0, (shard, FF)),
                (1, FF // 2, (shard, D)),
                (2, 0, (shard, 3 * D)),
                (2, None, (1, shard)),
            ],
            done,
        )
    else:

        def rows_of(layer, name):
            name, at, width = PLACES[layer][name]
            return [x[name][:, at : at + width] for x in (packs, sent_packs)]

        def grads_of(layer):
            if layer:
                return by_layer(cotangent[:ROWS], cotangent[ROWS:]), by_layer(
                    cotangent[ROWS:], cotangent[:ROWS]
                )
            return rows_of(1, named.outgoing)

        def one(lhs, rhs):
            parts = [
                sum(dot_tn(a, b) for a, b in zip(lhs(layer), rhs(layer))) for layer in range(2)
            ]
            return lax.psum_scatter(by_layer(*parts), "dp", scatter_dimension=0, tiled=True)

        def both(name):
            return lambda layer: rows_of(layer, name)

        grad_w_down = one(both(named.activated), grads_of)
        grad_w_up = one(both(named.second), both(named.grad_up))
        grad_w_qkv = one(both(named.entry), both(named.grad_proj))
        grad_w_out = one(both(named.mixed), both(named.grad_attn))
        vectors = by_layer(*[x[named.sums] + swap(x[named.sums]) for x in (first, second)])
        vectors = lax.psum_scatter(vectors, "dp", scatter_dimension=1, tiled=True)
        vectors = [vectors[i][None] for i in range(4)]

    return (
        rows[named.layer_out][None],
        rows[named.grad_in][None],
        vectors[0],
        vectors[1],
        grad_w_qkv[None],
        grad_w_out[None],
        vectors[2],
        vectors[3],
        grad_w_up[None],
        grad_w_down[None],
    )


def solution(mesh):
    placed = (
        P("dp", None),
        P("dp", None),
        P("dp", None),
        P(),
        P("pipe", None),
        P("pipe", None),
        P("pipe", None, None),
        P("pipe", None, None),
        P("pipe", None),
        P("pipe", None),
        P("pipe", None, None),
        P("pipe", None, None),
    )
    return jax.shard_map(
        body,
        mesh=mesh,
        in_specs=placed,
        out_specs=(
            P("pipe", "dp", None),
            P("pipe", "dp", None),
            P("pipe", "dp"),
            P("pipe", "dp"),
            P("pipe", "dp", None),
            P("pipe", "dp", None),
            P("pipe", "dp"),
            P("pipe", "dp"),
            P("pipe", "dp", None),
            P("pipe", "dp", None),
        ),
        check_vma=False,
    )
```

```python
import math
import types

import jax
import jax.numpy as jnp
from jax import lax
from jax.experimental import pallas as pl
from jax.experimental.pallas import tpu as pltpu
from jax.sharding import PartitionSpec as P

class Names:
    def __getattr__(self, name):
        return name


named = Names()

D = 768
HEADS = 12
HEAD = 64
FEAT = 32
FF = 3072
ROWS = 256
MOLS = 3
NSTACK = 4
STEP = 7
EPSILON = 1e-05

PACK = 4
GROUPS = HEADS // PACK
WIDE = PACK * HEAD
THIN = PACK * FEAT
PAIR = 2 * HEAD
CHUNK = 1024
CHUNKS = FF // CHUNK
SCALE = HEAD ** -0.25
MIB = 1024 * 1024
LIMIT = 40 * MIB

F32 = jnp.float32
BF16 = jnp.bfloat16

KEPT_WIDE = 3 * WIDE + 2 * THIN
TURNED_Q, TURNED_K, VALUE = (slice(i * WIDE, (i + 1) * WIDE) for i in range(3))
PHI_Q, PHI_K = (slice(3 * WIDE + i * THIN, 3 * WIDE + (i + 1) * THIN) for i in range(2))
ATTN_KEPT = {
    named.heads: (GROUPS * KEPT_WIDE, BF16),
    named.middle: (D, F32),
    named.cosine: (PAIR, F32),
    named.sine: (PAIR, F32),
}
WEIGHTS = {
    named.w_qkv: ((D, 3 * D), BF16),
    named.w_out: ((D, D), BF16),
    named.w_up: ((CHUNKS, D, CHUNK), BF16),
    named.w_down: ((CHUNKS, CHUNK, D), BF16),
    named.gains: ((4, D), F32),
    named.projection: ((FEAT, HEAD), F32),
}
PLACES = (
    {
        named.entry: (named.fwd0, 0, D),
        named.mixed: (named.fwd0, D, D),
        named.second: (named.fwd0, 2 * D, D),
        named.layer_out: (named.fwd0, 3 * D, D),
        named.activated: (named.fwd0, 4 * D, FF),
        named.grad_attn: (named.mid0, 0, D),
        named.grad_up: (named.mid0, D, FF),
        named.grad_high: (named.end0, 0, D),
        named.grad_low: (named.end0, D, D),
        named.grad_proj: (named.end0, 2 * D, 3 * D),
    },
    {
        named.activated: (named.act1, 0, FF),
        named.second: (named.mid1, 0, D),
        named.mixed: (named.mid1, D, D),
        named.entry: (named.mid1, 2 * D, D),
        named.layer_out: (named.mid1, 3 * D, D),
        named.grad_attn: (named.mid1, 4 * D, D),
        named.grad_up: (named.mid1, 5 * D, FF),
        named.outgoing: (named.end1, 0, D),
        named.grad_proj: (named.end1, D, 3 * D),
    },
)
PACKS = {named.fwd0: 4 * D + FF, named.act1: FF, named.mid1: 5 * D + FF, named.end1: 4 * D, named.mid0: D + FF, named.end0: 5 * D}


class Copies:
    def __init__(self, semaphores):
        self.semaphores = semaphores
        self.count = 0

    def start(self, source, target):
        copy = pltpu.make_async_copy(source, target, self.semaphores.at[self.count])
        self.count += 1
        copy.start()
        return copy

    def either(self, condition, source, other, target):
        semaphore = self.semaphores.at[self.count]
        self.count += 1
        copy = pltpu.make_async_copy(source, target, semaphore)

        @pl.when(condition)
        def _():
            copy.start()

        @pl.when(jnp.logical_not(condition))
        def _():
            pltpu.make_async_copy(other, target, semaphore).start()

        return copy


class Kernel:
    def __init__(self, outer, held, semaphores, layer):
        self.outer = outer
        self.held = held
        self.copies = Copies(semaphores)
        self.loads = {}
        self.saves = []
        self.core = lax.axis_index("pipe")
        self.layer = layer
        self.present = set()

    def __getattr__(self, name):
        return self.held[name]

    def new(self, name):
        return name not in self.loads and name not in self.present

    def load(self, *names):
        for name in names:
            if self.new(name):
                self.loads[name] = [self.copies.start(self.outer[named.from_ + name], self.held[name])]

    def load_from(self, name, source, target=None):
        if self.new(name):
            target = self.held[name] if target is None else target
            self.loads[name] = [self.copies.start(source, target)]

    def load_slope(self):
        for c in range(CHUNKS):
            if self.new((named.slope, c)):
                source = self.outer[named.from_slope].at[:, pl.ds(c * CHUNK, CHUNK)]
                self.loads[named.slope, c] = [self.copies.start(source, self.held[named.slope].at[c])]

    def load_weight(self, name, chunk=None):
        key = name if chunk is None else (name, chunk)
        if not self.new(key):
            return
        target = self.held[name]
        if chunk is not None:
            target = target.at[chunk]
        at = pl.ds((chunk or 0) * CHUNK, CHUNK)

        def part(source):
            if name == named.w_up:
                return source.at[0, :, at]
            if name == named.w_down:
                return source.at[0, at]
            return source if name == named.gains else source.at[0]

        self.loads[key] = [
            self.copies.either(
                self.core == self.layer,
                part(self.outer[named.own_ + name]),
                part(self.outer[named.sent_ + name]),
                target,
            )
        ]

    def load_hidden(self):
        if self.layer == 0:
            rows = pl.ds(pl.multiple_of(self.core * ROWS, ROWS), ROWS)
            source = self.outer[named.from_hidden].at[rows]
        else:
            source = self.place(named.layer_out, 0, named.from_)
        self.load_from(named.hidden, source)

    def load_projection(self):
        self.load_from(named.projection, self.outer[named.from_projection].at[STEP % NSTACK])

    def load_grad(self):
        if self.layer:
            rows = pl.ds(pl.multiple_of(self.core * ROWS, ROWS), ROWS)
            source = self.outer[named.from_grad_ffn].at[rows]
        else:
            source = self.place(named.outgoing, 1, named.from_)
        self.load_from(named.grad_ffn, source)

    def ready(self, *names):
        for name in names:
            for copy in self.loads.pop(name, ()):
                copy.wait()
            self.present.add(name)

    def save(self, *names):
        for name in names:
            if name in self.outer:
                self.put(self.held[name], self.outer[name])

    def pack(self, name):
        self.put(self.held[name], self.place(name, self.layer))

    def place(self, name, layer, prefix=""):
        pack, first, width = PLACES[layer][name]
        return self.outer[prefix + pack].at[:, pl.ds(first, width)]

    def put(self, source, target):
        self.saves.append(self.copies.start(source, target))

    def finish(self):
        assert not self.loads
        for copy in self.saves:
            copy.wait()


def call(kernel, name, given, made, held, layer=0, changed=(), after=()):
    anywhere = pl.BlockSpec(memory_space=pl.ANY)
    names, places = list(given), list(held)
    outs = list(changed) + list(made)
    shapes = [jax.ShapeDtypeStruct(given[key].shape, given[key].dtype) for key in changed]
    shapes += [jax.ShapeDtypeStruct(*x) for x in made.values()]

    def run(*refs):
        outer = dict(zip(names, refs))
        refs = refs[len(names) + len(after) :]
        outer |= dict(zip(outs, refs))
        refs = refs[len(outs) :]
        k = Kernel(outer, dict(zip(places, refs)), refs[-1], layer)
        kernel(k)
        k.finish()

    results = pl.pallas_call(
        run,
        out_shape=[pltpu.HBM(x.shape, x.dtype) for x in shapes],
        in_specs=[
            pl.BlockSpec(memory_space=pltpu.SMEM) if key == named.lengths else anywhere for key in names
        ]
        + [anywhere] * len(after),
        out_specs=[anywhere] * len(shapes),
        input_output_aliases={names.index(key): i for i, key in enumerate(changed)},
        scratch_shapes=[pltpu.VMEM(*x) for x in held.values()]
        + [pltpu.SemaphoreType.DMA((80,))],
        compiler_params=pltpu.CompilerParams(vmem_limit_bytes=LIMIT),
        cost_estimate=pl.CostEstimate(
            flops=10**12, bytes_accessed=1000, transcendentals=0
        ),
        name=name,
    )(
        *[
            x
            if key == named.lengths or key.startswith(named.sent_)
            else pltpu.with_memory_space_constraint(x, pltpu.HBM)
            for key, x in given.items()
        ],
        *[pltpu.with_memory_space_constraint(x, pltpu.HBM) for x in after],
    )
    return dict(zip(outs, results))


def dot(a, b):
    return jnp.dot(a, b, preferred_element_type=F32)


def dot_nt(a, b):
    return lax.dot_general(a, b, (((1,), (1,)), ((), ())), preferred_element_type=F32)


def dot_tn(a, b):
    return lax.dot_general(a, b, (((0,), (0,)), ((), ())), preferred_element_type=F32)


def beside(*parts):
    return jnp.concatenate(parts, axis=1)


def below(*parts):
    return jnp.concatenate(parts, axis=0)


def normalize(hidden):
    average = jnp.mean(hidden, axis=-1, keepdims=True)
    centred = hidden - average
    inverse = lax.rsqrt(jnp.mean(centred * centred, axis=-1, keepdims=True) + EPSILON)
    return centred * inverse, inverse


def normalize_back(grad_normed, normed, inverse):
    return inverse * (
        grad_normed
        - jnp.mean(grad_normed, axis=-1, keepdims=True)
        - normed * jnp.mean(grad_normed * normed, axis=-1, keepdims=True)
    )


def iota(shape, axis):
    return lax.broadcasted_iota(jnp.int32, shape, axis)


def molecules(lengths, block, row):
    which = jnp.full(row.shape, MOLS, jnp.int32)
    first = jnp.zeros(row.shape, jnp.int32)
    opening = jnp.int32(0)
    for s in range(MOLS):
        closing = opening + lengths[block, s]
        inside = (row >= opening) & (row < closing)
        which = jnp.where(inside, s, which)
        first = jnp.where(inside, opening, first)
        opening = closing
    return which, first


def together(lengths, block):
    down, _ = molecules(lengths, block, iota((ROWS, 128), 0))
    along, _ = molecules(lengths, block, iota((1, ROWS), 1))
    halves = [
        jnp.where((down == along[:, at : at + 128]) & (down < MOLS), 1.0, 0.0)
        for at in range(0, ROWS, 128)
    ]
    return beside(*halves)


def tables(lengths, block):
    row = iota((ROWS, PAIR), 0)
    _, first = molecules(lengths, block, row)
    lane = iota((1, PAIR), 1)
    index = (lane & (HEAD // 2 - 1)).astype(F32)
    angles = (row - first).astype(F32) * jnp.exp(index * (-2.0 * math.log(10000.0) / HEAD))
    sine = jnp.sin(angles)
    return jnp.cos(angles), jnp.where(lane & (HEAD // 2) == 0, -sine, sine)


def swap_halves(x):
    half = HEAD // 2
    width = x.shape[1]
    low = iota((1, width), 1) & half == 0
    return jnp.where(low, pltpu.roll(x, width - half, 1), pltpu.roll(x, half, 1))


def block_diagonal(projection):
    tiled = below(*[beside(*[projection] * PACK)] * PACK)
    same = iota((THIN, WIDE), 0) >> 5 == iota((THIN, WIDE), 1) >> 6
    return jnp.where(same, tiled, 0.0), same.astype(F32)


def two_parts(x):
    high = x.astype(BF16)
    return high, (x - high.astype(F32)).astype(BF16)


def features(turned, proj_both, proj_high, norm_part):
    scaled = turned * SCALE
    high, low = two_parts(scaled)
    square_high, square_low = two_parts(scaled * scaled)
    both = dot_nt(high, proj_both)
    rest = dot_nt(beside(low, square_high, square_low), beside(proj_high, norm_part, norm_part))
    return jnp.exp(both[:, :THIN] + both[:, THIN:] + rest) * (1.0 / math.sqrt(FEAT))


def only(x, head, width):
    lane = iota((1, x.shape[1]), 1)
    return jnp.where((lane >= head * width) & (lane < (head + 1) * width), x, jnp.zeros_like(x))


def gelu_and_slope(u):
    bell = jnp.exp(-0.5 * u * u)
    t = 1.0 / (1.0 + jnp.abs(u) * (0.3275911 * math.sqrt(0.5)))
    tail = 0.5 * 1.061405429
    for c in (-1.453152027, 1.421413741, -0.284496736, 0.254829592):
        tail = tail * t + 0.5 * c
    tail = tail * t * bell
    phi = jnp.where(u >= 0.0, 1.0 - tail, tail)
    return u * phi, phi + u * bell * (1.0 / math.sqrt(2.0 * math.pi))


def attention_kernel(k):
    k.load_weight(named.gains)
    k.load_hidden()
    k.load_projection()
    k.load_weight(named.w_qkv)
    k.load_weight(named.w_out)
    lengths = k.outer[named.lengths]
    if k.layer == 0:
        k.cosine[...], k.sine[...] = tables(lengths, k.core)
        k.save(named.cosine, named.sine)
    else:
        k.load(named.cosine, named.sine)
    k.mask[...] = together(lengths, k.core)
    k.ready(named.projection)
    proj_block, own = block_diagonal(k.projection[...])
    proj_high, proj_low = two_parts(proj_block)
    proj_both = below(proj_high, proj_low)
    norm_part = (-0.5 * own).astype(BF16)
    k.ready(named.hidden, named.gains)
    normed, _ = normalize(k.hidden[...].astype(F32))
    k.entry[...] = (normed * k.gains[0:1] + k.gains[1:2]).astype(BF16)
    k.pack(named.entry)
    if k.layer:
        k.ready(named.cosine, named.sine)
    k.ready(named.w_qkv)
    for g in range(GROUPS):
        cols = slice(g * WIDE, (g + 1) * WIDE)
        thin = slice(g * THIN, (g + 1) * THIN)
        entry = k.entry[...]
        cosine = beside(k.cosine[...], k.cosine[...])
        sine = beside(k.sine[...], k.sine[...])
        query = dot(entry, k.w_qkv[:, g * WIDE : (g + 1) * WIDE])
        key = dot(entry, k.w_qkv[:, D + g * WIDE : D + (g + 1) * WIDE])
        value = dot(entry, k.w_qkv[:, 2 * D + g * WIDE : 2 * D + (g + 1) * WIDE])
        query = query * cosine + swap_halves(query) * sine
        key = key * cosine + swap_halves(key) * sine
        phi_q = features(query, proj_both, proj_high, norm_part)
        phi_k = features(key, proj_both, proj_high, norm_part)
        k.heads[:, g * KEPT_WIDE : (g + 1) * KEPT_WIDE] = beside(
            query, key, value, phi_q, phi_k
        ).astype(BF16)
        q_high, q_low = two_parts(phi_q)
        k_high, k_low = two_parts(phi_k)
        v_high, v_low = two_parts(value)
        scores = dot_nt(
            below(*[beside(only(q_high, h, FEAT), only(q_low, h, FEAT)) for h in range(PACK)]),
            beside(k_high, k_high),
        ) + dot_nt(below(*[only(q_high, h, FEAT) for h in range(PACK)]), k_low)
        mask = k.mask[...]
        inside = jnp.sum(mask, axis=1, keepdims=True) > 0.5
        for pair in range(PACK // 2):
            at = slice(pair * PAIR, (pair + 1) * PAIR)
            lanes = slice(g * WIDE + pair * PAIR, g * WIDE + (pair + 1) * PAIR)
            parts, inverses = [], []
            for h in (2 * pair, 2 * pair + 1):
                score = scores[h * ROWS : (h + 1) * ROWS] * mask
                den = jnp.sum(score, axis=1, keepdims=True)
                inverses.append(jnp.where(inside, 1.0 / jnp.where(inside, den, 1.0), 0.0))
                parts.append(two_parts(score))
            high = below(parts[0][0], parts[1][0])
            low = below(parts[0][1], parts[1][1])
            both = dot(high, beside(v_high[:, at], v_low[:, at]))
            summed = both[:, :PAIR] + both[:, PAIR:] + dot(low, v_high[:, at])
            left = iota((1, PAIR), 1) < HEAD
            inverse = jnp.where(left, inverses[0], inverses[1])
            mixed = jnp.where(left, summed[:ROWS], summed[ROWS:]) * inverse
            k.mixed[:, lanes] = mixed.astype(BF16)
    k.save(named.heads)
    k.pack(named.mixed)
    k.ready(named.w_out)
    k.middle[...] = k.hidden[...].astype(F32) + dot(k.mixed[...], k.w_out[...])
    k.present.add(named.middle)
    k.save(named.middle)


def ffn_kernel(k):
    k.load_weight(named.gains)
    k.load(named.middle)
    for c in range(CHUNKS):
        k.load_weight(named.w_up, c)
        k.load_weight(named.w_down, c)
    k.ready(named.middle, named.gains)
    normed, _ = normalize(k.middle[...])
    k.second[...] = (normed * k.gains[2:3] + k.gains[3:4]).astype(BF16)
    k.pack(named.second)
    k.total[...] = k.middle[...]
    if k.layer:
        for c in range(CHUNKS):
            k.ready((named.w_up, c), (named.w_down, c))

    def leave(c):
        at = pl.ds(c * CHUNK, CHUNK)
        k.put(k.activated.at[c], k.place(named.activated, k.layer).at[:, at])
        if named.slope in k.outer:
            k.put(k.slope.at[c], k.outer[named.slope].at[:, at])

    for c in range(CHUNKS):
        if not k.layer:
            k.ready((named.w_up, c), (named.w_down, c))
        activated, slope = gelu_and_slope(dot(k.second[...], k.w_up[c]))
        k.activated[c] = activated.astype(BF16)
        k.slope[c] = slope.astype(BF16)
        k.present.add((named.slope, c))
        if not k.layer:
            leave(c)
        k.total[...] += dot(k.activated[c], k.w_down[c])
    if k.layer:
        for c in range(CHUNKS):
            leave(c)
    k.layer_out[...] = k.total[...].astype(BF16)
    k.pack(named.layer_out)


def ffn_back_kernel(k):
    k.load_grad()
    k.load_slope()
    for c in range(CHUNKS):
        k.load_weight(named.w_down, c)
        k.load_weight(named.w_up, c)
    k.load(named.middle)
    k.load_weight(named.gains)
    k.vectors[...] = jnp.zeros_like(k.vectors)
    k.ready(named.grad_ffn)
    k.ready((named.w_down, 0))
    grad_act = dot_nt(k.grad_ffn[...], k.w_down[0])
    for c in range(CHUNKS):
        at = slice(c * CHUNK, (c + 1) * CHUNK)
        if c + 1 < CHUNKS:
            k.ready((named.w_down, c + 1))
            upcoming = dot_nt(k.grad_ffn[...], k.w_down[c + 1])
        k.ready((named.slope, c), (named.w_up, c))
        k.grad_up[:, at] = (grad_act * k.slope[c].astype(F32)).astype(BF16)
        piece = dot_nt(k.grad_up[:, at], k.w_up[c])
        if c == 0:
            k.total[...] = piece
        else:
            k.total[...] += piece
        if c + 1 < CHUNKS:
            grad_act = upcoming
    k.pack(named.grad_up)
    k.ready(named.middle, named.gains)
    normed, inverse = normalize(k.middle[...])
    grad = k.total[...]
    k.vectors[2:3] = jnp.sum(grad * normed, axis=0, keepdims=True)
    k.vectors[3:4] = jnp.sum(grad, axis=0, keepdims=True)
    k.save(named.vectors)
    k.grad_middle[...] = k.grad_ffn[...].astype(F32) + normalize_back(
        grad * k.gains[2:3], normed, inverse
    )
    k.grad_attn[...] = k.grad_middle[...].astype(BF16)
    k.pack(named.grad_attn)
    k.present |= {named.grad_middle, named.vectors, named.grad_attn}
    k.save(named.grad_middle)


def attention_back_kernel(k):
    k.load(named.grad_middle)
    k.load_weight(named.w_out)
    k.load_projection()
    k.load(named.cosine, named.sine)
    for g in range(GROUPS):
        at = pl.ds(g * KEPT_WIDE, KEPT_WIDE)
        k.load_from((named.heads, g), k.outer[named.from_heads].at[:, at], k.heads.at[:, at])
    k.load_weight(named.w_qkv)
    k.load_hidden()
    k.load_weight(named.gains)
    k.load(named.vectors)
    k.mask[...] = together(k.outer[named.lengths], k.core)
    k.ready(named.projection, named.grad_middle, named.w_out, named.cosine, named.sine)
    if named.grad_attn not in k.present:
        k.grad_attn[...] = k.grad_middle[...].astype(BF16)
    proj_block, own = block_diagonal(k.projection[...])
    back_part = beside(proj_block, own).astype(BF16)
    back_part = below(back_part, back_part)
    for g in range(GROUPS):
        cols = slice(g * WIDE, (g + 1) * WIDE)
        thin = slice(g * THIN, (g + 1) * THIN)
        cosine = beside(k.cosine[...], k.cosine[...])
        sine = beside(k.sine[...], k.sine[...])
        mask = k.mask[...]
        inside = jnp.sum(mask, axis=1, keepdims=True) > 0.5
        grad_mixed = dot_nt(k.grad_attn[...], k.w_out[cols, :]).astype(BF16)
        if g == 0:
            k.ready(*[(named.heads, i) for i in range(GROUPS)])
        heads = k.heads[:, g * KEPT_WIDE : (g + 1) * KEPT_WIDE]
        value = heads[:, VALUE]
        phi_q, k_high = heads[:, PHI_Q], heads[:, PHI_K]
        q_all = [only(phi_q, h, FEAT) for h in range(PACK)]
        k_all = [only(k_high, h, FEAT) for h in range(PACK)]
        grad_scores, grad_value = [], []
        for pair in range(PACK // 2):
            at = slice(pair * PAIR, (pair + 1) * PAIR)
            own_grad = [only(grad_mixed[:, at], i, HEAD) for i in range(2)]
            score = dot_nt(below(*q_all[2 * pair : 2 * pair + 2]), k_high)
            grad_share = dot_nt(below(*own_grad), value[:, at])
            shares = []
            for i in range(2):
                one = score[i * ROWS : (i + 1) * ROWS] * mask
                den = jnp.sum(one, axis=1, keepdims=True)
                inverse = jnp.where(inside, 1.0 / jnp.where(inside, den, 1.0), 0.0)
                share = one * inverse
                grad = grad_share[i * ROWS : (i + 1) * ROWS]
                centre = jnp.sum(share * grad, axis=1, keepdims=True)
                grad_scores.append((((grad - centre) * inverse) * mask).astype(BF16))
                shares.append(share.astype(BF16))
            grad_value.append(dot_tn(below(*shares), below(*own_grad)))
        grad_phi_q = dot(beside(*grad_scores), below(*k_all))
        grad_phi_k = dot_tn(below(*grad_scores), below(*q_all))

        def features_back(grad_phi, phi, turned):
            high, low = two_parts(grad_phi * phi.astype(F32))
            back = dot(beside(high, low), back_part)
            grad = (back[:, :WIDE] - turned.astype(F32) * SCALE * back[:, WIDE:]) * SCALE
            return (grad * cosine + swap_halves(grad * sine)).astype(BF16)

        grad_query = features_back(grad_phi_q, phi_q, heads[:, TURNED_Q])
        grad_key = features_back(grad_phi_k, k_high, heads[:, TURNED_K])
        k.grad_proj[:, g * WIDE : (g + 1) * WIDE] = grad_query
        k.grad_proj[:, D + g * WIDE : D + (g + 1) * WIDE] = grad_key
        k.grad_proj[:, 2 * D + g * WIDE : 2 * D + (g + 1) * WIDE] = beside(*grad_value).astype(BF16)
    k.pack(named.grad_proj)
    k.ready(named.w_qkv)
    for i in range(3):
        at = slice(i * D, (i + 1) * D)
        piece = dot_nt(k.grad_proj[:, at], k.w_qkv[:, at])
        if i == 0:
            k.total[...] = piece
        else:
            k.total[...] += piece
    k.ready(named.hidden, named.gains, named.vectors)
    normed, inverse = normalize(k.hidden[...].astype(F32))
    grad = k.total[...]
    k.vectors[0:1] = jnp.sum(grad * normed, axis=0, keepdims=True)
    k.vectors[1:2] = jnp.sum(grad, axis=0, keepdims=True)
    k.held[named.sums][...] = k.vectors[...]
    k.save(named.sums)
    grad_hidden = k.grad_middle[...] + normalize_back(grad * k.gains[0:1], normed, inverse)
    if k.layer:
        k.outgoing[...] = grad_hidden.astype(BF16)
        k.pack(named.outgoing)
    else:
        k.grad_in[...] = grad_hidden
        k.save(named.grad_in)
        k.grad_high[...], k.grad_low[...] = two_parts(grad_hidden)
        k.pack(named.grad_high)
        k.pack(named.grad_low)


def second_layer_kernel(k):
    k.load_weight(named.gains)
    k.load_hidden()
    k.load_projection()
    k.load(named.cosine, named.sine)
    k.load_weight(named.w_qkv)
    k.load_weight(named.w_out)
    for c in range(CHUNKS):
        k.load_weight(named.w_up, c)
        k.load_weight(named.w_down, c)
    k.load_grad()
    attention_kernel(k)
    ffn_kernel(k)
    ffn_back_kernel(k)


CORNERS = (1, 2, 4, 8)
VECTORS = -1
DOWN = (named.activated, named.grad_ffn)
PLANS = {
    named.down: (((DOWN, 0, 384),), ((DOWN, 384, 384),)),
    named.up: (
        (
            ((named.second, named.grad_up), 0, 768),
            ((named.second, named.grad_up), 768, 768),
            ((named.mixed, named.grad_attn), 0, 384),
        ),
        (
            ((named.second, named.grad_up), 1536, 768),
            ((named.second, named.grad_up), 2304, 768),
            ((named.mixed, named.grad_attn), 384, 384),
        ),
    ),
    named.attn: (
        (((named.entry, named.grad_proj), 0, 768), ((named.entry, named.grad_proj), 768, 384), (VECTORS, 0, 128)),
        (((named.entry, named.grad_proj), 1152, 768), ((named.entry, named.grad_proj), 1920, 384), (VECTORS, 0, 128)),
    ),
}


USED = {
    name: {tile[0] for tiles in plan for tile in tiles if tile[0] != VECTORS}
    for name, plan in PLANS.items()
}


def orders(z_first):
    x, y, near, far = CORNERS
    return ((near, x, y, far), (near, y, x, far)) if z_first else ((x, y, near, far), (y, x, near, far))


def product_kernel(k, name, z_first):
    me = lax.axis_index("dp")
    rows = k.out.shape[0]
    shard = rows // lax.axis_size("dp")

    def fetch(name, target, first, width, at):
        if name == named.grad_ffn and k.layer:
            sources = [
                k.outer[named.grad_ffn].at[pl.ds(pl.multiple_of((k.core ^ i) * ROWS, ROWS), ROWS)]
                for i in range(2)
            ]
        elif name == named.grad_ffn:
            sources = [k.place(named.outgoing, 1, x) for x in (named.own_, named.sent_)]
        else:
            sources = [k.place(name, k.layer, x) for x in (named.own_, named.sent_)]
        return [
            k.copies.start(
                x.at[:, pl.ds(first, width)], target.at[pl.ds(i * ROWS, ROWS), pl.ds(at, width)]
            )
            for i, x in enumerate(sources)
        ]

    def leave(group, at, width):
        order = orders(z_first)[group]
        for slot in range(16):
            step = sum(bit for i, bit in enumerate(order) if slot & (8 >> i) == 0)
            where = me ^ step
            half = k.outer[named.send if slot < 8 else named.keep]
            target = half.at[pl.ds((slot & 7) * shard, shard), pl.ds(at, width)]
            k.put(k.out.at[pl.ds(pl.multiple_of(where * shard, 16), shard), pl.ds(at, width)], target)

    for group, tiles in enumerate(PLANS[name]):

        @pl.when(k.core == group)
        def _():
            k.loads, k.saves, k.copies.count, k.present = {}, [], 0, set()
            if name == named.down:
                ((left, right), first, width) = tiles[0]
                k.loads[named.right] = fetch(right, k.right, first, width, 0)
                for c in range(0, rows, D):
                    k.loads[named.left, c] = fetch(left, k.left_activated, c, D, c)
                k.ready(named.right)
                for c in range(0, rows, D):
                    k.ready((named.left, c))
                    k.out[c : c + D] = dot_tn(k.left_activated[:, c : c + D], k.right[...]).astype(BF16)
                leave(group, 0, width)
            else:
                at = 0
                for i, (names, first, width) in enumerate(tiles):
                    if names == VECTORS:
                        k.load(named.vectors)
                    else:
                        left = names[0]
                        if left not in k.loads:
                            k.loads[left] = fetch(left, k.held[named.left_ + left], 0, D, 0)
                        k.loads[named.right, i] = fetch(names[1], k.right, first, width, at)
                    at += width
                at = 0
                for i, (names, first, width) in enumerate(tiles):
                    if names == VECTORS:
                        k.ready(named.vectors)
                        total = below(k.vectors[...], jnp.zeros((width - 8, D), F32))
                        got = total.T
                    else:
                        k.ready(names[0], (named.right, i))
                        got = dot_tn(k.held[named.left_ + names[0]][...], k.right[:, at : at + width])
                    k.out[:, at : at + width] = got.astype(BF16)
                    leave(group, at, width)
                    at += width
            k.finish()

    k.loads, k.saves = {}, []


def product(name, layer, given, after, z_first):
    plan = PLANS[name]
    lefts = sorted({tile[0][0] for tiles in plan for tile in tiles if tile[0] != VECTORS})
    widths = {x: PLACES[1][x][2] for x in lefts}
    rows = widths[lefts[0]]
    columns = sum(tile[2] for tile in plan[0])
    held = {named.left_ + x: ((2 * ROWS, w), BF16) for x, w in widths.items()}
    held |= {named.right: ((2 * ROWS, columns), BF16), named.out: ((rows, columns), BF16)}
    if name == named.attn:
        held[named.vectors] = ((8, D), F32)
    made = {kind: ((rows // 2, columns), BF16) for kind in (named.send, named.keep)}
    return call(
        lambda k: product_kernel(k, name, z_first),
        named.product_ + name,
        given,
        made,
        held,
        layer=layer,
        after=after,
    )


def small_call(kernel, name, given, made, after, last=False):
    inside = pl.BlockSpec(memory_space=pltpu.VMEM)
    anywhere = pl.BlockSpec(memory_space=pl.ANY)

    def run(*refs):
        kernel(refs[: len(given)], refs[len(given) + len(after) :])

    return pl.pallas_call(
        run,
        out_shape=[pltpu.HBM(*x) if last else jax.ShapeDtypeStruct(*x) for x in made],
        in_specs=[inside] * len(given) + [anywhere] * len(after),
        out_specs=[inside] * len(made),
        compiler_params=pltpu.CompilerParams(vmem_limit_bytes=24 * MIB),
        cost_estimate=pl.CostEstimate(flops=10**12, bytes_accessed=1000, transcendentals=0),
        name=name,
    )(*given, *[pltpu.with_memory_space_constraint(x, pltpu.HBM) for x in after])


class CornerSum:
    def __init__(self, made, z_first):
        self.orders = orders(z_first)
        self.keep = made[named.keep]
        self.stage = 0
        self.hop(made[named.send])

    def hop(self, x):
        count = lax.axis_size("dp")
        pairs = []
        for core in range(2):
            bit = self.orders[core][self.stage]
            pairs += [(core * count + i, core * count + (i ^ bit)) for i in range(count)]
        self.arriving = lax.ppermute(x, ("pipe", "dp"), pairs)
        self.stage += 1


def steps(jobs, after):
    given, made = [], []
    for job, other in jobs:
        given += [job.keep, job.arriving]
        rows, columns = job.keep.shape
        if job.stage < len(CORNERS):
            made += [((rows // 2, columns), BF16), ((rows // 2, columns), F32)]
        elif other is None:
            made += [((rows, columns), F32)]
        else:
            given.append(other)
            made += [((rows, columns), F32)] * 2

    def kernel(given, made):
        given, made = list(given), list(made)
        for job, other in jobs:
            keep, arrived = given.pop(0), given.pop(0)
            half = keep.shape[0] // 2
            if job.stage < len(CORNERS):
                made.pop(0)[...] = (
                    keep[:half].astype(F32) + arrived[:half].astype(F32)
                ).astype(BF16)
                made.pop(0)[...] = keep[half:].astype(F32) + arrived[half:].astype(F32)
                continue
            total = keep[...] + arrived[...].astype(F32)
            if other is None:
                made.pop(0)[...] = total
                continue
            second = given.pop(0)[...]
            core = lax.axis_index("pipe")
            made.pop(0)[...] = jnp.where(core == 0, total, second)
            made.pop(0)[...] = jnp.where(core == 0, second, total)

    ending = any(other is not None for _, other in jobs)
    made = list(small_call(kernel, named.steps, given, made, after, ending))
    done = [made[0]]
    for job, other in jobs:
        if job.stage < len(CORNERS):
            sent, job.keep = made.pop(0), made.pop(0)
            job.hop(sent)
        elif other is None:
            job.total = made.pop(0)
        else:
            job.total = (made.pop(0), swap(made.pop(0)))
    return done


def assemble(parts, name, shapes, after):
    def kernel(given, made):
        core = lax.axis_index("pipe")
        for out, (i, first, (rows, columns)) in zip(made, shapes):
            stayed, came = given[2 * i : 2 * i + 2]
            if first is None:
                total = stayed[:, -PAIR:] + came[:, -PAIR:]
                total = below(total, jnp.zeros((PAIR - total.shape[0], PAIR), F32)).T
                for j in range(4):
                    made[len(shapes) - 1 + j][...] = total[j : j + 1, :columns]
                break
            half = columns // 2
            at = slice(first, first + half)

            @pl.when(core == 0)
            def _():
                out[:, :half] = stayed[:, at]
                out[:, half:] = came[:, at]

            @pl.when(core != 0)
            def _():
                out[:, :half] = came[:, at]
                out[:, half:] = stayed[:, at]

    made = []
    for _, first, shape in shapes:
        made += [(shape, F32)] * (4 if first is None else 1)
    return small_call(kernel, name, [x for pair in parts for x in pair], made, after, True)


def place_rows(packs, sent, grad_in, after):
    def kernel(k):
        for layer in range(2):

            @pl.when(k.core == layer)
            def _():
                k.saves, k.loads, k.copies.count, k.present = [], {}, 0, set()
                for i, whose in enumerate((named.own_, named.sent_)):
                    k.load_from((named.out, i), k.place(named.layer_out, layer, whose), k.low.at[i])
                    if layer:
                        k.load_from((named.grad, i), k.place(named.outgoing, 1, whose), k.low.at[2 + i])
                if not layer:
                    k.load_from((named.grad, 0), k.outer[named.from_grad_in], k.high.at[0])
                    for i, name in enumerate((named.grad_high, named.grad_low)):
                        k.load_from((named.grad, 1 + i), k.place(name, 0, named.sent_), k.low.at[2 + i])
                for i in range(2):
                    rows = pl.ds((layer ^ i) * ROWS, ROWS)
                    k.ready((named.out, i))
                    k.put(k.low.at[i], k.outer[named.layer_out].at[rows])
                    k.ready((named.grad, i))
                    if layer:
                        k.high[i] = k.low[2 + i].astype(F32)
                    elif i:
                        k.ready((named.grad, 2))
                        k.high[i] = k.low[2].astype(F32) + k.low[3].astype(F32)
                    k.put(k.high.at[i], k.outer[named.grad_in].at[rows])
                k.finish()

        k.saves = []

    given = {named.from_grad_in: grad_in}
    for name in (named.fwd0, named.mid1, named.end0, named.end1):
        given |= {named.own_ + name: packs[name], named.sent_ + name: sent[name]}
    made = {named.layer_out: ((2 * ROWS, D), BF16), named.grad_in: ((2 * ROWS, D), F32)}
    held = {named.low: ((4, ROWS, D), BF16), named.high: ((2, ROWS, D), F32)}
    return call(kernel, named.place_rows, given, made, held, after=after)


def swap(x):
    return lax.ppermute(x, "pipe", [(0, 1), (1, 0)])


def body(
    inputs,
    cotangent,
    lengths,
    proj_stack,
    gain_one,
    bias_one,
    w_qkv,
    w_out,
    gain_two,
    bias_two,
    w_up,
    w_down,
):
    count = lax.axis_size("dp")
    by_corners = count == 2 ** len(CORNERS) and D // count % 16 == 0
    core = lax.axis_index("pipe")
    gains = jnp.concatenate([gain_one, bias_one, gain_two, bias_two], axis=0)
    own = {named.gains: gains, named.w_qkv: w_qkv, named.w_out: w_out, named.w_up: w_up, named.w_down: w_down}
    sent = {k: swap(own[k]) for k in (named.gains, named.w_qkv, named.w_out)}
    later = lax.optimization_barrier((w_up, w_down, *sent.values()))
    sent |= {named.w_up: swap(later[0]), named.w_down: swap(later[1])}
    projection = jnp.swapaxes(proj_stack, 1, 2)

    def weights(*names):
        return {named.own_ + k: own[k] for k in names} | {named.sent_ + k: sent[k] for k in names}

    def room(*names):
        return {k: WEIGHTS[k] for k in names}

    wide, full = ((ROWS, D), BF16), ((ROWS, D), F32)
    up, proj, few = ((ROWS, FF), BF16), ((ROWS, 3 * D), BF16), ((8, D), F32)
    mask = {named.mask: ((ROWS, ROWS), F32)}
    kept = {k: ((ROWS, columns), dtype) for k, (columns, dtype) in ATTN_KEPT.items()}
    pack = {k: ((ROWS, columns), BF16) for k, columns in PACKS.items()}

    chunked = ((CHUNKS, ROWS, CHUNK), BF16)
    takes = [k for k in ATTN_KEPT if k != named.middle]
    attention_held = kept | room(named.gains, named.w_qkv, named.w_out, named.projection) | mask
    attention_held |= {named.hidden: wide, named.entry: wide, named.mixed: wide}
    ffn_held = room(named.gains, named.w_up, named.w_down) | {named.middle: full, named.total: full, named.slope: chunked}
    forward_held = ffn_held | {named.second: wide, named.layer_out: wide, named.activated: chunked}
    back_held = ffn_held | {named.grad_ffn: wide, named.grad_up: up, named.grad_middle: full}
    back_held |= {named.grad_attn: wide, named.vectors: few}
    last_held = room(named.gains, named.w_qkv, named.w_out, named.projection) | mask | {k: kept[k] for k in takes}
    last_held |= {named.hidden: wide, named.grad_middle: full, named.total: full, named.vectors: few, named.sums: few}
    last_held |= {named.grad_attn: wide, named.grad_proj: proj}
    places = {named.lengths: lengths, named.from_projection: projection}

    packs, sent_packs = {}, {}

    def run(kernel, name, given, made, held, packs_made=(), packs_changed=(), layer=0, after=()):
        given = given | {k: packs[k] for k in packs_changed}
        made = made | {k: pack[k] for k in packs_made}
        result = call(kernel, name, given, made, held, layer, list(packs_changed), after)
        packs.update({k: result.pop(k) for k in (*packs_made, *packs_changed)})
        return result

    first = run(
        attention_kernel,
        named.attention,
        places | {named.from_hidden: inputs} | weights(named.gains, named.w_qkv, named.w_out),
        kept,
        attention_held,
        [named.fwd0],
    )
    first |= run(
        ffn_kernel,
        named.feed_forward,
        {named.from_middle: first[named.middle]} | weights(named.gains, named.w_up, named.w_down),
        {named.slope: up},
        forward_held,
        [],
        [named.fwd0],
    )
    second = {named.cosine: first[named.cosine], named.sine: first[named.sine]}
    second |= run(
        second_layer_kernel,
        named.second_layer,
        places
        | {named.from_fwd0: packs[named.fwd0], named.from_grad_ffn: cotangent}
        | {named.from_ + k: first[k] for k in (named.cosine, named.sine)}
        | weights(named.gains, named.w_qkv, named.w_out, named.w_up, named.w_down),
        {k: kept[k] for k in takes if k not in (named.cosine, named.sine)}
        | {named.grad_middle: full, named.vectors: few},
        attention_held | forward_held | back_held,
        [named.act1, named.mid1],
        layer=1,
    )
    sent_packs[named.act1] = swap(packs[named.act1])
    mid1, fwd0, _ = lax.optimization_barrier(
        (packs[named.mid1], packs[named.fwd0], sent_packs[named.act1])
    )
    sent_packs[named.mid1] = swap(mid1)
    sent_packs[named.fwd0] = swap(fwd0)

    def second_back(after):
        second.update(
            run(
                attention_back_kernel,
                named.second_layer_back,
                places
                | {named.from_fwd0: packs[named.fwd0]}
                | {named.from_ + k: second[k] for k in (*takes, named.grad_middle, named.vectors)}
                | weights(named.gains, named.w_qkv, named.w_out),
                {named.sums: few},
                last_held | {named.outgoing: wide},
                [named.end1],
                layer=1,
                after=after,
            )
        )
        sent_packs[named.end1] = swap(packs[named.end1])

    def first_ffn_back(after):
        first.update(
            run(
                ffn_back_kernel,
                named.first_layer_ffn_back,
                {named.from_end1: packs[named.end1]}
                | {named.from_ + k: first[k] for k in (named.slope, named.middle)}
                | weights(named.gains, named.w_up, named.w_down),
                {named.grad_middle: full, named.vectors: few},
                back_held,
                [named.mid0],
                after=after,
            )
        )
        sent_packs[named.mid0] = swap(packs[named.mid0])

    def first_attention_back(after):
        first.update(
            run(
                attention_back_kernel,
                named.first_layer_attention_back,
                places
                | {named.from_hidden: inputs}
                | {named.from_ + k: first[k] for k in (*takes, named.grad_middle, named.vectors)}
                | weights(named.gains, named.w_qkv, named.w_out),
                {named.sums: few, named.grad_in: full},
                last_held | {named.grad_in: full, named.grad_high: wide, named.grad_low: wide},
                [named.end0],
                after=after,
            )
        )
        sent_packs[named.end0] = swap(packs[named.end0])

    sums = {}

    def start(name, layer, after=()):
        if not by_corners:
            return []
        used = {PLACES[layer][x][0] for pair in USED[name] for x in pair if x in PLACES[layer]}
        if name == named.down and not layer:
            used.add(named.end1)
        given = {}
        for k in sorted(used):
            given |= {named.own_ + k: packs[k], named.sent_ + k: sent_packs[k]}
        if name == named.down and layer:
            given[named.grad_ffn] = cotangent
        if name == named.attn:
            given[named.from_vectors] = (first, second)[layer][named.sums]
        z_first = (name, layer) in ((named.attn, 1), (named.down, 0), (named.down, 1),)
        made = product(name, layer, given, after, z_first)
        sums[name, layer] = CornerSum(made, z_first)
        return [made[named.send]]

    def step(after, *jobs):
        if not by_corners:
            return []
        pairs = []
        for name, layer in jobs:
            last = layer == 0 and sums[name, layer].stage == len(CORNERS)
            pairs.append((sums[name, layer], sums[name, 1].total if last else None))
        return steps(pairs, after)

    down1, up1, attn1 = (named.down, 1), (named.up, 1), (named.attn, 1)
    down0, up0, attn0 = (named.down, 0), (named.up, 0), (named.attn, 0)
    done = start(named.down, 1)
    second_back([*done, sent_packs[named.fwd0]])
    done = [packs[named.end1]]
    done = start(named.up, 1, done)
    done = start(named.attn, 1, done)
    first_ffn_back(done)
    done = [packs[named.mid0]]
    done = step(done, down1)
    done = step(done, up1)
    done = start(named.up, 0, done)
    done = start(named.down, 0, done)
    done = step(done, down1, attn1)
    first_attention_back(done)
    done = [packs[named.end0]]
    done = step(done, up0, down1, up1)
    done = step(done, attn1)
    done = start(named.attn, 0, done)
    done = step(done, up0)
    done = step(done, attn1)
    done = step(done, down0, up1, down1)
    rows = place_rows(packs, sent_packs, first[named.grad_in], done)
    done = [rows[named.layer_out]]
    done = step(done, attn0)
    done = step(done, up0)
    done = step(done, down0)
    done = step(done, attn0)
    done = step(done, attn1)
    done = step(done, down0, up1)
    done = step(done, attn0)
    done = step(done, up0)
    done = step(done, down0)
    done = step(done, attn0)

    def by_layer(first, second):
        return jnp.where(core == 0, first, second)

    if by_corners:
        shard = D // count
        grad_w_down, grad_w_up, grad_w_out, grad_w_qkv, *vectors = assemble(
            [sums[name, 0].total for name in (named.down, named.up, named.attn)],
            named.gather,
            [
                (0, 0, (FF // count, D)),
                (1, 0, (shard, FF)),
                (1, FF // 2, (shard, D)),
                (2, 0, (shard, 3 * D)),
                (2, None, (1, shard)),
            ],
            done,
        )
    else:

        def rows_of(layer, name):
            name, at, width = PLACES[layer][name]
            return [x[name][:, at : at + width] for x in (packs, sent_packs)]

        def grads_of(layer):
            if layer:
                return by_layer(cotangent[:ROWS], cotangent[ROWS:]), by_layer(
                    cotangent[ROWS:], cotangent[:ROWS]
                )
            return rows_of(1, named.outgoing)

        def one(lhs, rhs):
            parts = [
                sum(dot_tn(a, b) for a, b in zip(lhs(layer), rhs(layer))) for layer in range(2)
            ]
            return lax.psum_scatter(by_layer(*parts), "dp", scatter_dimension=0, tiled=True)

        def both(name):
            return lambda layer: rows_of(layer, name)

        grad_w_down = one(both(named.activated), grads_of)
        grad_w_up = one(both(named.second), both(named.grad_up))
        grad_w_qkv = one(both(named.entry), both(named.grad_proj))
        grad_w_out = one(both(named.mixed), both(named.grad_attn))
        vectors = by_layer(*[x[named.sums] + swap(x[named.sums]) for x in (first, second)])
        vectors = lax.psum_scatter(vectors, "dp", scatter_dimension=1, tiled=True)
        vectors = [vectors[i][None] for i in range(4)]

    return (
        rows[named.layer_out][None],
        rows[named.grad_in][None],
        vectors[0],
        vectors[1],
        grad_w_qkv[None],
        grad_w_out[None],
        vectors[2],
        vectors[3],
        grad_w_up[None],
        grad_w_down[None],
    )


def solution(mesh):
    placed = (
        P("dp", None),
        P("dp", None),
        P("dp", None),
        P(),
        P("pipe", None),
        P("pipe", None),
        P("pipe", None, None),
        P("pipe", None, None),
        P("pipe", None),
        P("pipe", None),
        P("pipe", None, None),
        P("pipe", None, None),
    )
    return jax.shard_map(
        body,
        mesh=mesh,
        in_specs=placed,
        out_specs=(
            P("pipe", "dp", None),
            P("pipe", "dp", None),
            P("pipe", "dp"),
            P("pipe", "dp"),
            P("pipe", "dp", None),
            P("pipe", "dp", None),
            P("pipe", "dp"),
            P("pipe", "dp"),
            P("pipe", "dp", None),
            P("pipe", "dp", None),
        ),
        check_vma=False,
    )
```
